32 devices in a mesh: pb: 8 (over y, x, core), slot: 4 (over z).
Axes of the slice: x: 2, y: 2, z: 4, core: 2. Of those that a mesh axis runs over, the one named last changes fastest.
Arguments:
- x_in: bfloat16 [8, 16, 128, 1024], P(None, 'pb', 'slot'), may hold values from -6 to 6
- memory: bfloat16 [8, 16, 384, 1024], P(None, 'pb', 'slot'), may hold values from -6 to 6
- doc_scores: float32 [16, 8], P('pb'), may hold values from -6 to 6
- valid_count: int32 [16], P('pb'), may hold values from 2 to 8, as said below
- target_ids: int32 [16, 128], P('pb'), may hold values from 0 to 50175
- target_len: int32 [16], P('pb'), may hold values from 64 to 128, as said below
- mem_len: int32 [8, 16], P('slot', 'pb'), may hold values from 192 to 384, as said below
- attn_w: bfloat16 [8192, 1024], P(('pb', 'slot')), as said below
- ffn_in: bfloat16 [4096, 1024], P(('pb', 'slot')), may hold values from -0.1875 to 0.1875
- ffn_out: bfloat16 [4096, 1024], P(('pb', 'slot')), may hold values from -0.09375 to 0.09375
- ffn_bias: float32 [4096], replicated, may hold values from -4 to 4
- norms: float32 [6, 1024], replicated, as said below
- embedding: bfloat16 [50176, 1024], P('slot'), may hold values from -0.375 to 0.375
Outputs:
- loss: float32 [], replicated
- entropy: float32 [], replicated
- grad_x: bfloat16 [8, 16, 128, 1024], P(None, 'pb', 'slot')
- grad_memory: bfloat16 [8, 16, 384, 1024], P(None, 'pb', 'slot')
- grad_attn: float32 [8192, 1024], P(('pb', 'slot'))
- grad_ffn_in: float32 [4096, 1024], P(('pb', 'slot'))
- grad_ffn_out: float32 [4096, 1024], P(('pb', 'slot'))
- grad_ffn_bias: float32 [4096], P(('pb', 'slot'))
- grad_norms: float32 [6, 1024], replicated
- grad_embedding: float32 [50176, 1024], P('slot', 'pb')
The draws below stay inside these ranges and needn't reach their ends.
Inputs may be any that keep to these rules, and one draw needn't show every extreme that they name: `valid_count`: some question has 8 valid slots and some other question has 2. `target_len`: some question has 128 real tokens and some other question has 64; real tokens come first. `mem_len`: for every slot, some question has 384 real positions and some other question has 192; real positions come first. `attn_w`: independent normal entries with a fixed scale for each of the eight blocks. `norms`: gains in rows 0, 2, 4 and shifts in rows 1, 3, 5.
All inputs are finite; a program needn't handle non-finite values.
Results may differ from the reference program's by a relative error of at most 0.03.
Values may be sent and summed in bfloat16 or wider, within the bound.
A program may use at most 448 MiB of HBM per device.

```python
import jax
import jax.numpy as jnp
from jax import lax

D = 1024
HEADS = 16
FF = 4096
VOCAB = 50176
SLOTS = 8
TGT = 128
MEM = 384
QUESTIONS = 16


def ends_drawn(key, shape, lowest, highest):
    count_key, full_key, offset_key = jax.random.split(key, 3)
    counts = jax.random.randint(count_key, shape + (QUESTIONS,), lowest, highest + 1)
    full_index = jax.random.randint(full_key, shape + (1,), 0, QUESTIONS)
    offset = jax.random.randint(offset_key, shape + (1,), 1, QUESTIONS)
    short_index = (full_index + offset) % QUESTIONS
    places = jnp.arange(QUESTIONS)
    counts = jnp.where(places == short_index, lowest, counts)
    counts = jnp.where(places == full_index, highest, counts)
    return counts.astype(jnp.int32)


def draw_valid_count(key, part):
    key = jax.random.fold_in(key, 14)
    return ends_drawn(key, (), 2, SLOTS)


def draw_target_len(key, part):
    key = jax.random.fold_in(key, 13)
    return ends_drawn(key, (), TGT // 2, TGT)


def draw_mem_len(key, part):
    key = jax.random.fold_in(key, 15)
    return ends_drawn(key, (SLOTS,), MEM // 2, MEM)


def draw_attn_w(key, part):
    key = jax.random.fold_in(key, 11)
    block_gains = jnp.array([1.5, 1.5, 1.0, 4.0, 1.5, 1.5, 1.0, 6.0], jnp.float32)
    row_gains = jnp.repeat(block_gains, D)[:, None]
    values = jax.random.normal(key, (8 * D, D), jnp.float32) * row_gains * D ** (-0.5)
    return values.astype(jnp.bfloat16)


def draw_norms(key, part):
    key = jax.random.fold_in(key, 12)
    first_key, second_key = jax.random.split(key)
    gains = jax.random.uniform(first_key, (3, D), jnp.float32, 0.5, 1.5)
    shifts = jax.random.normal(second_key, (3, D), jnp.float32) * 0.3
    return jnp.stack([gains, shifts], axis=1).reshape(6, D)


def plant(values, key, smallest, top_value):
    dims = values.shape
    place = [jax.random.randint(jax.random.fold_in(key, axis), (), 0, dims[axis]) for axis in range(len(dims))]
    values = values.at[tuple(place)].set(smallest)
    longest = dims.index(max(dims))
    place[longest] = (place[longest] + 1) % dims[longest]
    return values.at[tuple(place)].set(top_value)


def level_of(key, extent, pieces, low, high):
    def one(dim, parts):
        steps = jax.random.uniform(jax.random.fold_in(jax.random.fold_in(key, 6), dim), (parts,), jnp.float32, low / len(pieces), high / len(pieces))
        return jnp.repeat(jnp.exp(steps), extent[dim] // parts).reshape((-1,) + (1,) * (len(extent) - dim - 1))

    level = one(*pieces[0])
    for cut in pieces[1:]:
        level = level * one(*cut)
    return level


def bell_draw(stream_key, extent, deviation, most, pieces=(), held_as=jnp.bfloat16):
    result = deviation * jax.random.normal(stream_key, extent, jnp.float32)
    if pieces:
        result = result * level_of(stream_key, extent, pieces, -0.22, 0.18)
    return jnp.clip(result, -most, most).astype(held_as)


def setup_inputs(seed: int = 0) -> dict:
    key_list = jax.random.split(jax.random.key(seed), 14)
    x_in = bell_draw(key_list[0], (SLOTS, QUESTIONS, TGT, D), 1.0, 6.0, ((1, 8), (2, 4)))
    memory = bell_draw(key_list[1], (SLOTS, QUESTIONS, MEM, D), 1.0, 6.0, ((1, 8), (2, 4)))
    doc_scores = bell_draw(key_list[2], (QUESTIONS, SLOTS), 1.5, 6.0, ((0, 8),), jnp.float32)
    valid_count = draw_valid_count(jax.random.fold_in(key_list[13], 71), 0)
    target_ids = plant(jax.random.randint(key_list[4], (QUESTIONS, TGT), 0, VOCAB), jax.random.fold_in(key_list[4], 1), 0, VOCAB - 1).astype(jnp.int32)
    target_len = draw_target_len(jax.random.fold_in(key_list[13], 71), 0)
    mem_len = draw_mem_len(jax.random.fold_in(key_list[13], 71), 0)
    attn_w = draw_attn_w(jax.random.fold_in(key_list[13], 71), 0)
    ffn_in = bell_draw(key_list[8], (FF, D), D ** -0.5, 0.1875, ((0, 32),))
    ffn_out = bell_draw(key_list[9], (FF, D), FF ** -0.5, 0.09375, ((0, 32),))
    ffn_bias = bell_draw(key_list[10], (FF,), 0.3, 4.0, (), jnp.float32)
    norms = draw_norms(jax.random.fold_in(key_list[13], 71), 0)
    embedding = bell_draw(key_list[12], (VOCAB, D), (D // 4) ** -0.5, 0.375, ((0, 4),))
    return dict(x_in=x_in, memory=memory, doc_scores=doc_scores, valid_count=valid_count, target_ids=target_ids, target_len=target_len, mem_len=mem_len, attn_w=attn_w, ffn_in=ffn_in, ffn_out=ffn_out, ffn_bias=ffn_bias, norms=norms, embedding=embedding)


@jax.custom_vjp
def low(v):
    return lax.optimization_barrier(v.astype(jnp.bfloat16)).astype(jnp.float32)

@jax.custom_vjp
def low_back(v):
    return v

def low_keep(v):
    return (low(v), None)

def low_pass(kept, grad):
    return (grad,)

def back_keep(v):
    return (v, None)

def back_low(kept, grad):
    return (low(grad),)
low.defvjp(low_keep, low_pass)
low_back.defvjp(back_keep, back_low)
eps_norm = 1e-05
entropy_weight = 0.25
mask_fill = -1e+30

def both_ways(value):
    return low_back(low(value))

def matmul_high(left, right):
    return jnp.dot(left, right, precision=lax.Precision.HIGHEST)

def layer_norm(resid, gain, shift):
    row_mean = lax.optimization_barrier(jnp.mean(resid, axis=-1, keepdims=True))
    centered = resid - row_mean
    inv_root = lax.rsqrt(lax.optimization_barrier(jnp.mean(centered * centered, axis=-1, keepdims=True)) + eps_norm)
    return centered * inv_root * gain + shift

def attention(queries, key_rows, value_rows, allowed):
    scores = low_back(jnp.einsum('nqhe,nkhe->nhqk', queries, key_rows, precision=lax.Precision.HIGHEST))
    scores = jnp.where(allowed, scores, mask_fill)
    attn_probs = low(jax.nn.softmax(scores, axis=-1))
    return jnp.einsum('nhqk,nkhe->nqhe', attn_probs, value_rows, precision=lax.Precision.HIGHEST)

def slot_likelihood(x_slot, mem_slot, mem_valid, params, target_ids, target_len):
    attn_w, ffn_in, ffn_out, ffn_bias, norms, embedding = params
    n_quest = x_slot.shape[0]
    model_width = x_slot.shape[2]
    head_dim = model_width // HEADS
    scaling = head_dim ** (-0.5)
    blocks = [attn_w[block_index * model_width:(block_index + 1) * model_width] for block_index in range(8)]

    def split_heads(value):
        return value.reshape(value.shape[0], value.shape[1], HEADS, head_dim)

    def merge_heads(value):
        return value.reshape(value.shape[0], value.shape[1], model_width)
    inputs = low_back(x_slot)
    memory_rows = low_back(mem_slot)
    queries = both_ways(matmul_high(inputs, blocks[0]) * scaling)
    key_rows = both_ways(matmul_high(inputs, blocks[1]))
    value_rows = both_ways(matmul_high(inputs, blocks[2]))
    positions = jnp.arange(TGT)
    causal = (positions[None, :] <= positions[:, None])[None, None]
    self_out = both_ways(merge_heads(attention(split_heads(queries), split_heads(key_rows), split_heads(value_rows), causal)))
    hidden_one = layer_norm(inputs + low_back(matmul_high(self_out, blocks[3])), norms[0], norms[1])
    cross_queries = both_ways(matmul_high(low(hidden_one), blocks[4]) * scaling)
    cross_keys = both_ways(matmul_high(memory_rows, blocks[5]))
    cross_values = both_ways(matmul_high(memory_rows, blocks[6]))
    seen = (jnp.arange(MEM)[None, :] < mem_valid[:, None])[:, None, None, :]
    cross_out = both_ways(merge_heads(attention(split_heads(cross_queries), split_heads(cross_keys), split_heads(cross_values), seen)))
    hidden_two = layer_norm(hidden_one + low_back(matmul_high(cross_out, blocks[7])), norms[2], norms[3])
    pre_act = low_back(matmul_high(low(hidden_two), ffn_in.T) + ffn_bias)
    ffn_term = low_back(matmul_high(low(jax.nn.gelu(pre_act, approximate=False)), ffn_out))
    hidden_three = layer_norm(hidden_two + ffn_term, norms[4], norms[5])
    logits = low_back(matmul_high(low(hidden_three).reshape(-1, model_width), embedding.T))
    log_probs = jax.nn.log_softmax(logits, axis=-1)
    picked = jnp.take_along_axis(log_probs, target_ids.reshape(-1, 1), axis=1).reshape(n_quest, TGT)
    live = positions[None, :] < target_len[:, None]
    return lax.optimization_barrier(jnp.sum(jnp.where(live, picked, 0.0), axis=1)) / target_len.astype(jnp.float32)

def reference(x_in, memory, doc_scores, valid_count, target_ids, target_len, mem_len, attn_w, ffn_in, ffn_out, ffn_bias, norms, embedding):
    params = (attn_w.astype(jnp.float32), ffn_in.astype(jnp.float32), ffn_out.astype(jnp.float32), ffn_bias, norms, embedding.astype(jnp.float32))
    lengths = target_len.astype(jnp.float32)
    valid = jnp.arange(SLOTS)[:, None] < valid_count[None, :]
    scores_t = doc_scores.T

    def objective(inputs, memory_in, weights):

        def one_slot(item):
            return jax.checkpoint(slot_likelihood)(item[0], item[1], item[2], weights, target_ids, target_len)
        per_slot = lax.map(one_slot, (inputs, memory_in, mem_len))
        joint = jnp.where(valid, scores_t + per_slot, mask_fill)
        prior = jnp.where(valid, scores_t, mask_fill)
        joint_total = jax.nn.logsumexp(joint, axis=0)
        neg_marginal = jax.nn.logsumexp(prior, axis=0) - joint_total
        log_post = joint - joint_total
        entropy_q = -lax.optimization_barrier(jnp.sum(jnp.exp(log_post) * log_post, axis=0))
        return (jnp.sum(lengths * (neg_marginal + entropy_weight * entropy_q)), entropy_q)
    total_value, pullback, entropy_q = jax.vjp(objective, x_in.astype(jnp.float32), memory.astype(jnp.float32), params, has_aux=True)
    grad_inputs, grad_mem, grad_params = pullback(jnp.ones_like(total_value))
    loss = total_value / jnp.sum(lengths)
    entropy = jnp.mean(entropy_q)
    return (loss, entropy, grad_inputs.astype(jnp.bfloat16), grad_mem.astype(jnp.bfloat16), grad_params[0], grad_params[1], grad_params[2], grad_params[3], grad_params[4], grad_params[5])
```

```python
import jax
import jax.numpy as jnp
from jax import lax
from jax.sharding import PartitionSpec as P

HEADS = 16


eps_norm = 1e-05
entropy_weight = 0.25
mask_fill = -1e30
root_half = 0.7071067811865476
inv_root_tau = 0.3989422804014327


def merged(value, axis, join):
    size = lax.axis_size(axis)
    packed = jnp.stack(value)
    me = lax.axis_index(axis)
    parts = jnp.stack([packed] + [shifted(packed, axis, step) for step in range(1, size)])
    parts = parts[(me - jnp.arange(size)) % size]
    pieces = tuple(parts[:, i] for i in range(len(value)))
    head = jax.tree.map(lambda part: part[0], pieces)
    tail = jax.tree.map(lambda part: part[1:], pieces)
    running, _ = lax.scan(lambda running, section: (join(running, section), None), head, tail)
    return running


def grid_of(n_pb):
    cores = 2 if n_pb % 2 == 0 else 1
    chips = n_pb // cores
    wide = max(d for d in range(1, chips + 1) if chips % d == 0 and d * d <= chips)
    return chips // wide, wide, cores


def shifted(value, axis, step):
    if axis == "slot":
        size = lax.axis_size("slot")
        return lax.ppermute(value, "slot", [(i, (i + step) % size) for i in range(size)])
    n_pb = lax.axis_size("pb")
    tall, wide, cores = grid_of(n_pb)
    pairs = []
    for i in range(n_pb):
        y, x, c = i // (wide * cores), i // cores % wide, i % cores
        if axis == "y":
            y = (y + step) % tall
        elif axis == "x":
            x = (x + step) % wide
        else:
            c = (c + step) % cores
        pairs.append((i, (y * wide + x) * cores + c))
    return lax.ppermute(value, "pb", pairs)


def place_of(axis):
    if axis == "slot":
        return lax.axis_index("slot"), lax.axis_size("slot")
    tall, wide, cores = grid_of(lax.axis_size("pb"))
    i = lax.axis_index("pb")
    if axis == "y":
        return i // (wide * cores), tall
    if axis == "x":
        return i // cores % wide, wide
    return i % cores, cores


def pick(value, index, dim):
    return lax.dynamic_index_in_dim(value, index, dim, keepdims=False)


def ring_gather(value, axis):
    me, size = place_of(axis)
    found = [(me, value)]
    for step in range(1, size):
        value = shifted(value, axis, 1)
        found.append(((me - step) % size, value))
    return found


def ring_scatter(value, axis, dim):
    me, size = place_of(axis)
    total = pick(value, (me - 1) % size, dim).astype(jnp.bfloat16)
    for step in range(1, size):
        part = pick(value, (me - 1 - step) % size, dim)
        total = shifted(total, axis, 1).astype(jnp.float32) + part.astype(jnp.float32)
        if step < size - 1:
            total = total.astype(jnp.bfloat16)
    return total


def gather_all(shard):
    tall, wide, cores = grid_of(lax.axis_size("pb"))
    rows, width = shard.shape
    slots = lax.axis_size("slot")
    column = jnp.zeros((slots, rows, width), shard.dtype)
    for index, block in ring_gather(shard, "slot"):
        column = lax.dynamic_update_index_in_dim(column, block, index, 0)
    column = column.reshape(slots * rows, width)
    half = slots * rows // 2
    core, _ = place_of("core")
    whole = jnp.zeros((tall * wide, cores, 2, half, width), shard.dtype)
    for side, (first, second) in enumerate((("x", "y"), ("y", "x"))):
        part = column[side * half : (side + 1) * half]
        for at_first, block in ring_gather(part, first):
            for at_second, block in ring_gather(block, second):
                x, y = (at_first, at_second) if first == "x" else (at_second, at_first)
                for at_core, block in ring_gather(block, "core"):
                    whole = lax.dynamic_update_slice(
                        whole, block[None, None, None], (y * wide + x, at_core, side, 0, 0)
                    )
    return whole.reshape(tall * wide * cores, slots * rows, width)


def scatter_pb(value):
    tall, wide, cores = grid_of(lax.axis_size("pb"))
    rest = value.shape[1:]
    value = value.reshape((tall * wide, cores) + rest)
    value = ring_scatter(value, "core", 1).astype(jnp.bfloat16)
    value = value.reshape((tall, wide) + rest)
    half = rest[0] // 2
    first = ring_scatter(value[:, :, :half], "x", 1)
    second = ring_scatter(value[:, :, half:], "y", 0)
    first = ring_scatter(first.astype(jnp.bfloat16), "y", 0)
    second = ring_scatter(second.astype(jnp.bfloat16), "x", 0)
    return jnp.concatenate([first, second], axis=0)


def scatter_all(value):
    n_pb, slots = lax.axis_size("pb"), lax.axis_size("slot")
    rows = value.shape[0] // (n_pb * slots)
    value = value.reshape((n_pb, slots, rows) + value.shape[1:])
    column = scatter_pb(value)
    return ring_scatter(column.astype(jnp.bfloat16), "slot", 0)


def sum_all(value, axes):
    for axis in axes:
        me, size = place_of(axis)
        parts = [value] + [shifted(value, axis, step) for step in range(1, size)]
        placed = jnp.stack(parts)
        value = jnp.sum(placed[(me - jnp.arange(size)) % size], axis=0)
    return value


def to_slots(value):
    me, size = place_of("slot")
    every, questions, steps, width = value.shape
    chunks = value.reshape(size, every // size, questions, steps, width)
    result = jnp.zeros((every // size, questions, size, steps, width), value.dtype)
    for step in range(size):
        block = pick(chunks, (me + step) % size, 0)
        if step:
            block = shifted(block, "slot", step)
        result = lax.dynamic_update_index_in_dim(result, block, (me - step) % size, 2)
    return result.reshape(every // size, questions, size * steps, width)


def to_positions(value):
    me, size = place_of("slot")
    own, questions, steps, width = value.shape
    chunks = value.reshape(own, questions, size, steps // size, width)
    result = jnp.zeros((size, own, questions, steps // size, width), value.dtype)
    for step in range(size):
        block = pick(chunks, (me + step) % size, 2)
        if step:
            block = shifted(block, "slot", step)
        result = lax.dynamic_update_index_in_dim(result, block, (me - step) % size, 0)
    return result.reshape(size * own, questions, steps // size, width)


def product(left, right):
    return jnp.dot(left, right, preferred_element_type=jnp.float32)


def contract_rows(left, right):
    return lax.dot_general(
        left, right, (((0,), (0,)), ((), ())), preferred_element_type=jnp.float32
    )


def contract_cols(left, right):
    return lax.dot_general(
        left, right, (((1,), (1,)), ((), ())), preferred_element_type=jnp.float32
    )


def norm_forward(resid, gain, shift):
    row_mean = jnp.mean(resid, axis=-1, keepdims=True)
    centered = resid - row_mean
    inv_root = lax.rsqrt(jnp.mean(centered * centered, axis=-1, keepdims=True) + eps_norm)
    normed = centered * inv_root
    return (normed * gain + shift, normed, inv_root)


def norm_backward(grad_out, normed, inv_root, gain):
    scaled = grad_out * gain
    grad_in = inv_root * (
        scaled
        - jnp.mean(scaled, axis=-1, keepdims=True)
        - normed * jnp.mean(scaled * normed, axis=-1, keepdims=True)
    )
    return (grad_in, jnp.sum(grad_out * normed, axis=0), jnp.sum(grad_out, axis=0))


def attend_forward(queries, key_rows, value_rows, allowed):
    scores = jnp.einsum("nqhe,nkhe->nhqk", queries, key_rows, preferred_element_type=jnp.float32)
    scores = jnp.where(allowed, scores, mask_fill)
    row_max = jnp.max(scores, axis=-1, keepdims=True)
    expos = jnp.exp(scores - row_max)
    row_sum = jnp.sum(expos, axis=-1, keepdims=True)
    probs_low = (expos / row_sum).astype(jnp.bfloat16)
    result = jnp.einsum(
        "nhqk,nkhe->nqhe", probs_low, value_rows, preferred_element_type=jnp.float32
    )
    return (result, row_max + jnp.log(row_sum))


def attend_backward(queries, key_rows, value_rows, allowed, row_lse, grad_out):
    scores = jnp.einsum("nqhe,nkhe->nhqk", queries, key_rows, preferred_element_type=jnp.float32)
    scores = jnp.where(allowed, scores, mask_fill)
    attn_probs = jnp.exp(scores - row_lse)
    grad_values = jnp.einsum(
        "nhqk,nqhe->nkhe",
        attn_probs.astype(jnp.bfloat16),
        grad_out,
        preferred_element_type=jnp.float32,
    )
    grad_probs = jnp.einsum(
        "nqhe,nkhe->nhqk", grad_out, value_rows, preferred_element_type=jnp.float32
    )
    row_delta = jnp.sum(grad_probs * attn_probs, axis=-1, keepdims=True)
    grad_scores = (attn_probs * (grad_probs - row_delta)).astype(jnp.bfloat16)
    grad_queries = jnp.einsum(
        "nhqk,nkhe->nqhe", grad_scores, key_rows, preferred_element_type=jnp.float32
    )
    grad_keys = jnp.einsum(
        "nhqk,nqhe->nkhe", grad_scores, queries, preferred_element_type=jnp.float32
    )
    return (grad_queries, grad_keys, grad_values)


def body(
    x_in,
    memory,
    doc_scores,
    valid_count,
    target_ids,
    target_len,
    mem_len,
    attn_w,
    ffn_in,
    ffn_out,
    ffn_bias,
    norms,
    embedding,
):
    x_here, mem_here = (
        to_slots(x_in),
        to_slots(memory),
    )
    slots_here, questions, tgt_steps, model_width = x_here.shape
    mem_steps = mem_here.shape[2]
    seq_count = slots_here * questions
    head_dim = model_width // HEADS
    scaling = head_dim ** (-0.5)
    attn_full, in_full, out_full = (
        gather_all(attn_w).reshape(-1, model_width),
        gather_all(ffn_in).reshape(-1, model_width),
        gather_all(ffn_out).reshape(-1, model_width),
    )
    blocks = [
        attn_full[block_index * model_width : (block_index + 1) * model_width]
        for block_index in range(8)
    ]

    def split_heads(value, steps):
        return value.reshape(seq_count, steps, HEADS, head_dim)

    def merge_rows(value):
        return value.reshape(-1, model_width)

    inputs = x_here.reshape(seq_count * tgt_steps, model_width)
    memory_rows = mem_here.reshape(seq_count * mem_steps, model_width)
    positions = jnp.arange(tgt_steps)
    causal = (positions[None, :] <= positions[:, None])[None, None]
    seen = (jnp.arange(mem_steps)[None, None, :] < mem_len[:, :, None]).reshape(
        seq_count, 1, 1, mem_steps
    )
    queries = (product(inputs, blocks[0]) * scaling).astype(jnp.bfloat16)
    key_rows = product(inputs, blocks[1]).astype(jnp.bfloat16)
    value_rows = product(inputs, blocks[2]).astype(jnp.bfloat16)
    self_out, self_lse = attend_forward(
        split_heads(queries, tgt_steps),
        split_heads(key_rows, tgt_steps),
        split_heads(value_rows, tgt_steps),
        causal,
    )
    self_out = merge_rows(self_out).astype(jnp.bfloat16)
    hidden_one, normed_one, root_one = norm_forward(
        inputs.astype(jnp.float32) + product(self_out, blocks[3]), norms[0], norms[1]
    )
    one_low = hidden_one.astype(jnp.bfloat16)
    cross_queries = (product(one_low, blocks[4]) * scaling).astype(jnp.bfloat16)
    cross_keys = product(memory_rows, blocks[5]).astype(jnp.bfloat16)
    cross_values = product(memory_rows, blocks[6]).astype(jnp.bfloat16)
    cross_out, cross_lse = attend_forward(
        split_heads(cross_queries, tgt_steps),
        split_heads(cross_keys, mem_steps),
        split_heads(cross_values, mem_steps),
        seen,
    )
    cross_out = merge_rows(cross_out).astype(jnp.bfloat16)
    hidden_two, normed_two, root_two = norm_forward(
        hidden_one + product(cross_out, blocks[7]), norms[2], norms[3]
    )
    two_low = hidden_two.astype(jnp.bfloat16)
    pre_act = contract_cols(two_low, in_full) + ffn_bias
    act_low = jax.nn.gelu(pre_act, approximate=False).astype(jnp.bfloat16)
    hidden_three, normed_three, root_three = norm_forward(
        hidden_two + product(act_low, out_full), norms[4], norms[5]
    )
    three_low = hidden_three.astype(jnp.bfloat16).reshape(
        slots_here, questions, tgt_steps, model_width
    )
    vocab_here = embedding.shape[0]
    vocab_start = lax.axis_index("slot") * vocab_here
    local_ids = target_ids - vocab_start
    slot_count = lax.axis_size("slot")
    piece = jnp.zeros((slot_count,) + three_low.shape, three_low.dtype)
    for index, block in ring_gather(three_low, "slot"):
        piece = lax.dynamic_update_index_in_dim(piece, block, index, 0)
    piece = piece.reshape((-1,) + three_low.shape[1:])
    flat_rows = piece.reshape(-1, model_width)
    logits = contract_cols(flat_rows, embedding).reshape(
        piece.shape[0], questions, tgt_steps, vocab_here
    )
    rows_all = piece
    onehot = jnp.arange(vocab_here)[None, None, None, :] == local_ids[None, :, :, None]
    row_max = jnp.max(logits, axis=-1)
    row_sum = jnp.sum(jnp.exp(logits - row_max[..., None]), axis=-1)
    target_logit = jnp.sum(jnp.where(onehot, logits, 0.0), axis=-1)

    def merge_stats(first, second):
        joint_max = jnp.maximum(first[0], second[0])
        joint_sum = first[1] * jnp.exp(first[0] - joint_max) + second[1] * jnp.exp(
            second[0] - joint_max
        )
        return (joint_max, joint_sum, first[2] + second[2])

    row_max, row_sum, target_logit = merged((row_max, row_sum, target_logit), "slot", merge_stats)
    log_norm = row_max + jnp.log(row_sum)
    live = positions[None, :] < target_len[:, None]
    lengths = target_len.astype(jnp.float32)
    per_slot = (
        jnp.sum(jnp.where(live[None], target_logit - log_norm, 0.0), axis=2) / lengths[None, :]
    )
    valid = jnp.arange(per_slot.shape[0])[:, None] < valid_count[None, :]
    scores_t = doc_scores.T
    joint = jnp.where(valid, scores_t + per_slot, mask_fill)
    prior = jnp.where(valid, scores_t, mask_fill)
    joint_total = jax.nn.logsumexp(joint, axis=0)
    neg_marginal = jax.nn.logsumexp(prior, axis=0) - joint_total
    log_post = joint - joint_total
    posterior = jnp.exp(log_post)
    entropy_q = -jnp.sum(posterior * log_post, axis=0)
    objective_part = jnp.sum(lengths * (neg_marginal + entropy_weight * entropy_q))
    sum_objective, sum_lengths, sum_entropy = lax.psum(
        (objective_part, jnp.sum(lengths), jnp.sum(entropy_q)), "pb"
    )
    loss = sum_objective / sum_lengths
    entropy = sum_entropy / (questions * lax.axis_size("pb"))
    slot_weight = -posterior * (1.0 + entropy_weight * (log_post + entropy_q[None, :]))
    token_weight = jnp.where(live[None], slot_weight[:, :, None], 0.0)
    soft_probs = jnp.exp(logits - log_norm[..., None])
    grad_logits = (token_weight[..., None] * (onehot.astype(jnp.float32) - soft_probs)).astype(
        jnp.bfloat16
    )
    grad_embed = contract_rows(
        grad_logits.reshape(-1, vocab_here), rows_all.reshape(-1, model_width)
    )
    grad_embed = scatter_pb(
        grad_embed.astype(jnp.bfloat16)
        .reshape(vocab_here, lax.axis_size("pb"), -1)
        .transpose(1, 0, 2)
    )
    piece = grad_logits
    grad_three = ring_scatter(
        product(piece.reshape(-1, vocab_here), embedding)
        .astype(jnp.bfloat16)
        .reshape(slot_count, -1, model_width),
        "slot",
        0,
    )
    back_blocks, in_back, out_back = blocks, in_full, out_full
    grad_res_three, gain_three, shift_three = norm_backward(
        grad_three, normed_three, root_three, norms[4]
    )
    grad_ffn = grad_res_three.astype(jnp.bfloat16)
    grad_out_w = contract_rows(act_low, grad_ffn)
    grad_act = contract_cols(grad_ffn, out_back)
    cdf_part = 0.5 * (1.0 + lax.erf(pre_act * root_half))
    pdf_part = pre_act * inv_root_tau * jnp.exp(-0.5 * pre_act * pre_act)
    grad_pre = (grad_act * (cdf_part + pdf_part)).astype(jnp.bfloat16)
    grad_in_w = contract_rows(grad_pre, two_low)
    grad_bias = jnp.sum(grad_pre.astype(jnp.float32), axis=0)
    grad_two = grad_res_three + product(grad_pre, in_back)
    grad_res_two, gain_two, shift_two = norm_backward(grad_two, normed_two, root_two, norms[2])
    grad_cross = grad_res_two.astype(jnp.bfloat16)
    grad_w7 = contract_rows(cross_out, grad_cross)
    grad_cross_out = contract_cols(grad_cross, back_blocks[7]).astype(jnp.bfloat16)
    cq_grad, ck_grad, cv_grad = attend_backward(
        split_heads(cross_queries, tgt_steps),
        split_heads(cross_keys, mem_steps),
        split_heads(cross_values, mem_steps),
        seen,
        cross_lse,
        split_heads(grad_cross_out, tgt_steps),
    )
    cq_grad = merge_rows(cq_grad).astype(jnp.bfloat16)
    ck_grad = merge_rows(ck_grad).astype(jnp.bfloat16)
    cv_grad = merge_rows(cv_grad).astype(jnp.bfloat16)
    grad_w4 = contract_rows(one_low, cq_grad) * scaling
    grad_w5 = contract_rows(memory_rows, ck_grad)
    grad_w6 = contract_rows(memory_rows, cv_grad)
    grad_memory = (
        contract_cols(ck_grad, back_blocks[5]) + contract_cols(cv_grad, back_blocks[6])
    ).astype(jnp.bfloat16)
    grad_one = grad_res_two + contract_cols(cq_grad, back_blocks[4]) * scaling
    grad_res_one, gain_one, shift_one = norm_backward(grad_one, normed_one, root_one, norms[0])
    grad_attn_out = grad_res_one.astype(jnp.bfloat16)
    grad_w3 = contract_rows(self_out, grad_attn_out)
    grad_self_out = contract_cols(grad_attn_out, back_blocks[3]).astype(jnp.bfloat16)
    sq_grad, sk_grad, sv_grad = attend_backward(
        split_heads(queries, tgt_steps),
        split_heads(key_rows, tgt_steps),
        split_heads(value_rows, tgt_steps),
        causal,
        self_lse,
        split_heads(grad_self_out, tgt_steps),
    )
    sq_grad = merge_rows(sq_grad).astype(jnp.bfloat16)
    sk_grad = merge_rows(sk_grad).astype(jnp.bfloat16)
    sv_grad = merge_rows(sv_grad).astype(jnp.bfloat16)
    grad_w0 = contract_rows(inputs, sq_grad) * scaling
    grad_w1 = contract_rows(inputs, sk_grad)
    grad_w2 = contract_rows(inputs, sv_grad)
    grad_inputs = (
        grad_res_one
        + contract_cols(sq_grad, back_blocks[0]) * scaling
        + contract_cols(sk_grad, back_blocks[1])
        + contract_cols(sv_grad, back_blocks[2])
    )
    grad_inputs = grad_inputs.astype(jnp.bfloat16).reshape(
        slots_here, questions, tgt_steps, model_width
    )
    grad_memory = grad_memory.reshape(slots_here, questions, mem_steps, model_width)
    grad_inputs, grad_memory = (
        to_positions(grad_inputs),
        to_positions(grad_memory),
    )
    grad_attn = jnp.concatenate(
        [grad_w0, grad_w1, grad_w2, grad_w3, grad_w4, grad_w5, grad_w6, grad_w7], axis=0
    )
    grad_attn, grad_in_w, grad_out_w = (
        scatter_all(grad_attn),
        scatter_all(grad_in_w),
        scatter_all(grad_out_w),
    )
    small = jnp.concatenate(
        [
            jnp.stack([gain_one, shift_one, gain_two, shift_two, gain_three, shift_three], axis=0),
            grad_bias.reshape(-1, model_width),
        ],
        axis=0,
    )
    small = sum_all(small, ("core", "x", "y", "slot"))
    grad_norms = small[:6]
    grad_bias = small[6:].reshape(-1)
    own_bias = grad_bias.shape[0] // (lax.axis_size("pb") * slot_count)
    grad_bias = lax.dynamic_slice_in_dim(
        grad_bias,
        (lax.axis_index("pb") * slot_count + lax.axis_index("slot")) * own_bias,
        own_bias,
    )
    return (
        loss,
        entropy,
        grad_inputs,
        grad_memory,
        grad_attn,
        grad_in_w,
        grad_out_w,
        grad_bias,
        grad_norms,
        grad_embed,
    )


def solution(mesh):
    placed = (
        P(None, "pb", "slot", None),
        P(None, "pb", "slot", None),
        P("pb", None),
        P("pb"),
        P("pb", None),
        P("pb"),
        P("slot", "pb"),
        P(("pb", "slot"), None),
        P(("pb", "slot"), None),
        P(("pb", "slot"), None),
        P(),
        P(),
        P("slot", None),
    )
    return jax.shard_map(
        body,
        mesh=mesh,
        in_specs=placed,
        out_specs=(
            P(),
            P(),
            P(None, "pb", "slot", None),
            P(None, "pb", "slot", None),
            P(("pb", "slot"), None),
            P(("pb", "slot"), None),
            P(("pb", "slot"), None),
            P(("pb", "slot")),
            P(),
            P("slot", "pb"),
        ),
        check_vma=False,
    )
```

```python
import functools

import jax
import jax.numpy as jnp
from jax import lax
from jax.experimental import pallas as pl
from jax.experimental.pallas import tpu as pltpu
from jax.sharding import PartitionSpec as P

HEADS = 16


eps_norm = 1e-05
entropy_weight = 0.25
mask_fill = -1e30
root_half = 0.7071067811865476
inv_root_tau = 0.3989422804014327


def grid_of(n_pb):
    cores = 2 if n_pb % 2 == 0 else 1
    chips = n_pb // cores
    wide = max(d for d in range(1, chips + 1) if chips % d == 0 and d * d <= chips)
    return chips // wide, wide, cores


def shifted(value, axis, step):
    if axis == "slot":
        size = lax.axis_size("slot")
        return lax.ppermute(value, "slot", [(i, (i + step) % size) for i in range(size)])
    n_pb = lax.axis_size("pb")
    tall, wide, cores = grid_of(n_pb)
    pairs = []
    for i in range(n_pb):
        y, x, c = i // (wide * cores), i // cores % wide, i % cores
        if axis == "y":
            y = (y + step) % tall
        elif axis == "x":
            x = (x + step) % wide
        else:
            c = (c + step) % cores
        pairs.append((i, (y * wide + x) * cores + c))
    return lax.ppermute(value, "pb", pairs)


def place_of(axis):
    if axis == "slot":
        return lax.axis_index("slot"), lax.axis_size("slot")
    tall, wide, cores = grid_of(lax.axis_size("pb"))
    i = lax.axis_index("pb")
    if axis == "y":
        return i // (wide * cores), tall
    if axis == "x":
        return i // cores % wide, wide
    return i % cores, cores


def pick(value, index, dim):
    return lax.dynamic_index_in_dim(value, index, dim, keepdims=False)


def ring_gather(value, axis):
    me, size = place_of(axis)
    found = [(me, value)]
    for step in range(1, size):
        value = shifted(value, axis, 1)
        found.append(((me - step) % size, value))
    return found


def ring_scatter(value, axis, dim):
    me, size = place_of(axis)
    total = pick(value, (me - 1) % size, dim).astype(jnp.bfloat16)
    for step in range(1, size):
        part = pick(value, (me - 1 - step) % size, dim)
        total = shifted(total, axis, 1).astype(jnp.float32) + part.astype(jnp.float32)
        if step < size - 1:
            total = total.astype(jnp.bfloat16)
    return total


def gather_all(shard):
    tall, wide, cores = grid_of(lax.axis_size("pb"))
    rows, width = shard.shape
    slots = lax.axis_size("slot")
    column = jnp.zeros((slots, rows, width), shard.dtype)
    for index, block in ring_gather(shard, "slot"):
        column = lax.dynamic_update_index_in_dim(column, block, index, 0)
    column = column.reshape(slots * rows, width)
    half = slots * rows // 2
    core, _ = place_of("core")
    whole = jnp.zeros((tall * wide, cores, 2, half, width), shard.dtype)
    for side, (first, second) in enumerate((("x", "y"), ("y", "x"))):
        part = column[side * half : (side + 1) * half]
        for at_first, block in ring_gather(part, first):
            for at_second, block in ring_gather(block, second):
                x, y = (at_first, at_second) if first == "x" else (at_second, at_first)
                for at_core, block in ring_gather(block, "core"):
                    whole = lax.dynamic_update_slice(
                        whole, block[None, None, None], (y * wide + x, at_core, side, 0, 0)
                    )
    return whole.reshape(tall * wide * cores, slots * rows, width)


def scatter_pb(value):
    tall, wide, cores = grid_of(lax.axis_size("pb"))
    rest = value.shape[1:]
    value = value.reshape((tall * wide, cores) + rest)
    value = ring_scatter(value, "core", 1).astype(jnp.bfloat16)
    value = value.reshape((tall, wide) + rest)
    half = rest[0] // 2
    first = ring_scatter(value[:, :, :half], "x", 1)
    second = ring_scatter(value[:, :, half:], "y", 0)
    first = ring_scatter(first.astype(jnp.bfloat16), "y", 0)
    second = ring_scatter(second.astype(jnp.bfloat16), "x", 0)
    return jnp.concatenate([first, second], axis=0)


def scatter_all(value):
    n_pb, slots = lax.axis_size("pb"), lax.axis_size("slot")
    rows = value.shape[0] // (n_pb * slots)
    value = value.reshape((n_pb, slots, rows) + value.shape[1:])
    column = scatter_pb(value)
    return ring_scatter(column.astype(jnp.bfloat16), "slot", 0)


def sum_all(value, axes):
    for axis in axes:
        me, size = place_of(axis)
        parts = [value] + [shifted(value, axis, step) for step in range(1, size)]
        placed = jnp.stack(parts)
        value = jnp.sum(placed[(me - jnp.arange(size)) % size], axis=0)
    return value


def to_slots(value):
    me, size = place_of("slot")
    every, questions, steps, width = value.shape
    chunks = value.reshape(size, every // size, questions, steps, width)
    result = jnp.zeros((every // size, questions, size, steps, width), value.dtype)
    for step in range(size):
        block = pick(chunks, (me + step) % size, 0)
        if step:
            block = shifted(block, "slot", step)
        result = lax.dynamic_update_index_in_dim(result, block, (me - step) % size, 2)
    return result.reshape(every // size, questions, size * steps, width)


def to_positions(value):
    me, size = place_of("slot")
    own, questions, steps, width = value.shape
    chunks = value.reshape(own, questions, size, steps // size, width)
    result = jnp.zeros((size, own, questions, steps // size, width), value.dtype)
    for step in range(size):
        block = pick(chunks, (me + step) % size, 2)
        if step:
            block = shifted(block, "slot", step)
        result = lax.dynamic_update_index_in_dim(result, block, (me - step) % size, 0)
    return result.reshape(size * own, questions, steps // size, width)


def product(left, right):
    return jnp.dot(left, right, preferred_element_type=jnp.float32)


def contract_rows(left, right):
    return lax.dot_general(
        left, right, (((0,), (0,)), ((), ())), preferred_element_type=jnp.float32
    )


def contract_cols(left, right):
    return lax.dot_general(
        left, right, (((1,), (1,)), ((), ())), preferred_element_type=jnp.float32
    )


def norm_forward(resid, gain, shift):
    row_mean = jnp.mean(resid, axis=-1, keepdims=True)
    centered = resid - row_mean
    inv_root = lax.rsqrt(jnp.mean(centered * centered, axis=-1, keepdims=True) + eps_norm)
    normed = centered * inv_root
    return (normed * gain + shift, normed, inv_root)


def norm_backward(grad_out, normed, inv_root, gain):
    scaled = grad_out * gain
    grad_in = inv_root * (
        scaled
        - jnp.mean(scaled, axis=-1, keepdims=True)
        - normed * jnp.mean(scaled * normed, axis=-1, keepdims=True)
    )
    return (grad_in, jnp.sum(grad_out * normed, axis=0), jnp.sum(grad_out, axis=0))


def attend_forward(queries, key_rows, value_rows, allowed):
    scores = jnp.einsum("nqhe,nkhe->nhqk", queries, key_rows, preferred_element_type=jnp.float32)
    scores = jnp.where(allowed, scores, mask_fill)
    row_max = jnp.max(scores, axis=-1, keepdims=True)
    expos = jnp.exp(scores - row_max)
    row_sum = jnp.sum(expos, axis=-1, keepdims=True)
    probs_low = (expos / row_sum).astype(jnp.bfloat16)
    result = jnp.einsum(
        "nhqk,nkhe->nqhe", probs_low, value_rows, preferred_element_type=jnp.float32
    )
    return (result, row_max + jnp.log(row_sum))


def attend_backward(queries, key_rows, value_rows, allowed, row_lse, grad_out):
    scores = jnp.einsum("nqhe,nkhe->nhqk", queries, key_rows, preferred_element_type=jnp.float32)
    scores = jnp.where(allowed, scores, mask_fill)
    attn_probs = jnp.exp(scores - row_lse)
    grad_values = jnp.einsum(
        "nhqk,nqhe->nkhe",
        attn_probs.astype(jnp.bfloat16),
        grad_out,
        preferred_element_type=jnp.float32,
    )
    grad_probs = jnp.einsum(
        "nqhe,nkhe->nhqk", grad_out, value_rows, preferred_element_type=jnp.float32
    )
    row_delta = jnp.sum(grad_probs * attn_probs, axis=-1, keepdims=True)
    grad_scores = (attn_probs * (grad_probs - row_delta)).astype(jnp.bfloat16)
    grad_queries = jnp.einsum(
        "nhqk,nkhe->nqhe", grad_scores, key_rows, preferred_element_type=jnp.float32
    )
    grad_keys = jnp.einsum(
        "nhqk,nqhe->nkhe", grad_scores, queries, preferred_element_type=jnp.float32
    )
    return (grad_queries, grad_keys, grad_values)


PIECE = 128
CHUNK = 256


def vocab_tile(share):
    return max(d for d in range(16, 901, 16) if share % d == 0)


def each_count(live, chunks, run):
    for taken in range(1, chunks + 1):
        low = (taken - 1) * (CHUNK // PIECE)
        high = taken * (CHUNK // PIECE)
        upper = live <= high if taken < chunks else live >= 0

        @pl.when(jnp.logical_and(live > low, upper))
        def _():
            run(taken)


def rows_kernel(info, own_ids, mate_ids, own, mate, table, expo, sums, stats, acc, top, total):
    tile = pl.program_id(0)
    wide = table.shape[0]
    group = own.shape[0]
    chunks = group // CHUNK

    @pl.when(tile == 0)
    def _():
        acc[...] = jnp.zeros_like(acc)
        top[...] = jnp.full_like(top, mask_fill)
        total[...] = jnp.zeros_like(total)
        stats[...] = jnp.zeros_like(stats)

    lane = lax.broadcasted_iota(jnp.int32, (CHUNK, 128), 1)
    column = lax.broadcasted_iota(jnp.int32, (CHUNK, wide), 1)

    for side, (rows, ids) in enumerate(((own, own_ids), (mate, mate_ids))):

        def scores(chunk):
            return lax.dot_general(
                rows[chunk * CHUNK : (chunk + 1) * CHUNK, :],
                table[...],
                (((1,), (1,)), ((), ())),
                preferred_element_type=jnp.float32,
            )

        def soften(chunk, logits):
            here = slice(side * group + chunk * CHUNK, side * group + (chunk + 1) * CHUNK)
            target = ids[chunk * CHUNK : (chunk + 1) * CHUNK, :] - tile * wide
            logits = jnp.where(column == target, mask_fill, logits)
            before = top[here, 0:1]
            now = jnp.maximum(before, jnp.max(logits, axis=1, keepdims=True))
            fade = jnp.exp(before - now)
            grown = jnp.exp(logits - now)
            total[here, :] = jnp.broadcast_to(
                total[here, 0:1] * fade + jnp.sum(grown, axis=1, keepdims=True), (CHUNK, 128)
            )
            top[here, :] = jnp.broadcast_to(now, (CHUNK, 128))
            stats[here, :] = jnp.where(lane == tile, now, stats[here, :])
            grown = grown.astype(jnp.bfloat16)
            expo[0, here, :] = grown
            return here, grown, fade

        def gather(here, grown, fade):
            acc[here, :] = acc[here, :] * fade + jnp.dot(
                grown, table[...], preferred_element_type=jnp.float32
            )

        def run(taken):
            logits = [scores(0)]
            late = None
            for chunk in range(taken):
                if chunk + 1 < taken:
                    logits.append(scores(chunk + 1))
                ready = soften(chunk, logits[chunk])
                if late is not None:
                    gather(*late)
                late = ready
            gather(*late)

        each_count(info[1 + side], chunks, run)

    @pl.when(tile == pl.num_programs(0) - 1)
    def _():
        for chunk in range(2 * chunks):
            here = slice(chunk * CHUNK, (chunk + 1) * CHUNK)
            mass = total[here, :]
            share = jnp.where(mass[:, 0:1] > 0.0, 1.0 / jnp.maximum(mass[:, 0:1], 1e-30), 0.0)
            sums[here, :] = (acc[here, :] * share).astype(jnp.bfloat16)
            stats[here, :] = jnp.where(
                lane == 127, top[here, :] + jnp.log(jnp.maximum(mass, 1e-30)), stats[here, :]
            )


def rows_pass(info, own_ids, mate_ids, own, mate, table, cores):
    group, width = own.shape
    share = table.shape[0] // cores
    wide = vocab_tile(share)
    tiles = share // wide
    rows = 2 * group
    whole = lambda i, s: (0, 0)
    return pl.pallas_call(
        rows_kernel,
        grid_spec=pltpu.PrefetchScalarGridSpec(
            num_scalar_prefetch=1,
            grid=(tiles,),
            in_specs=[
                pl.BlockSpec((group, 1), whole),
                pl.BlockSpec((group, 1), whole),
                pl.BlockSpec((group, width), whole),
                pl.BlockSpec((group, width), whole),
                pl.BlockSpec((wide, width), lambda i, s: (s[0] * tiles + i, 0)),
            ],
            out_specs=[
                pl.BlockSpec((1, rows, wide), lambda i, s: (i, 0, 0)),
                pl.BlockSpec((rows, width), whole),
                pl.BlockSpec((rows, 128), whole),
            ],
            scratch_shapes=[
                pltpu.VMEM((rows, width), jnp.float32),
                pltpu.VMEM((rows, 128), jnp.float32),
                pltpu.VMEM((rows, 128), jnp.float32),
            ],
        ),
        out_shape=[
            jax.ShapeDtypeStruct((tiles, rows, wide), jnp.bfloat16),
            jax.ShapeDtypeStruct((rows, width), jnp.bfloat16),
            jax.ShapeDtypeStruct((rows, 128), jnp.float32),
        ],
        compiler_params=pltpu.CompilerParams(vmem_limit_bytes=56 << 20),
        cost_estimate=pl.CostEstimate(
            flops=4 * rows * share * width, bytes_accessed=4 * share * width, transcendentals=0
        ),
        name="rows_pass",
    )(info, own_ids, mate_ids, own, mate, table)


def table_kernel(first, sources, info, ids, scales, *refs):
    rows, expos, (out, acc) = refs[: 2 * sources], refs[2 * sources : 3 * sources], refs[3 * sources :]
    tile = pl.program_id(0) + first
    wide = expos[0].shape[2]
    group = rows[0].shape[0]
    acc[...] = jnp.zeros_like(acc)
    for part in range(2 * sources):
        low = part % 2 * group

        def run(taken):
            count = taken * CHUNK
            here = slice(part * group, part * group + count)
            scale = scales[here, :]
            lane = lax.broadcasted_iota(jnp.int32, (count, 128), 1)
            column = lax.broadcasted_iota(jnp.int32, (count, wide), 1)
            spread = jnp.sum(jnp.where(lane == tile, scale, 0.0), axis=1, keepdims=True)
            hit = jnp.sum(jnp.where(lane == 127, scale, 0.0), axis=1, keepdims=True)
            grad = expos[part // 2][0, low : low + count, :].astype(jnp.float32) * spread
            grad = jnp.where(column == ids[here, :] - tile * wide, hit, grad).astype(jnp.bfloat16)
            acc[...] += lax.dot_general(
                grad,
                rows[part][0:count, :],
                (((0,), (0,)), ((), ())),
                preferred_element_type=jnp.float32,
            )

        each_count(info[part], group // CHUNK, run)
    for place in range(out.shape[0]):
        size = out.shape[3]
        out[place, 0] = acc[:, place * size : (place + 1) * size].astype(jnp.bfloat16)


def table_pass(info, ids, scales, rows, expos, first, tiles, n_pb):
    sources = len(expos)
    _, both, wide = expos[0].shape
    group, width = rows[0].shape
    own = width // n_pb
    whole = lambda i, s: (0, 0)
    once = pl.Buffered(1)
    return pl.pallas_call(
        functools.partial(table_kernel, first, sources),
        grid_spec=pltpu.PrefetchScalarGridSpec(
            num_scalar_prefetch=1,
            grid=(tiles,),
            in_specs=[
                pl.BlockSpec((sources * both, 1), whole, pipeline_mode=once),
                pl.BlockSpec((sources * both, 128), whole, pipeline_mode=once),
            ]
            + [pl.BlockSpec((group, width), whole, pipeline_mode=once)] * (2 * sources)
            + [pl.BlockSpec((1, both, wide), lambda i, s: (i + first, 0, 0))] * sources,
            out_specs=pl.BlockSpec((n_pb, 1, wide, own), lambda i, s: (0, i, 0, 0)),
            scratch_shapes=[pltpu.VMEM((wide, width), jnp.float32)],
        ),
        out_shape=jax.ShapeDtypeStruct((n_pb, tiles, wide, own), jnp.bfloat16),
        compiler_params=pltpu.CompilerParams(vmem_limit_bytes=60 << 20),
        cost_estimate=pl.CostEstimate(
            flops=2 * sources * both * tiles * wide * width,
            bytes_accessed=4 * sources * both * tiles * wide,
            transcendentals=0,
        ),
        name=f"table_pass_{first}",
    )(info, ids, scales, *rows, *expos)


def gather_kernel(*refs):
    mats, rows = refs[:3], refs[3:5]
    full, laid = refs[5:8], refs[8:10]
    send, recv, near = refs[10:]
    slots = full[0].shape[1]
    pb, place = lax.axis_index("pb"), lax.axis_index("slot")
    mate = pb // 2 * 2 + (pb + 1) % 2
    side_x = pb // 4 * 4 + (pb + 2) % 4
    side_y = (pb + 4) % 8
    corner = (side_x + 4) % 8
    barrier = pltpu.get_barrier_semaphore()
    partners = [(mate, place), (side_x, place), (side_y, place)]
    partners += [(pb, (place + step) % slots) for step in range(1, slots)]
    for partner in partners:
        pl.semaphore_signal(barrier, inc=1, device_id=partner, device_id_type=pl.DeviceIdType.MESH)
    pl.semaphore_wait(barrier, len(partners))

    sent, unread, stays, ready = [], {}, [], {}

    def push(source, target, device):
        copy = pltpu.make_async_remote_copy(
            src_ref=source,
            dst_ref=target,
            send_sem=send.at[len(sent)],
            recv_sem=recv.at[len(sent)],
            device_id=device,
            device_id_type=pl.DeviceIdType.MESH,
        )
        copy.start()
        unread[len(sent)] = copy
        sent.append(copy)
        return len(sent) - 1

    def read(number):
        unread.pop(number).wait_recv()

    def put(source, target):
        copy = pltpu.make_async_copy(source, target, near.at[len(stays)])
        copy.start()
        stays.append(copy)

    def move_rows(step):
        goal = (place + step) % slots
        for source, target in zip(rows, laid):
            own = target.shape[0]
            block = source.at[pl.ds(goal * own, own)]
            spot = target.at[:, :, place]
            if step:
                push(block, spot, (pb, goal))
            else:
                put(block, spot)

    def part(mat, at_pb, origin, half):
        size = full[mat].shape[2] // 2
        return full[mat].at[at_pb, origin, pl.ds(half * size, size)]

    def own_moves(step, mat, origin, source):
        size = full[mat].shape[2] // 2
        first, second = (source.at[pl.ds(half * size, size)] for half in range(2))
        first_at, second_at = (part(mat, pb, origin, half) for half in range(2))
        ready[step, mat] = [
            push(first, first_at, (side_x, place)),
            push(second, second_at, (side_y, place)),
            push(first, first_at, (side_y, place)),
            push(second, second_at, (side_x, place)),
        ]
        push(source, full[mat].at[pb, origin], (mate, place))

    def onward(step, mat, origin):
        over_x, over_y, _, _ = ready[step, mat]
        read(over_x)
        block = part(mat, side_x, origin, 0)
        ready[step, mat].append(push(block, block, (side_y, place)))
        push(block, block, (mate, place))
        read(over_y)
        block = part(mat, side_y, origin, 1)
        ready[step, mat].append(push(block, block, (side_x, place)))
        push(block, block, (mate, place))

    def finish(step, mat, origin):
        _, _, over_y, over_x, first, second = ready[step, mat]
        for number, at_pb, half in (
            (over_y, side_y, 0),
            (over_x, side_x, 1),
            (first, corner, 0),
            (second, corner, 1),
        ):
            read(number)
            block = part(mat, at_pb, origin, half)
            push(block, block, (mate, place))

    count = len(mats)
    following = (pb, (place + 1) % slots)
    ring = [push(mats[mat], full[mat].at[pb, place], following) for mat in range(count)]
    for mat in range(count):
        own_moves(0, mat, place, mats[mat])
        put(mats[mat], full[mat].at[pb, place])
    move_rows(1)
    move_rows(0)
    for step in range(1, slots + 1):
        origin = (place + slots - step) % slots
        before = (place + slots - step + 1) % slots
        if step < slots:
            for mat in range(count):
                read(ring[mat])
                block = full[mat].at[pb, origin]
                if step < slots - 1:
                    ring[mat] = push(block, block, following)
                own_moves(step, mat, origin, block)
        if step == 1:
            move_rows(slots - 1)
        if step == 2:
            for other in range(2, slots - 1):
                move_rows(other)
        for mat in range(count):
            onward(step - 1, mat, before)
        for mat in range(count):
            finish(step - 1, mat, before)
    for number in sorted(unread):
        read(number)
    for copy in sent:
        copy.wait_send()
    for copy in stays:
        copy.wait()


def gather_inputs(x_in, memory, attn_w, ffn_in, ffn_out):
    n_pb, slots = lax.axis_size("pb"), lax.axis_size("slot")
    mats, rows = (attn_w, ffn_in, ffn_out), (x_in, memory)
    width = attn_w.shape[1]
    if (n_pb, slots) != (8, 4):
        return (
            to_slots(x_in),
            to_slots(memory),
            *(gather_all(mat).reshape(-1, width) for mat in mats),
        )
    shapes = [jax.ShapeDtypeStruct((n_pb, slots) + mat.shape, mat.dtype) for mat in mats]
    for row in rows:
        every, questions, steps, _ = row.shape
        shapes.append(
            jax.ShapeDtypeStruct((every // slots, questions, slots, steps, width), row.dtype)
        )
    copies = 13 * len(mats) * slots + (slots - 1) * (len(mats) + len(rows))
    anywhere = pl.BlockSpec(memory_space=pl.ANY)
    *full, x_here, mem_here = pl.pallas_call(
        gather_kernel,
        in_specs=[anywhere] * 5,
        out_specs=[anywhere] * 5,
        out_shape=shapes,
        scratch_shapes=[
            pltpu.SemaphoreType.DMA((copies,)),
            pltpu.SemaphoreType.DMA((copies,)),
            pltpu.SemaphoreType.DMA((len(mats) + len(rows),)),
        ],
        compiler_params=pltpu.CompilerParams(collective_id=0, has_side_effects=True),
        name="gather_inputs",
    )(*mats, *rows)
    own, questions, _, _, _ = x_here.shape
    return (
        x_here.reshape(own, questions, -1, width),
        mem_here.reshape(own, questions, -1, width),
        *(mat.reshape(-1, width) for mat in full),
    )


def body(
    x_in,
    memory,
    doc_scores,
    valid_count,
    target_ids,
    target_len,
    mem_len,
    attn_w,
    ffn_in,
    ffn_out,
    ffn_bias,
    norms,
    embedding,
):
    x_here, mem_here, attn_full, in_full, out_full = gather_inputs(
        x_in, memory, attn_w, ffn_in, ffn_out
    )
    slots_here, questions, tgt_steps, model_width = x_here.shape
    mem_steps = mem_here.shape[2]
    seq_count = slots_here * questions
    head_dim = model_width // HEADS
    scaling = head_dim ** (-0.5)
    blocks = [
        attn_full[block_index * model_width : (block_index + 1) * model_width]
        for block_index in range(8)
    ]

    def split_heads(value, steps):
        return value.reshape(seq_count, steps, HEADS, head_dim)

    def merge_rows(value):
        return value.reshape(-1, model_width)

    inputs = x_here.reshape(seq_count * tgt_steps, model_width)
    memory_rows = mem_here.reshape(seq_count * mem_steps, model_width)
    positions = jnp.arange(tgt_steps)
    causal = (positions[None, :] <= positions[:, None])[None, None]
    seen = (jnp.arange(mem_steps)[None, None, :] < mem_len[:, :, None]).reshape(
        seq_count, 1, 1, mem_steps
    )
    queries = (product(inputs, blocks[0]) * scaling).astype(jnp.bfloat16)
    key_rows = product(inputs, blocks[1]).astype(jnp.bfloat16)
    value_rows = product(inputs, blocks[2]).astype(jnp.bfloat16)
    self_out, self_lse = attend_forward(
        split_heads(queries, tgt_steps),
        split_heads(key_rows, tgt_steps),
        split_heads(value_rows, tgt_steps),
        causal,
    )
    self_out = merge_rows(self_out).astype(jnp.bfloat16)
    hidden_one, normed_one, root_one = norm_forward(
        inputs.astype(jnp.float32) + product(self_out, blocks[3]), norms[0], norms[1]
    )
    one_low = hidden_one.astype(jnp.bfloat16)
    cross_queries = (product(one_low, blocks[4]) * scaling).astype(jnp.bfloat16)
    cross_keys = product(memory_rows, blocks[5]).astype(jnp.bfloat16)
    cross_values = product(memory_rows, blocks[6]).astype(jnp.bfloat16)
    cross_out, cross_lse = attend_forward(
        split_heads(cross_queries, tgt_steps),
        split_heads(cross_keys, mem_steps),
        split_heads(cross_values, mem_steps),
        seen,
    )
    cross_out = merge_rows(cross_out).astype(jnp.bfloat16)
    hidden_two, normed_two, root_two = norm_forward(
        hidden_one + product(cross_out, blocks[7]), norms[2], norms[3]
    )
    two_low = hidden_two.astype(jnp.bfloat16)
    pre_act = contract_cols(two_low, in_full) + ffn_bias
    act_low = jax.nn.gelu(pre_act, approximate=False).astype(jnp.bfloat16)
    hidden_three, normed_three, root_three = norm_forward(
        hidden_two + product(act_low, out_full), norms[4], norms[5]
    )
    three_low = hidden_three.astype(jnp.bfloat16).reshape(
        slots_here, questions, tgt_steps, model_width
    )
    place, slot_count = place_of("slot")
    core, cores = place_of("core")
    vocab_here = embedding.shape[0]
    share = vocab_here // cores
    pieces = slots_here * questions

    def both_cores(value):
        return jnp.stack([value, shifted(value, "core", 1)]) if cores > 1 else value[None]

    tokens = jnp.concatenate([target_ids, valid_count[:, None], target_len[:, None]], axis=1)
    tokens = both_cores(tokens)
    ids_all, valid_all, len_all = tokens[:, :, :tgt_steps], tokens[:, :, -2], tokens[:, :, -1]

    local = target_ids - place * vocab_here
    held = jnp.logical_and(local >= 0, local < vocab_here)
    target_rows = jnp.take(embedding, jnp.clip(local, 0, vocab_here - 1), axis=0)
    target_rows = jnp.where(held[..., None], target_rows, jnp.zeros_like(target_rows))
    found = [shifted(target_rows, "slot", step) for step in range(1, slot_count)]
    target_rows = sum([f.astype(jnp.float32) for f in found], target_rows.astype(jnp.float32))

    slot_ids = jnp.arange(slot_count * slots_here).reshape(slot_count, 1, slots_here, 1)
    live_piece = (slot_ids < valid_all[None, :, None, :]).reshape(slot_count, -1, pieces)
    order_all = jnp.argsort(jnp.logical_not(live_piece), axis=-1, stable=True).astype(jnp.int32)
    live_all = jnp.sum(live_piece, axis=-1).astype(jnp.int32)
    piece_ids = jnp.broadcast_to(
        ids_all[None, :, None], (slot_count, cores, slots_here, questions, tgt_steps)
    ).reshape(slot_count, cores, pieces, tgt_steps)
    piece_ids = piece_ids - (place * vocab_here + core * share)
    sorted_ids = jnp.take_along_axis(piece_ids, order_all[..., None], axis=2)
    ring = (place - jnp.arange(slot_count)) % slot_count
    order_ring, live_ring, ids_ring = order_all[ring], live_all[ring], sorted_ids[ring]

    own_order = order_ring[0, 0]
    group = pieces * tgt_steps
    three_pieces = three_low.reshape(pieces, tgt_steps, model_width)
    moving = jnp.concatenate(
        [lax.dynamic_index_in_dim(three_pieces, own_order[i], 0) for i in range(pieces)], axis=0
    ).reshape(group, model_width)

    def join(first, second):
        rows_a, log_a = first
        rows_b, log_b = second
        log = jnp.logaddexp(log_a, log_b)
        rows = rows_a.astype(jnp.float32) * jnp.exp(log_a - log)[:, None]
        rows = rows + rows_b.astype(jnp.float32) * jnp.exp(log_b - log)[:, None]
        return rows, log

    def lower(part):
        return part[0].astype(jnp.bfloat16), part[1]

    row_list, expo_list, stat_list = [], [], []
    partial, own_part = None, None
    for step in range(slot_count):
        if step:
            moving, _ = lax.optimization_barrier((moving, expo_list[-1]))
        other = shifted(moving, "core", 1)
        following = shifted(moving, "slot", 1) if step + 1 < slot_count else None
        info = jnp.concatenate([core[None].astype(jnp.int32), live_ring[step]])
        expo, sums, stats = rows_pass(
            info,
            ids_ring[step, 0].reshape(group, 1),
            ids_ring[step, 1].reshape(group, 1),
            moving,
            other,
            embedding,
            cores,
        )
        row_list += [moving, other]
        expo_list.append(expo)
        stat_list.append(stats)
        logs = stats[:, 127]
        arrived = (shifted(sums[group:], "core", 1), shifted(logs[group:], "core", 1))
        part = lower(join((sums[:group], logs[:group]), arrived))
        if step == 0:
            own_part = part
        else:
            if partial is not None:
                part = lower(join(part, partial))
            partial = tuple(shifted(value, "slot", 1) for value in part)
        moving = following
    mean_rows, log_rest = join(own_part, partial)
    back = jnp.argsort(own_order)

    def natural(value):
        value = value.reshape((pieces, tgt_steps) + value.shape[1:])
        return jnp.concatenate(
            [lax.dynamic_index_in_dim(value, back[i], 0) for i in range(pieces)], axis=0
        ).reshape((slots_here, questions, tgt_steps) + value.shape[2:])

    mean_rows, log_rest = natural(mean_rows), natural(log_rest)
    target_logit = jnp.sum(three_low.astype(jnp.float32) * target_rows[None], axis=-1)

    packed = jnp.stack([log_rest, target_logit])
    spread = [packed] + [shifted(packed, "slot", step) for step in range(1, slot_count)]
    spread = jnp.stack(spread)[ring]
    spread = both_cores(spread)
    spread = spread.transpose(2, 1, 3, 0, 4, 5).reshape(
        2, slot_count * slots_here, cores, questions, tgt_steps
    )
    rest_all, hit_all = spread[0], spread[1]
    log_norm = jnp.logaddexp(rest_all, hit_all)
    live = positions < len_all[..., None]
    lengths = len_all.astype(jnp.float32)
    per_slot = jnp.sum(jnp.where(live[None], hit_all - log_norm, 0.0), axis=3) / lengths[None]
    valid = jnp.arange(per_slot.shape[0])[:, None, None] < valid_all[None]
    scores_t = both_cores(doc_scores).transpose(2, 0, 1)
    joint = jnp.where(valid, scores_t + per_slot, mask_fill)
    prior = jnp.where(valid, scores_t, mask_fill)
    joint_total = jax.nn.logsumexp(joint, axis=0)
    neg_marginal = jax.nn.logsumexp(prior, axis=0) - joint_total
    log_post = joint - joint_total
    posterior = jnp.exp(log_post)
    entropy_q = -jnp.sum(posterior * log_post, axis=0)
    objective_part = jnp.sum((lengths * (neg_marginal + entropy_weight * entropy_q))[0])
    slot_weight = -posterior * (1.0 + entropy_weight * (log_post + entropy_q[None]))
    token_weight = jnp.where(live[None], slot_weight[..., None], 0.0)
    hit_weight = token_weight * jax.nn.sigmoid(rest_all - hit_all)

    def own_slots(value):
        value = value[:, 0].reshape(slot_count, slots_here, questions, tgt_steps)
        return pick(value, place, 0)

    grad_three = own_slots(hit_weight)[..., None] * (target_rows[None] - mean_rows)
    grad_three = grad_three.reshape(-1, model_width)

    def ring_rows(value):
        value = value.reshape(slot_count, slots_here, cores, questions, tgt_steps)
        value = value.transpose(0, 2, 1, 3, 4).reshape(slot_count, cores, pieces, tgt_steps)
        value = jnp.take_along_axis(value, order_all[..., None], axis=2)
        return value[ring].reshape(-1, 1)

    weight_rows, norm_rows, hit_rows = (
        ring_rows(token_weight),
        ring_rows(log_norm),
        ring_rows(hit_weight),
    )
    tops = jnp.concatenate(stat_list, axis=0)
    scales = jnp.where(weight_rows == 0.0, 0.0, -weight_rows * jnp.exp(tops - norm_rows))
    scales = jnp.where(jnp.arange(128)[None, :] == 127, hit_rows, scales)
    tiles = expo_list[0].shape[0]
    cut = tiles // 2 + 1
    n_pb = lax.axis_size("pb")
    tall, wide, _ = grid_of(n_pb)
    grad_pieces = []
    for first, count in ((0, cut), (cut, tiles - cut)):
        chunk = table_pass(
            live_ring.reshape(-1),
            ids_ring.reshape(-1, 1),
            scales,
            row_list,
            expo_list,
            first,
            count,
            n_pb,
        )
        chunk = chunk.reshape((tall, wide, cores, -1) + chunk.shape[3:])
        half = chunk.shape[3] // 2
        early = ring_scatter(chunk[:, :, :, :half], "x", 1).astype(jnp.bfloat16)
        late = ring_scatter(chunk[:, :, :, half:], "y", 0).astype(jnp.bfloat16)
        early = ring_scatter(early, "y", 0).astype(jnp.bfloat16)
        late = ring_scatter(late, "x", 0).astype(jnp.bfloat16)
        chunk = jnp.concatenate([early, late], axis=1)
        kept = pick(chunk, core, 0)
        given = shifted(pick(chunk, 1 - core, 0), "core", 1)
        grad_pieces.append(jnp.stack([kept, given]))
    grad_embed = jnp.concatenate(grad_pieces, axis=1)
    grad_embed = jnp.where(core == 0, grad_embed, grad_embed[::-1])
    grad_embed = grad_embed.reshape(vocab_here, -1).astype(jnp.float32)
    back_blocks, in_back, out_back = blocks, in_full, out_full
    grad_res_three, gain_three, shift_three = norm_backward(
        grad_three, normed_three, root_three, norms[4]
    )
    grad_ffn = grad_res_three.astype(jnp.bfloat16)
    grad_out_w = contract_rows(act_low, grad_ffn)
    grad_act = contract_cols(grad_ffn, out_back)
    cdf_part = 0.5 * (1.0 + lax.erf(pre_act * root_half))
    pdf_part = pre_act * inv_root_tau * jnp.exp(-0.5 * pre_act * pre_act)
    grad_pre = (grad_act * (cdf_part + pdf_part)).astype(jnp.bfloat16)
    grad_in_w = contract_rows(grad_pre, two_low)
    grad_bias = jnp.sum(grad_pre.astype(jnp.float32), axis=0)
    grad_two = grad_res_three + product(grad_pre, in_back)
    grad_res_two, gain_two, shift_two = norm_backward(grad_two, normed_two, root_two, norms[2])
    grad_cross = grad_res_two.astype(jnp.bfloat16)
    grad_w7 = contract_rows(cross_out, grad_cross)
    grad_cross_out = contract_cols(grad_cross, back_blocks[7]).astype(jnp.bfloat16)
    cq_grad, ck_grad, cv_grad = attend_backward(
        split_heads(cross_queries, tgt_steps),
        split_heads(cross_keys, mem_steps),
        split_heads(cross_values, mem_steps),
        seen,
        cross_lse,
        split_heads(grad_cross_out, tgt_steps),
    )
    cq_grad = merge_rows(cq_grad).astype(jnp.bfloat16)
    ck_grad = merge_rows(ck_grad).astype(jnp.bfloat16)
    cv_grad = merge_rows(cv_grad).astype(jnp.bfloat16)
    grad_w4 = contract_rows(one_low, cq_grad) * scaling
    grad_w5 = contract_rows(memory_rows, ck_grad)
    grad_w6 = contract_rows(memory_rows, cv_grad)
    grad_memory = (
        contract_cols(ck_grad, back_blocks[5]) + contract_cols(cv_grad, back_blocks[6])
    ).astype(jnp.bfloat16)
    grad_one = grad_res_two + contract_cols(cq_grad, back_blocks[4]) * scaling
    grad_res_one, gain_one, shift_one = norm_backward(grad_one, normed_one, root_one, norms[0])
    grad_attn_out = grad_res_one.astype(jnp.bfloat16)
    grad_w3 = contract_rows(self_out, grad_attn_out)
    grad_self_out = contract_cols(grad_attn_out, back_blocks[3]).astype(jnp.bfloat16)
    sq_grad, sk_grad, sv_grad = attend_backward(
        split_heads(queries, tgt_steps),
        split_heads(key_rows, tgt_steps),
        split_heads(value_rows, tgt_steps),
        causal,
        self_lse,
        split_heads(grad_self_out, tgt_steps),
    )
    sq_grad = merge_rows(sq_grad).astype(jnp.bfloat16)
    sk_grad = merge_rows(sk_grad).astype(jnp.bfloat16)
    sv_grad = merge_rows(sv_grad).astype(jnp.bfloat16)
    grad_w0 = contract_rows(inputs, sq_grad) * scaling
    grad_w1 = contract_rows(inputs, sk_grad)
    grad_w2 = contract_rows(inputs, sv_grad)
    grad_inputs = (
        grad_res_one
        + contract_cols(sq_grad, back_blocks[0]) * scaling
        + contract_cols(sk_grad, back_blocks[1])
        + contract_cols(sv_grad, back_blocks[2])
    )
    grad_inputs = grad_inputs.astype(jnp.bfloat16).reshape(
        slots_here, questions, tgt_steps, model_width
    )
    grad_memory = grad_memory.reshape(slots_here, questions, mem_steps, model_width)
    grad_inputs, grad_memory = (
        to_positions(grad_inputs),
        to_positions(grad_memory),
    )
    grad_attn = jnp.concatenate(
        [grad_w0, grad_w1, grad_w2, grad_w3, grad_w4, grad_w5, grad_w6, grad_w7], axis=0
    )
    grad_attn, grad_in_w, grad_out_w = (
        scatter_all(grad_attn),
        scatter_all(grad_in_w),
        scatter_all(grad_out_w),
    )
    small = jnp.concatenate(
        [
            jnp.stack([gain_one, shift_one, gain_two, shift_two, gain_three, shift_three], axis=0),
            grad_bias.reshape(-1, model_width),
            jnp.zeros((1, model_width), jnp.float32)
            .at[0, :3]
            .set(jnp.stack([objective_part, jnp.sum(lengths[0]), jnp.sum(entropy_q[0])])),
        ],
        axis=0,
    )
    small = sum_all(small, ("core", "x", "y", "slot"))
    grad_norms = small[:6]
    loss = small[-1, 0] / small[-1, 1]
    entropy = small[-1, 2] / (questions * n_pb * slot_count)
    grad_bias = small[6:-1].reshape(-1)
    own_bias = grad_bias.shape[0] // (lax.axis_size("pb") * slot_count)
    grad_bias = lax.dynamic_slice_in_dim(
        grad_bias,
        (lax.axis_index("pb") * slot_count + lax.axis_index("slot")) * own_bias,
        own_bias,
    )
    return (
        loss,
        entropy,
        grad_inputs,
        grad_memory,
        grad_attn,
        grad_in_w,
        grad_out_w,
        grad_bias,
        grad_norms,
        grad_embed,
    )


def solution(mesh):
    placed = (
        P(None, "pb", "slot", None),
        P(None, "pb", "slot", None),
        P("pb", None),
        P("pb"),
        P("pb", None),
        P("pb"),
        P("slot", "pb"),
        P(("pb", "slot"), None),
        P(("pb", "slot"), None),
        P(("pb", "slot"), None),
        P(),
        P(),
        P("slot", None),
    )
    return jax.shard_map(
        body,
        mesh=mesh,
        in_specs=placed,
        out_specs=(
            P(),
            P(),
            P(None, "pb", "slot", None),
            P(None, "pb", "slot", None),
            P(("pb", "slot"), None),
            P(("pb", "slot"), None),
            P(("pb", "slot"), None),
            P(("pb", "slot")),
            P(),
            P("slot", "pb"),
        ),
        check_vma=False,
    )
```

```python
import functools

import jax
import jax.numpy as jnp
from jax import lax
from jax.experimental import pallas as pl
from jax.experimental.pallas import tpu as pltpu
from jax.sharding import PartitionSpec as P

HEADS = 16


eps_norm = 1e-05
entropy_weight = 0.25
mask_fill = -1e30
root_half = 0.7071067811865476
inv_root_tau = 0.3989422804014327


def grid_of(n_pb):
    cores = 2 if n_pb % 2 == 0 else 1
    chips = n_pb // cores
    wide = max(d for d in range(1, chips + 1) if chips % d == 0 and d * d <= chips)
    return chips // wide, wide, cores


def shifted(value, axis, step):
    if axis == "slot":
        size = lax.axis_size("slot")
        return lax.ppermute(value, "slot", [(i, (i + step) % size) for i in range(size)])
    n_pb = lax.axis_size("pb")
    tall, wide, cores = grid_of(n_pb)
    pairs = []
    for i in range(n_pb):
        y, x, c = i // (wide * cores), i // cores % wide, i % cores
        if axis == "y":
            y = (y + step) % tall
        elif axis == "x":
            x = (x + step) % wide
        else:
            c = (c + step) % cores
        pairs.append((i, (y * wide + x) * cores + c))
    return lax.ppermute(value, "pb", pairs)


def place_of(axis):
    if axis == "slot":
        return lax.axis_index("slot"), lax.axis_size("slot")
    tall, wide, cores = grid_of(lax.axis_size("pb"))
    i = lax.axis_index("pb")
    if axis == "y":
        return i // (wide * cores), tall
    if axis == "x":
        return i // cores % wide, wide
    return i % cores, cores


def after(value, *tokens):
    for token in tokens:
        first = token[(0,) * token.ndim].astype(jnp.float32)
        value = jnp.where(first == first, value, jnp.zeros_like(value))
    return value


def pick(value, index, dim):
    return lax.dynamic_index_in_dim(value, index, dim, keepdims=False)


def ring_gather(value, axis):
    me, size = place_of(axis)
    found = [(me, value)]
    for step in range(1, size):
        value = shifted(value, axis, 1)
        found.append(((me - step) % size, value))
    return found


def ring_scatter(value, axis, dim, late=None):
    me, size = place_of(axis)
    total = pick(value, (me - 1) % size, dim).astype(jnp.bfloat16)
    for step in range(1, size):
        part = pick(value, (me - 1 - step) % size, dim)
        total = shifted(total, axis, 1)
        if late is not None:
            total = after(total, late)
        total = total.astype(jnp.float32) + part.astype(jnp.float32)
        if step < size - 1:
            total = total.astype(jnp.bfloat16)
    return total


def ring_first(value, axis, dim):
    me, size = place_of(axis)
    return pick(value, (me - 1) % size, dim).astype(jnp.bfloat16)


def gather_all(shard):
    tall, wide, cores = grid_of(lax.axis_size("pb"))
    rows, width = shard.shape
    slots = lax.axis_size("slot")
    column = jnp.zeros((slots, rows, width), shard.dtype)
    for index, block in ring_gather(shard, "slot"):
        column = lax.dynamic_update_index_in_dim(column, block, index, 0)
    column = column.reshape(slots * rows, width)
    half = slots * rows // 2
    core, _ = place_of("core")
    whole = jnp.zeros((tall * wide, cores, 2, half, width), shard.dtype)
    for side, (first, second) in enumerate((("x", "y"), ("y", "x"))):
        part = column[side * half : (side + 1) * half]
        for at_first, block in ring_gather(part, first):
            for at_second, block in ring_gather(block, second):
                x, y = (at_first, at_second) if first == "x" else (at_second, at_first)
                for at_core, block in ring_gather(block, "core"):
                    whole = lax.dynamic_update_slice(
                        whole, block[None, None, None], (y * wide + x, at_core, side, 0, 0)
                    )
    return whole.reshape(tall * wide * cores, slots * rows, width)


def scatter_pb(value, lates=(None, None, None)):
    tall, wide, cores = grid_of(lax.axis_size("pb"))
    rest = value.shape[1:]
    value = value.reshape((tall * wide, cores) + rest)
    value = ring_scatter(value, "core", 1, lates[0]).astype(jnp.bfloat16)
    value = value.reshape((tall, wide) + rest)
    half = rest[0] // 2
    first = ring_scatter(value[:, :, :half], "x", 1, lates[1])
    second = ring_scatter(value[:, :, half:], "y", 0, lates[1])
    first = ring_scatter(first.astype(jnp.bfloat16), "y", 0, lates[2])
    second = ring_scatter(second.astype(jnp.bfloat16), "x", 0, lates[2])
    return jnp.concatenate([first, second], axis=0)


def scatter_all(value):
    n_pb, slots = lax.axis_size("pb"), lax.axis_size("slot")
    rows = value.shape[0] // (n_pb * slots)
    value = value.reshape((n_pb, slots, rows) + value.shape[1:])
    column = scatter_pb(value)
    return ring_scatter(column.astype(jnp.bfloat16), "slot", 0)


def scatter_slot(value, late):
    me, size = place_of("slot")
    parts = [
        after(shifted(pick(value, (me + step) % size, 0), "slot", step), late)
        for step in range(1, size)
    ]
    return sum([part.astype(jnp.float32) for part in parts], pick(value, me, 0).astype(jnp.float32))


def sum_all(value, axes):
    for axis in axes:
        me, size = place_of(axis)
        parts = [value] + [shifted(value, axis, step) for step in range(1, size)]
        placed = jnp.stack(parts)
        value = jnp.sum(placed[(me - jnp.arange(size)) % size], axis=0)
    return value


def to_slots(value):
    me, size = place_of("slot")
    every, questions, steps, width = value.shape
    chunks = value.reshape(every // size, size, questions, steps, width)
    result = jnp.zeros((every // size, questions, size, steps, width), value.dtype)
    for step in range(size):
        block = pick(chunks, (me + step) % size, 1)
        if step:
            block = shifted(block, "slot", step)
        result = lax.dynamic_update_index_in_dim(result, block, (me - step) % size, 2)
    return result.reshape(every // size, questions, size * steps, width)


def leave_slots(value):
    me, size = place_of("slot")
    own, questions, steps, width = value.shape
    chunks = value.reshape(own, questions, size, steps // size, width)
    return [pick(chunks, (me + step) % size, 2) for step in range(size)]


def to_positions(blocks, late=None):
    me, size = place_of("slot")
    own, questions, steps, width = blocks[0].shape
    result = jnp.zeros((own, size, questions, steps, width), blocks[0].dtype)
    for step, block in enumerate(blocks):
        if step:
            block = shifted(block, "slot", step)
            block = block if late is None else after(block, late)
        result = lax.dynamic_update_index_in_dim(result, block, (me - step) % size, 1)
    return result.reshape(size * own, questions, steps, width)


def product(left, right):
    return jnp.dot(left, right, preferred_element_type=jnp.float32)


def contract_rows(left, right):
    return lax.dot_general(
        left, right, (((0,), (0,)), ((), ())), preferred_element_type=jnp.float32
    )


def contract_cols(left, right):
    return lax.dot_general(
        left, right, (((1,), (1,)), ((), ())), preferred_element_type=jnp.float32
    )


def norm_forward(resid, gain, shift):
    row_mean = jnp.mean(resid, axis=-1, keepdims=True)
    centered = resid - row_mean
    inv_root = lax.rsqrt(jnp.mean(centered * centered, axis=-1, keepdims=True) + eps_norm)
    normed = centered * inv_root
    return (normed * gain + shift, normed, inv_root)


def norm_backward(grad_out, normed, inv_root, gain):
    scaled = grad_out * gain
    grad_in = inv_root * (
        scaled
        - jnp.mean(scaled, axis=-1, keepdims=True)
        - normed * jnp.mean(scaled * normed, axis=-1, keepdims=True)
    )
    return (grad_in, jnp.sum(grad_out * normed, axis=0), jnp.sum(grad_out, axis=0))


def two_heads(value):
    left = lax.broadcasted_iota(jnp.int32, value.shape, 1) < value.shape[1] // 2
    none = jnp.zeros_like(value)
    return jnp.concatenate([jnp.where(left, value, none), jnp.where(left, none, value)], axis=0)


def one_pair(value):
    rows = value.shape[0] // 2
    left = lax.broadcasted_iota(jnp.int32, (rows, value.shape[1]), 1) < value.shape[1] // 2
    return jnp.where(left, value[:rows], value[rows:])


def pair_scores(info, causal, queries, key_rows):
    scores = lax.dot_general(
        queries, key_rows, (((1,), (1,)), ((), ())), preferred_element_type=jnp.float32
    )
    column = lax.broadcasted_iota(jnp.int32, scores.shape, 1)
    if causal:
        row = lax.broadcasted_iota(jnp.int32, scores.shape, 0)
        allowed = column <= jnp.where(row < scores.shape[0] // 2, row, row - scores.shape[0] // 2)
    else:
        allowed = column < info[pl.program_id(0)]
    return jnp.where(allowed, scores, mask_fill)


def attend_kernel(causal, info, queries, keys, values, out, logs):
    steps, width = queries.shape
    lane = lax.broadcasted_iota(jnp.int32, (steps, 128), 1)
    kept = jnp.zeros((steps, 128), jnp.float32)
    for pair in range(width // 128):
        here = slice(pair * 128, (pair + 1) * 128)
        scores = pair_scores(info, causal, two_heads(queries[:, here]), keys[:, here])
        row_max = jnp.max(scores, axis=1, keepdims=True)
        expos = jnp.exp(scores - row_max)
        row_sum = jnp.sum(expos, axis=1, keepdims=True)
        probs = (expos * (1.0 / row_sum)).astype(jnp.bfloat16)
        out[:, here] = one_pair(
            jnp.dot(probs, values[:, here], preferred_element_type=jnp.float32)
        ).astype(jnp.bfloat16)
        log = row_max + jnp.log(row_sum)
        kept = jnp.where(lane == 2 * pair, log[:steps], kept)
        kept = jnp.where(lane == 2 * pair + 1, log[steps:], kept)
    logs[...] = kept


def attend_back_kernel(causal, info, queries, keys, values, logs, grads, *refs):
    d_queries, d_keys, d_values = refs[-3:]
    steps, width = queries.shape
    rows_first = (((0,), (0,)), ((), ()))
    for pair in range(width // 128):
        here = slice(pair * 128, (pair + 1) * 128)
        both = two_heads(queries[:, here])
        both_grads = two_heads(grads[:, here])
        log = jnp.concatenate(
            [logs[:, 2 * pair : 2 * pair + 1], logs[:, 2 * pair + 1 : 2 * pair + 2]], axis=0
        )
        probs = jnp.exp(pair_scores(info, causal, both, keys[:, here]) - log)
        d_probs = lax.dot_general(
            both_grads, values[:, here], (((1,), (1,)), ((), ())), preferred_element_type=jnp.float32
        )
        d_values[:, here] = lax.dot_general(
            probs.astype(jnp.bfloat16), both_grads, rows_first, preferred_element_type=jnp.float32
        ).astype(jnp.bfloat16)
        delta = jnp.sum(d_probs * probs, axis=1, keepdims=True)
        d_scores = (probs * (d_probs - delta)).astype(jnp.bfloat16)
        d_queries[:, here] = one_pair(
            jnp.dot(d_scores, keys[:, here], preferred_element_type=jnp.float32)
        ).astype(jnp.bfloat16)
        d_keys[:, here] = lax.dot_general(
            d_scores, both, rows_first, preferred_element_type=jnp.float32
        ).astype(jnp.bfloat16)


def attend(causal, lengths, queries, keys, values, logs=None, grads=None, earlier=()):
    count = lengths.shape[0]
    width = queries.shape[1]
    steps, spans = queries.shape[0] // count, keys.shape[0] // count
    short = pl.BlockSpec((steps, width), lambda i, s: (i, 0))
    long = pl.BlockSpec((spans, width), lambda i, s: (i, 0))
    thin = pl.BlockSpec((steps, 128), lambda i, s: (i, 0))
    like = lambda value: jax.ShapeDtypeStruct(value.shape, jnp.bfloat16)
    if grads is None:
        kernel, operands = attend_kernel, (queries, keys, values)
        in_specs, out_specs = [short, long, long], [short, thin]
        out_shape = [like(queries), jax.ShapeDtypeStruct((queries.shape[0], 128), jnp.float32)]
    else:
        kernel, operands = attend_back_kernel, (queries, keys, values, logs, grads, *earlier)
        in_specs, out_specs = [short, long, long, thin, short], [short, long, long]
        in_specs += [pl.BlockSpec(memory_space=pl.ANY)] * len(earlier)
        out_shape = [like(queries), like(keys), like(values)]
    flops = (4 if grads is None else 10) * queries.shape[0] * spans * width
    return pl.pallas_call(
        functools.partial(kernel, causal),
        grid_spec=pltpu.PrefetchScalarGridSpec(
            num_scalar_prefetch=1, grid=(count,), in_specs=in_specs, out_specs=out_specs
        ),
        out_shape=out_shape,
        compiler_params=pltpu.CompilerParams(vmem_limit_bytes=48 << 20),
        cost_estimate=pl.CostEstimate(
            flops=4 * flops, bytes_accessed=8 * keys.shape[0] * width, transcendentals=0
        ),
        name=("self" if causal else "cross") + ("_attend" if grads is None else "_attend_back"),
    )(lengths, *operands)


def gelu_parts(value):
    place = 1.0 / (1.0 + 0.3275911 * root_half * jnp.abs(value))
    bell = jnp.exp(-0.5 * value * value)
    series = 1.061405429
    for factor in (-1.453152027, 1.421413741, -0.284496736, 0.254829592):
        series = series * place + factor
    tail = 0.5 * series * place * bell
    share = jnp.where(value > 0.0, 1.0 - tail, tail)
    return value * share, share + value * (inv_root_tau * bell)


PIECE = 128
CHUNK = 256


def vocab_tile(share):
    return max(d for d in range(16, 901, 16) if share % d == 0)


def columns(block):
    return jnp.concatenate([block] * 16, axis=0).T


def each_count(live, chunks, run):
    for taken in range(1, chunks + 1):
        above = live > (taken - 1) * CHUNK
        upto = live <= taken * CHUNK if taken < chunks else live >= 0

        @pl.when(jnp.logical_and(above, upto))
        def _():
            run(taken)


def piece_places(info, step, count):
    base = 1 + step * (count + 1)
    return [pl.multiple_of(info[base + i], 16) for i in range(count)], info[base + count]


def rows_kernel(step, info, ids, own, mate, table, *refs):
    expo, packed, tops, own_sums, mate_sums, own_logs, mate_logs, acc, top, total, marks = refs[-11:]
    expo, packed, tops = expo.at[0], packed.at[0], tops.at[0]
    tile = pl.program_id(0)
    wide = table.shape[0]
    pieces = own.shape[0] // PIECE
    count = 2 * pieces
    places, live = piece_places(info, step, count)

    @pl.when(tile == 0)
    def _():
        acc[...] = jnp.zeros_like(acc)
        top[...] = jnp.full_like(top, mask_fill)
        total[...] = jnp.zeros_like(total)
        tops[...] = jnp.zeros_like(tops)
        packed[...] = jnp.zeros_like(packed)
        marks[...] = jnp.full_like(marks, -1.0)
        for piece in range(count):
            side = own if piece < pieces else mate
            low = piece % pieces * PIECE
            packed[pl.ds(places[piece], PIECE), :] = side[low : low + PIECE, :]
            marks[pl.ds(places[piece], PIECE), :] = columns(ids[piece])

    lane = lax.broadcasted_iota(jnp.int32, (CHUNK, 128), 1)
    column = lax.broadcasted_iota(jnp.int32, (CHUNK, wide), 1)

    def scores(chunk):
        return lax.dot_general(
            packed[chunk * CHUNK : (chunk + 1) * CHUNK, :],
            table[...],
            (((1,), (1,)), ((), ())),
            preferred_element_type=jnp.float32,
        )

    def soften(chunk, logits):
        here = slice(chunk * CHUNK, (chunk + 1) * CHUNK)
        target = marks[here, 0:1].astype(jnp.int32) - tile * wide
        logits = jnp.where(column == target, mask_fill, logits)
        before = top[here, 0:1]
        now = jnp.maximum(before, jnp.max(logits, axis=1, keepdims=True))
        fade = jnp.exp(before - now)
        grown = jnp.exp(logits - now)
        total[here, :] = jnp.broadcast_to(
            total[here, 0:1] * fade + jnp.sum(grown, axis=1, keepdims=True), (CHUNK, 128)
        )
        top[here, :] = jnp.broadcast_to(now, (CHUNK, 128))
        tops[here, :] = jnp.where(lane == tile, now, tops[here, :])
        grown = grown.astype(jnp.bfloat16)
        expo[0, here, :] = grown
        return here, grown, fade

    def gather(here, grown, fade):
        acc[here, :] = acc[here, :] * fade + jnp.dot(
            grown, table[...], preferred_element_type=jnp.float32
        )

    def run(taken):
        logits = [scores(0)]
        late = None
        for chunk in range(taken):
            if chunk + 1 < taken:
                logits.append(scores(chunk + 1))
            ready = soften(chunk, logits[chunk])
            if late is not None:
                gather(*late)
            late = ready
        gather(*late)

    each_count(live, count * PIECE // CHUNK, run)

    @pl.when(tile == pl.num_programs(0) - 1)
    def _():
        for piece in range(count):
            here = pl.ds(places[piece], PIECE)
            mass = total[here, :]
            share = jnp.where(mass > 0.0, 1.0 / jnp.maximum(mass, 1e-30), 0.0)[:, 0:1]
            sums, logs = (own_sums, own_logs) if piece < pieces else (mate_sums, mate_logs)
            low = piece % pieces * PIECE
            sums[low : low + PIECE, :] = (acc[here, :] * share).astype(jnp.bfloat16)
            logs[piece % pieces] = (top[here, :] + jnp.log(jnp.maximum(mass, 1e-30))).T[0:8]


def rows_pass(step, steps, info, ids, own, mate, table, cores, kept, earlier):
    group, width = own.shape
    share = table.shape[0] // cores
    wide = vocab_tile(share)
    tiles = share // wide
    rows = 2 * group
    count = rows // PIECE
    room = rows + PIECE
    whole = lambda i, s: (0, 0)
    cube = lambda i, s: (0, 0, 0)
    return pl.pallas_call(
        functools.partial(rows_kernel, step),
        grid_spec=pltpu.PrefetchScalarGridSpec(
            num_scalar_prefetch=1,
            grid=(tiles,),
            in_specs=[
                pl.BlockSpec((count, 8, 128), lambda i, s: (step, 0, 0)),
                pl.BlockSpec((group, width), whole),
                pl.BlockSpec((group, width), whole),
                pl.BlockSpec((wide, width), lambda i, s: (s[0] * tiles + i, 0)),
            ]
            + [pl.BlockSpec(memory_space=pl.ANY)] * (len(kept) + len(earlier)),
            out_specs=[
                pl.BlockSpec((1, 1, rows, wide), lambda i, s: (step, i, 0, 0)),
                pl.BlockSpec((1, room, width), lambda i, s: (step, 0, 0)),
                pl.BlockSpec((1, room, 128), lambda i, s: (step, 0, 0)),
                pl.BlockSpec((group, width), whole),
                pl.BlockSpec((group, width), whole),
                pl.BlockSpec((count // 2, 8, 128), cube),
                pl.BlockSpec((count // 2, 8, 128), cube),
            ],
            scratch_shapes=[
                pltpu.VMEM((room, width), jnp.float32),
                pltpu.VMEM((room, 128), jnp.float32),
                pltpu.VMEM((room, 128), jnp.float32),
                pltpu.VMEM((room, 128), jnp.float32),
            ],
        ),
        out_shape=[
            jax.ShapeDtypeStruct((steps, tiles, rows, wide), jnp.bfloat16),
            jax.ShapeDtypeStruct((steps, room, width), jnp.bfloat16),
            jax.ShapeDtypeStruct((steps, room, 128), jnp.float32),
            jax.ShapeDtypeStruct((group, width), jnp.bfloat16),
            jax.ShapeDtypeStruct((group, width), jnp.bfloat16),
            jax.ShapeDtypeStruct((count // 2, 8, 128), jnp.float32),
            jax.ShapeDtypeStruct((count // 2, 8, 128), jnp.float32),
        ],
        input_output_aliases={5 + place: place for place in range(len(kept))},
        compiler_params=pltpu.CompilerParams(vmem_limit_bytes=60 << 20),
        cost_estimate=pl.CostEstimate(
            flops=4 * rows * share * width, bytes_accessed=4 * share * width, transcendentals=0
        ),
        name=f"rows_pass_{step}",
    )(info, ids, own, mate, table, *kept, *earlier)


def join_kernel(own, other, own_log, other_log, out):
    for piece in range(own_log.shape[0]):
        here = slice(piece * PIECE, (piece + 1) * PIECE)
        log = jnp.logaddexp(own_log[piece], other_log[piece])
        left = columns(jnp.exp(own_log[piece] - log))[:, 0:1]
        right = columns(jnp.exp(other_log[piece] - log))[:, 0:1]
        out[here, :] = (
            own[here, :].astype(jnp.float32) * left + other[here, :].astype(jnp.float32) * right
        ).astype(jnp.bfloat16)


def join_pass(own, other, own_log, other_log):
    rows, width = own.shape
    flat = pl.BlockSpec((CHUNK, width), lambda i: (i, 0))
    cube = pl.BlockSpec((CHUNK // PIECE, 8, 128), lambda i: (i, 0, 0))
    return pl.pallas_call(
        join_kernel,
        grid=(rows // CHUNK,),
        in_specs=[flat, flat, cube, cube],
        out_specs=flat,
        out_shape=jax.ShapeDtypeStruct((rows, width), jnp.bfloat16),
        name="join_pass",
    )(own, other, own_log, other_log)


def home_kernel(count, logs, weight, targets, *refs):
    parts, out = refs[:count], refs[-1]
    log = logs[0]
    share = jnp.exp(log - jnp.max(log, axis=0, keepdims=True))
    share = columns(share / jnp.sum(share, axis=0, keepdims=True))
    mean = parts[0][...].astype(jnp.float32) * share[:, 0:1]
    for place in range(1, count):
        mean = mean + parts[place][...].astype(jnp.float32) * share[:, place : place + 1]
    out[...] = columns(weight[0])[:, 0:1] * (targets[0] - mean)


def home_pass(logs, weight, targets, parts, earlier):
    rows, width = parts[0].shape
    questions = targets.shape[0]
    flat = pl.BlockSpec((PIECE, width), lambda i: (i, 0))
    cube = pl.BlockSpec((1, 8, 128), lambda i: (i, 0, 0))
    return pl.pallas_call(
        functools.partial(home_kernel, len(parts)),
        grid=(rows // PIECE,),
        in_specs=[cube, cube, pl.BlockSpec((1, PIECE, width), lambda i: (i % questions, 0, 0))]
        + [flat] * len(parts)
        + [pl.BlockSpec(memory_space=pl.ANY)] * len(earlier),
        out_specs=flat,
        out_shape=jax.ShapeDtypeStruct((rows, width), jnp.float32),
        name="home_pass",
    )(logs, weight, targets, *parts, *earlier)


def table_kernel(first, info, facts, tops, rows, expos, *refs):
    outs, acc, scales = refs[-4:-2], refs[-2], refs[-1]
    tile = pl.program_id(0) + first
    sources, _, both, wide = expos.shape
    count = both // PIECE

    @pl.when(pl.program_id(0) == 0)
    def _():
        def ready(source, _):
            places, _ = piece_places(info, source, count)
            scales[source] = jnp.zeros(scales.shape[1:], jnp.float32)
            for piece in range(count):
                scales[source, pl.ds(places[piece], PIECE), :] = columns(facts[source * count + piece])
            raw = scales[source]
            lane = lax.broadcasted_iota(jnp.int32, raw.shape, 1)
            weight = raw[:, 0:1]
            spread = jnp.where(weight == 0.0, 0.0, -weight * jnp.exp(tops[source] - raw[:, 1:2]))
            spread = jnp.where(lane == 127, raw[:, 2:3], spread)
            scales[source] = jnp.where(lane == 126, raw[:, 3:4], spread)
            return 0

        lax.fori_loop(0, sources, ready, 0)

    acc[...] = jnp.zeros_like(acc)

    def add(source, begin, size):
        here = pl.ds(pl.multiple_of(begin, CHUNK), size)
        scale = scales[source, here, :]
        lane = lax.broadcasted_iota(jnp.int32, (size, 128), 1)
        column = lax.broadcasted_iota(jnp.int32, (size, wide), 1)
        spread = jnp.sum(jnp.where(lane == tile, scale, 0.0), axis=1, keepdims=True)
        target = scale[:, 126:127].astype(jnp.int32) - tile * wide
        grad = expos[source, 0, here, :].astype(jnp.float32) * spread
        grad = jnp.where(column == target, scale[:, 127:128], grad).astype(jnp.bfloat16)
        acc[...] += lax.dot_general(
            grad,
            rows[source, here, :],
            (((0,), (0,)), ((), ())),
            preferred_element_type=jnp.float32,
        )

    def add_source(source, _):
        live = info[1 + source * (count + 1) + count]
        chunks = (live + CHUNK - 1) // CHUNK

        def add_two(pair, _):
            add(source, pair * (2 * CHUNK), 2 * CHUNK)
            return 0

        lax.fori_loop(0, chunks // 2, add_two, 0)

        @pl.when(chunks % 2 == 1)
        def _():
            add(source, (chunks - 1) * CHUNK, CHUNK)

        return 0

    lax.fori_loop(0, sources, add_source, 0)
    half = wide // 2
    for side, out in enumerate(outs):
        for place in range(out.shape[0]):
            size = out.shape[3]
            out[place, 0] = acc[
                side * half : (side + 1) * half, place * size : (place + 1) * size
            ].astype(jnp.bfloat16)


def table_pass(info, facts, tops, rows, expos, first, tiles, n_pb, earlier):
    sources, _, both, wide = expos.shape
    _, room, width = rows.shape
    own = width // n_pb
    once = pl.Buffered(1)
    cube = lambda i, s: (0, 0, 0)
    return pl.pallas_call(
        functools.partial(table_kernel, first),
        grid_spec=pltpu.PrefetchScalarGridSpec(
            num_scalar_prefetch=1,
            grid=(tiles,),
            in_specs=[
                pl.BlockSpec(facts.shape, cube, pipeline_mode=once),
                pl.BlockSpec(tops.shape, cube, pipeline_mode=once),
                pl.BlockSpec(rows.shape, cube, pipeline_mode=once),
                pl.BlockSpec((sources, 1, both, wide), lambda i, s: (0, i + first, 0, 0)),
            ]
            + [pl.BlockSpec(memory_space=pl.ANY)] * len(earlier),
            out_specs=[pl.BlockSpec((n_pb, 1, wide // 2, own), lambda i, s: (0, i, 0, 0))] * 2,
            scratch_shapes=[
                pltpu.VMEM((wide, width), jnp.float32),
                pltpu.VMEM((sources, room, 128), jnp.float32),
            ],
        ),
        out_shape=[jax.ShapeDtypeStruct((n_pb, tiles, wide // 2, own), jnp.bfloat16)] * 2,
        compiler_params=pltpu.CompilerParams(vmem_limit_bytes=60 << 20),
        cost_estimate=pl.CostEstimate(
            flops=2 * sources * both * tiles * wide * width,
            bytes_accessed=4 * sources * both * tiles * wide,
            transcendentals=0,
        ),
        name=f"table_pass_{first}",
    )(info, facts, tops, rows, expos, *earlier)


def gather_kernel(*refs):
    mats, rows = refs[:3], refs[3:5]
    full, laid = refs[5:8], refs[8:10]
    send, recv, near = refs[10:]
    slots = full[0].shape[1]
    pb, place = lax.axis_index("pb"), lax.axis_index("slot")
    mate = pb // 2 * 2 + (pb + 1) % 2
    side_x = pb // 4 * 4 + (pb + 2) % 4
    side_y = (pb + 4) % 8
    corner = (side_x + 4) % 8
    barrier = pltpu.get_barrier_semaphore()
    partners = [(mate, place), (side_x, place), (side_y, place)]
    partners += [(pb, (place + step) % slots) for step in range(1, slots)]
    for partner in partners:
        pl.semaphore_signal(barrier, inc=1, device_id=partner, device_id_type=pl.DeviceIdType.MESH)
    pl.semaphore_wait(barrier, len(partners))

    sent, unread, stays, ready = [], {}, [], {}

    def push(source, target, device):
        copy = pltpu.make_async_remote_copy(
            src_ref=source,
            dst_ref=target,
            send_sem=send.at[len(sent)],
            recv_sem=recv.at[len(sent)],
            device_id=device,
            device_id_type=pl.DeviceIdType.MESH,
        )
        copy.start()
        unread[len(sent)] = copy
        sent.append(copy)
        return len(sent) - 1

    def read(number):
        unread.pop(number).wait_recv()

    def put(source, target):
        copy = pltpu.make_async_copy(source, target, near.at[len(stays)])
        copy.start()
        stays.append(copy)

    def move_rows(step):
        goal = (place + step) % slots
        for source, target in zip(rows, laid):
            block = source.at[:, goal]
            spot = target.at[:, :, place]
            if step:
                push(block, spot, (pb, goal))
            else:
                put(block, spot)

    def part(mat, at_pb, origin, half):
        size = full[mat].shape[2] // 2
        return full[mat].at[at_pb, origin, pl.ds(half * size, size)]

    def own_moves(step, mat, origin, source):
        size = full[mat].shape[2] // 2
        first, second = (source.at[pl.ds(half * size, size)] for half in range(2))
        first_at, second_at = (part(mat, pb, origin, half) for half in range(2))
        ready[step, mat] = [
            push(first, first_at, (side_x, place)),
            push(second, second_at, (side_y, place)),
            push(first, first_at, (side_y, place)),
            push(second, second_at, (side_x, place)),
        ]
        push(source, full[mat].at[pb, origin], (mate, place))

    def onward(step, mat, origin):
        over_x, over_y, _, _ = ready[step, mat]
        read(over_x)
        block = part(mat, side_x, origin, 0)
        ready[step, mat].append(push(block, block, (side_y, place)))
        push(block, block, (mate, place))
        read(over_y)
        block = part(mat, side_y, origin, 1)
        ready[step, mat].append(push(block, block, (side_x, place)))
        push(block, block, (mate, place))

    def finish(step, mat, origin):
        _, _, over_y, over_x, first, second = ready[step, mat]
        for number, at_pb, half in (
            (over_y, side_y, 0),
            (over_x, side_x, 1),
            (first, corner, 0),
            (second, corner, 1),
        ):
            read(number)
            block = part(mat, at_pb, origin, half)
            push(block, block, (mate, place))

    count = len(mats)
    following = (pb, (place + 1) % slots)
    ring = [push(mats[mat], full[mat].at[pb, place], following) for mat in range(count)]
    for mat in range(count):
        own_moves(0, mat, place, mats[mat])
        put(mats[mat], full[mat].at[pb, place])
    move_rows(1)
    move_rows(0)
    for step in range(1, slots + 1):
        origin = (place + slots - step) % slots
        before = (place + slots - step + 1) % slots
        if step < slots:
            for mat in range(count):
                read(ring[mat])
                block = full[mat].at[pb, origin]
                if step < slots - 1:
                    ring[mat] = push(block, block, following)
                own_moves(step, mat, origin, block)
        if step == 1:
            move_rows(slots - 1)
        if step == 2:
            for other in range(2, slots - 1):
                move_rows(other)
        for mat in range(count):
            onward(step - 1, mat, before)
        for mat in range(count):
            finish(step - 1, mat, before)
    for number in sorted(unread):
        read(number)
    for copy in sent:
        copy.wait_send()
    for copy in stays:
        copy.wait()


def gather_inputs(x_in, memory, attn_w, ffn_in, ffn_out):
    n_pb, slots = lax.axis_size("pb"), lax.axis_size("slot")
    mats, rows = (attn_w, ffn_in, ffn_out), (x_in, memory)
    width = attn_w.shape[1]
    rows = [row.reshape((-1, slots) + row.shape[1:]) for row in rows]
    if (n_pb, slots) != (8, 4):
        return (
            to_slots(x_in),
            to_slots(memory),
            *(gather_all(mat).reshape(-1, width) for mat in mats),
        )
    shapes = [jax.ShapeDtypeStruct((n_pb, slots) + mat.shape, mat.dtype) for mat in mats]
    for row in rows:
        own, _, questions, steps, _ = row.shape
        shapes.append(jax.ShapeDtypeStruct((own, questions, slots, steps, width), row.dtype))
    copies = 13 * len(mats) * slots + (slots - 1) * (len(mats) + len(rows))
    anywhere = pl.BlockSpec(memory_space=pl.ANY)
    *full, x_here, mem_here = pl.pallas_call(
        gather_kernel,
        in_specs=[anywhere] * 5,
        out_specs=[anywhere] * 5,
        out_shape=shapes,
        scratch_shapes=[
            pltpu.SemaphoreType.DMA((copies,)),
            pltpu.SemaphoreType.DMA((copies,)),
            pltpu.SemaphoreType.DMA((len(mats) + len(rows),)),
        ],
        compiler_params=pltpu.CompilerParams(collective_id=0, has_side_effects=True),
        name="gather_inputs",
    )(*mats, *rows)
    own, questions, _, _, _ = x_here.shape
    return (
        x_here.reshape(own, questions, -1, width),
        mem_here.reshape(own, questions, -1, width),
        *(mat.reshape(-1, width) for mat in full),
    )


UNIT = 64


def scatter_kernel(*refs):
    mats, rows, few = refs[:3], refs[3], refs[4]
    outs, laid, few_out = refs[5:8], refs[8], refs[9]
    (from_core, kept, wide_x, wide_y, narrow_x, narrow_y, from_slot, few_here, few_there, few_slot) = refs[10:20]
    send, recv, near = refs[20:]
    depth = kept.shape[0]
    slots = mats[0].shape[2]
    pb, place = lax.axis_index("pb"), lax.axis_index("slot")
    core, at_x, at_y = pb % 2, pb // 2 % 2, pb // 4
    mate = (pb // 2 * 2 + (pb + 1) % 2, place)
    side_x = (pb // 4 * 4 + (pb + 2) % 4, place)
    side_y = ((pb + 4) % 8, place)
    barrier = pltpu.get_barrier_semaphore()
    partners = [mate, side_x, side_y]
    partners += [(pb, (place + step) % slots) for step in range(1, slots)]
    for partner in partners:
        pl.semaphore_signal(barrier, inc=1, device_id=partner, device_id_type=pl.DeviceIdType.MESH)
    pl.semaphore_wait(barrier, len(partners))

    sent = []

    def push(source, target, device):
        copy = pltpu.make_async_remote_copy(
            src_ref=source,
            dst_ref=target,
            send_sem=send.at[len(sent)],
            recv_sem=recv.at[len(sent)],
            device_id=device,
            device_id_type=pl.DeviceIdType.MESH,
        )
        copy.start()
        sent.append(copy)
        return copy

    stays = []

    def put(source, target):
        copy = pltpu.make_async_copy(source, target, near.at[len(stays)])
        copy.start()
        stays.append(copy)
        return copy

    units = [
        (mat, unit)
        for mat in (1, 2, 0)
        for unit in range(mats[mat].shape[3] // UNIT)
    ]

    def block(number, which):
        mat, unit = units[number]
        return mats[mat].at[:, which, :, pl.ds(unit * UNIT, UNIT)]

    half = UNIT // 2
    first, second = pl.ds(0, half), pl.ds(half, half)
    by_core = [push(block(n, 1 - core), from_core.at[n], mate) for n in range(len(units))]
    loads = {n: put(block(n, core), kept.at[n % depth]) for n in range(min(depth, len(units)))}
    by_rows = []
    for step in range(1, slots):
        goal = (place + step) % slots
        by_rows.append(push(rows.at[:, :, goal], laid.at[:, place], (pb, goal)))
    at_home = put(rows.at[:, :, place], laid.at[:, place])
    by_few = push(few, few_there.at[0], mate)

    def total(left, right):
        return (left.astype(jnp.float32) + right.astype(jnp.float32)).astype(jnp.bfloat16)

    over, across, along = {}, {}, {}

    def from_cores(n):
        slot = n % depth
        by_core[n].wait_recv()
        loads[n].wait()

        def step(i, _):
            y, x, z = i // (2 * slots), i // slots % 2, i % slots
            kept[slot, 2 * y + x, z] = total(kept[slot, 2 * y + x, z], from_core[n, 2 * y + x, z])
            return 0

        lax.fori_loop(0, 4 * slots, step, 0)
        over[n] = [
            push(kept.at[slot, 1 - at_x, :, first], wide_x.at[n, 0], side_x),
            push(kept.at[slot, 2 + 1 - at_x, :, first], wide_x.at[n, 1], side_x),
            push(kept.at[slot, pl.ds(2 * (1 - at_y), 2), :, second], wide_y.at[n], side_y),
        ]

    def over_first(n):
        slot = n % depth
        for copy in over[n]:
            copy.wait_recv()

        def step(i, _):
            side, z = i // slots, i % slots
            spot = 2 * side + at_x
            kept[slot, spot, z, 0:half] = total(kept[slot, spot, z, 0:half], wide_x[n, side, z])
            spot = 2 * at_y + side
            kept[slot, spot, z, half:UNIT] = total(kept[slot, spot, z, half:UNIT], wide_y[n, side, z])
            return 0

        lax.fori_loop(0, 2 * slots, step, 0)
        across[n] = [
            push(kept.at[slot, 2 * (1 - at_y) + at_x, :, first], narrow_y.at[n], side_y),
            push(kept.at[slot, 2 * at_y + 1 - at_x, :, second], narrow_x.at[n], side_x),
        ]

    def over_second(n):
        slot = n % depth
        for copy in across[n]:
            copy.wait_recv()
        spot = 2 * at_y + at_x

        def step(z, _):
            kept[slot, spot, z, 0:half] = total(kept[slot, spot, z, 0:half], narrow_y[n, z])
            kept[slot, spot, z, half:UNIT] = total(kept[slot, spot, z, half:UNIT], narrow_x[n, z])
            return 0

        lax.fori_loop(0, slots, step, 0)
        along[n] = []
        for step_on in range(1, slots):
            goal = (place + step_on) % slots
            along[n].append(push(kept.at[slot, spot, goal], from_slot.at[n, step_on - 1], (pb, goal)))

    def over_slots(n):
        slot = n % depth
        mat, unit = units[n]
        for copy in along[n]:
            copy.wait_recv()
        here = kept[slot, 2 * at_y + at_x, place].astype(jnp.float32)
        for step_on in range(1, slots):
            here = here + from_slot[n, step_on - 1].astype(jnp.float32)
        outs[mat][unit * UNIT : (unit + 1) * UNIT, :] = here
        if n + depth < len(units):
            for copy in over[n] + across[n] + along[n]:
                copy.wait_send()
            loads[n + depth] = put(block(n + depth, core), kept.at[slot])

    stages = (from_cores, over_first, over_second, over_slots)
    for turn in range(len(units) + len(stages) - 1):
        for lag, stage in enumerate(stages):
            if 0 <= turn - lag < len(units):
                stage(turn - lag)
        if turn == 0:
            by_few.wait_recv()
            few_here[0] = few[...] + few_there[0]
            by_few = push(few_here.at[0], few_there.at[1], side_x)
        if turn == 1:
            by_few.wait_recv()
            few_here[1] = few_here[0] + few_there[1]
            by_few = push(few_here.at[1], few_there.at[2], side_y)
        if turn == 2:
            by_few.wait_recv()
            few_here[2] = few_here[1] + few_there[2]
            few_slot[place] = few_here[2]
            by_few = [
                push(few_here.at[2], few_slot.at[place], (pb, (place + step) % slots))
                for step in range(1, slots)
            ]
    for copy in by_few:
        copy.wait_recv()
    every = few_slot[0]
    for step in range(1, slots):
        every = every + few_slot[step]
    few_out[...] = every
    for copy in by_rows:
        copy.wait_recv()
    at_home.wait()
    freed = set()
    for n in range(len(units) - depth):
        freed.update(id(copy) for copy in over[n] + across[n] + along[n])
    for copy in sent:
        if id(copy) not in freed:
            copy.wait_send()


def scatter_outputs(grad_attn, grad_in_w, grad_out_w, grad_inputs, small):
    n_pb, slots = lax.axis_size("pb"), lax.axis_size("slot")
    if (n_pb, slots) != (8, 4):
        return (
            scatter_all(grad_attn),
            scatter_all(grad_in_w),
            scatter_all(grad_out_w),
            to_positions(leave_slots(grad_inputs)),
            sum_all(small, ("core", "x", "y", "slot")),
        )
    width = grad_attn.shape[1]
    mats = [
        mat.reshape(n_pb // 2, 2, slots, -1, width)
        for mat in (grad_attn, grad_in_w, grad_out_w)
    ]
    own, questions, steps, _ = grad_inputs.shape
    rows = grad_inputs.reshape(own, questions, slots, steps // slots, width)
    laid = jax.ShapeDtypeStruct((own, slots, questions, steps // slots, width), rows.dtype)
    units = sum(mat.shape[3] for mat in mats) // UNIT
    depth = 5
    copies = units * (1 + 3 + 2 + slots - 1) + (slots - 1) + 3 + slots - 1
    anywhere, inside = pl.BlockSpec(memory_space=pl.ANY), pl.BlockSpec(memory_space=pltpu.VMEM)
    half = UNIT // 2
    low, high = jnp.bfloat16, jnp.float32
    *shards, laid, small = pl.pallas_call(
        scatter_kernel,
        in_specs=[anywhere] * 4 + [inside],
        out_specs=[inside] * 3 + [anywhere, inside],
        out_shape=[jax.ShapeDtypeStruct(mat.shape[3:], high) for mat in mats]
        + [laid, jax.ShapeDtypeStruct(small.shape, high)],
        scratch_shapes=[
            pltpu.VMEM((units, 4, slots, UNIT, width), low),
            pltpu.VMEM((depth, 4, slots, UNIT, width), low),
            pltpu.VMEM((units, 2, slots, half, width), low),
            pltpu.VMEM((units, 2, slots, half, width), low),
            pltpu.VMEM((units, slots, half, width), low),
            pltpu.VMEM((units, slots, half, width), low),
            pltpu.VMEM((units, slots - 1, UNIT, width), low),
            pltpu.VMEM((3,) + small.shape, high),
            pltpu.VMEM((3,) + small.shape, high),
            pltpu.VMEM((slots,) + small.shape, high),
            pltpu.SemaphoreType.DMA((copies,)),
            pltpu.SemaphoreType.DMA((copies,)),
            pltpu.SemaphoreType.DMA((units + 1,)),
        ],
        compiler_params=pltpu.CompilerParams(
            collective_id=1, has_side_effects=True, vmem_limit_bytes=60 << 20
        ),
        name="scatter_outputs",
    )(*mats, rows, small)
    return (*shards, laid.reshape((-1,) + laid.shape[2:]), small)


def body(
    x_in,
    memory,
    doc_scores,
    valid_count,
    target_ids,
    target_len,
    mem_len,
    attn_w,
    ffn_in,
    ffn_out,
    ffn_bias,
    norms,
    embedding,
):
    x_here, mem_here, attn_full, in_full, out_full = gather_inputs(
        x_in, memory, attn_w, ffn_in, ffn_out
    )
    slots_here, questions, tgt_steps, model_width = x_here.shape
    mem_steps = mem_here.shape[2]
    seq_count = slots_here * questions
    head_dim = model_width // HEADS
    scaling = head_dim ** (-0.5)
    blocks = [
        attn_full[block_index * model_width : (block_index + 1) * model_width]
        for block_index in range(8)
    ]

    inputs = x_here.reshape(seq_count * tgt_steps, model_width)
    memory_rows = mem_here.reshape(seq_count * mem_steps, model_width)
    positions = jnp.arange(tgt_steps)
    place, slot_count = place_of("slot")
    core, cores = place_of("core")
    ring = (place - jnp.arange(slot_count)) % slot_count
    lengths_here = [mem_len] + [shifted(mem_len, "slot", step) for step in range(1, slot_count)]
    lengths_here = jnp.stack(lengths_here)[ring].reshape(slots_here, slot_count, questions)
    mem_lengths = pick(lengths_here, place, 1).reshape(seq_count)
    tgt_lengths = jnp.full_like(mem_lengths, tgt_steps)
    queries = (product(inputs, blocks[0]) * scaling).astype(jnp.bfloat16)
    key_rows = product(inputs, blocks[1]).astype(jnp.bfloat16)
    value_rows = product(inputs, blocks[2]).astype(jnp.bfloat16)
    self_out, self_lse = attend(True, tgt_lengths, queries, key_rows, value_rows)
    hidden_one, normed_one, root_one = norm_forward(
        inputs.astype(jnp.float32) + product(self_out, blocks[3]), norms[0], norms[1]
    )
    one_low = hidden_one.astype(jnp.bfloat16)
    cross_queries = (product(one_low, blocks[4]) * scaling).astype(jnp.bfloat16)
    cross_keys = product(memory_rows, blocks[5]).astype(jnp.bfloat16)
    cross_values = product(memory_rows, blocks[6]).astype(jnp.bfloat16)
    cross_out, cross_lse = attend(False, mem_lengths, cross_queries, cross_keys, cross_values)
    hidden_two, normed_two, root_two = norm_forward(
        hidden_one + product(cross_out, blocks[7]), norms[2], norms[3]
    )
    two_low = hidden_two.astype(jnp.bfloat16)
    pre_act = contract_cols(two_low, in_full) + ffn_bias
    act, slope = gelu_parts(pre_act)
    act_low, slope = act.astype(jnp.bfloat16), slope.astype(jnp.bfloat16)
    hidden_three, normed_three, root_three = norm_forward(
        hidden_two + product(act_low, out_full), norms[4], norms[5]
    )
    three_low = hidden_three.astype(jnp.bfloat16).reshape(
        slots_here, questions, tgt_steps, model_width
    )
    vocab_here = embedding.shape[0]
    share = vocab_here // cores
    pieces = slots_here * questions

    def both_cores(value):
        return jnp.stack([value, shifted(value, "core", 1)]) if cores > 1 else value[None]

    tokens = jnp.concatenate([target_ids, valid_count[:, None], target_len[:, None]], axis=1)
    tokens = both_cores(tokens)
    ids_all, valid_all, len_all = tokens[:, :, :tgt_steps], tokens[:, :, -2], tokens[:, :, -1]

    local = target_ids - place * vocab_here
    held = jnp.logical_and(local >= 0, local < vocab_here)
    target_rows = jnp.take(embedding, jnp.clip(local, 0, vocab_here - 1), axis=0)
    target_rows = jnp.where(held[..., None], target_rows, jnp.zeros_like(target_rows))
    target_rows = after(target_rows, x_here)
    found = [shifted(target_rows, "slot", step) for step in range(1, slot_count)]
    target_rows = sum([f.astype(jnp.float32) for f in found], target_rows.astype(jnp.float32))

    slot_ids = jnp.arange(slot_count)[:, None] + slot_count * jnp.arange(slots_here)[None]
    live_piece = slot_ids[:, None, :, None] < valid_all[None, :, None, :]
    long_piece = (len_all + 15) // 16 * 16
    long_piece = jnp.where(live_piece, long_piece[None, :, None, :], 0).reshape(slot_count, -1)
    ends = jnp.cumsum(long_piece, axis=1)
    packing = jnp.concatenate([ends - long_piece, ends[:, -1:]], axis=1)[ring]
    info = jnp.concatenate([core[None], packing.reshape(-1)]).astype(jnp.int32)
    piece_ids = (ids_all - (place * vocab_here + core * share)).astype(jnp.float32)
    piece_ids = jnp.broadcast_to(
        piece_ids[None, :, None], (slot_count, cores, slots_here, questions, tgt_steps)
    ).reshape(-1, 1, tgt_steps)
    ids_rows = jnp.broadcast_to(piece_ids, (piece_ids.shape[0], 8, tgt_steps))

    group = pieces * tgt_steps
    moving = three_low.reshape(group, model_width)
    arriving = [moving] + [shifted(moving, "slot", step) for step in range(1, slot_count)]
    kept, log_list, homes = (), [], []
    for step in range(slot_count):
        moving = arriving[step] if not step else after(arriving[step], own_logs)
        other = shifted(moving, "core", 1)
        earlier = (own_logs,) if step else ()
        *kept, own_sums, mate_sums, own_logs, mate_logs = rows_pass(
            step, slot_count, info, ids_rows, moving, other, embedding, cores, kept, earlier
        )
        log_list += [own_logs[:, 0], mate_logs[:, 0]]
        homes.append(
            join_pass(
                own_sums, shifted(mate_sums, "core", 1), own_logs, shifted(mate_logs, "core", 1)
            )
        )

    def by_slot(value):
        parts = [value] + [shifted(value, "slot", step) for step in range(1, slot_count)]
        return jnp.stack(parts)[ring]

    target_logit = jnp.sum(three_low.astype(jnp.float32) * target_rows[None], axis=-1)
    told = jnp.concatenate(log_list + [target_logit.reshape(-1, tgt_steps)], axis=0)
    told = both_cores(by_slot(told))
    hit_all = told[:, :, -pieces:].reshape(cores, slot_count, slots_here, questions, tgt_steps)
    hit_all = hit_all.transpose(2, 1, 0, 3, 4).reshape(-1, cores, questions, tgt_steps)
    logs = told[:, :, :-pieces].reshape(
        cores, slot_count, slot_count, cores, slots_here, questions, tgt_steps
    )
    logs = jnp.stack([logs[0], logs[1][:, :, ::-1]]) if cores > 1 else logs
    logs = jax.nn.logsumexp(logs, axis=0)
    turns = (jnp.arange(slot_count)[:, None] - jnp.arange(slot_count)[None]) % slot_count
    logs = jnp.take_along_axis(
        logs, turns.reshape((slot_count, slot_count) + (1,) * (logs.ndim - 2)), axis=1
    )
    rest_all = jax.nn.logsumexp(logs, axis=0)
    rest_all = rest_all.transpose(2, 0, 1, 3, 4).reshape(hit_all.shape)
    log_norm = jnp.logaddexp(rest_all, hit_all)
    live = positions < len_all[..., None]
    lengths = len_all.astype(jnp.float32)
    per_slot = jnp.sum(jnp.where(live[None], hit_all - log_norm, 0.0), axis=3) / lengths[None]
    valid = jnp.arange(per_slot.shape[0])[:, None, None] < valid_all[None]
    scores_t = both_cores(doc_scores).transpose(2, 0, 1)
    joint = jnp.where(valid, scores_t + per_slot, mask_fill)
    prior = jnp.where(valid, scores_t, mask_fill)
    joint_total = jax.nn.logsumexp(joint, axis=0)
    neg_marginal = jax.nn.logsumexp(prior, axis=0) - joint_total
    log_post = joint - joint_total
    posterior = jnp.exp(log_post)
    entropy_q = -jnp.sum(posterior * log_post, axis=0)
    objective_part = jnp.sum((lengths * (neg_marginal + entropy_weight * entropy_q))[0])
    slot_weight = -posterior * (1.0 + entropy_weight * (log_post + entropy_q[None]))
    token_weight = jnp.where(live[None], slot_weight[..., None], 0.0)
    hit_weight = token_weight * jax.nn.sigmoid(rest_all - hit_all)

    def own_slots(value):
        value = value[:, 0].reshape(slots_here, slot_count, questions, tgt_steps)
        return pick(value, place, 1)

    def ring_rows(value):
        value = value.reshape(slots_here, slot_count, cores, questions, tgt_steps)
        return value.transpose(1, 2, 0, 3, 4)[ring].reshape(-1, tgt_steps)

    facts = [ring_rows(value) for value in (token_weight, log_norm, hit_weight)]
    facts = jnp.stack(facts + [ids_rows[:, 0]] + [jnp.zeros_like(facts[0])] * 4, axis=1)
    expos, packed, tops = kept
    tiles = expos.shape[1]
    cut = tiles // 2 + 1
    n_pb = lax.axis_size("pb")
    tall, wide, _ = grid_of(n_pb)
    sends = tuple(homes[1:])
    homes[1:] = [
        shifted(homes[step], "slot", slot_count - step) for step in range(1, slot_count)
    ]
    table_grads = []
    for first, count in ((0, cut), (cut, tiles - cut)):
        sides = [
            side.reshape((tall, wide, cores) + side.shape[1:])
            for side in table_pass(
                info, facts, tops, packed, expos, first, count, n_pb, sends
            )
        ]
        sends = (ring_first(sides[0], "x", 1), ring_first(sides[1], "y", 0))
        table_grads.append(sides)

    def over_first(sides, late):
        return (
            ring_scatter(sides[0], "x", 1, late).astype(jnp.bfloat16),
            ring_scatter(sides[1], "y", 0, late).astype(jnp.bfloat16),
        )

    def over_second(sides, late):
        return (
            ring_scatter(sides[0], "y", 0, late).astype(jnp.bfloat16),
            ring_scatter(sides[1], "x", 0, late).astype(jnp.bfloat16),
        )

    def second_sends(sides):
        return ring_first(sides[0], "y", 0), ring_first(sides[1], "x", 0)

    home_logs = pick(logs, place, 1)[:, 0][(place + jnp.arange(slot_count)) % slot_count]
    home_logs = home_logs.reshape(slot_count, pieces, tgt_steps).transpose(1, 0, 2)
    home_logs = jnp.pad(
        home_logs, ((0, 0), (0, 8 - slot_count), (0, 0)), constant_values=mask_fill
    )
    own_weight = own_slots(hit_weight).reshape(pieces, 1, tgt_steps)
    own_weight = jnp.broadcast_to(own_weight, (pieces, 8, tgt_steps))
    grad_three = home_pass(home_logs, own_weight, target_rows, homes, sends)
    back_blocks, in_back, out_back = blocks, in_full, out_full
    grad_res_three, gain_three, shift_three = norm_backward(
        grad_three, normed_three, root_three, norms[4]
    )
    grad_ffn = grad_res_three.astype(jnp.bfloat16)
    grad_out_w = contract_rows(act_low, grad_ffn)
    grad_act = contract_cols(grad_ffn, out_back)
    grad_pre = (grad_act * slope.astype(jnp.float32)).astype(jnp.bfloat16)
    grad_in_w = contract_rows(grad_pre, two_low)
    grad_bias = jnp.sum(lax.optimization_barrier(grad_pre).astype(jnp.float32), axis=0)
    grad_two = grad_res_three + product(grad_pre, in_back)
    grad_res_two, gain_two, shift_two = norm_backward(grad_two, normed_two, root_two, norms[2])
    grad_cross = grad_res_two.astype(jnp.bfloat16)
    grad_w7 = contract_rows(cross_out, grad_cross)
    grad_cross_out = contract_cols(grad_cross, back_blocks[7]).astype(jnp.bfloat16)
    cq_grad, ck_grad, cv_grad = attend(
        False, mem_lengths, cross_queries, cross_keys, cross_values, cross_lse, grad_cross_out
    )
    grad_w4 = contract_rows(one_low, cq_grad) * scaling
    grad_w5 = contract_rows(memory_rows, ck_grad)
    grad_w6 = contract_rows(memory_rows, cv_grad)
    grad_memory = (
        contract_cols(ck_grad, back_blocks[5]) + contract_cols(cv_grad, back_blocks[6])
    ).astype(jnp.bfloat16)
    grad_memory = leave_slots(
        grad_memory.reshape(slots_here, questions, mem_steps, model_width)
    )
    table_sum = [over_first(sides, cq_grad) for sides in table_grads]
    earlier = grad_memory[1:] + [*second_sends(table_sum[0]), *second_sends(table_sum[1])]
    grad_one = grad_res_two + contract_cols(cq_grad, back_blocks[4]) * scaling
    grad_res_one, gain_one, shift_one = norm_backward(grad_one, normed_one, root_one, norms[0])
    grad_attn_out = grad_res_one.astype(jnp.bfloat16)
    grad_w3 = contract_rows(self_out, grad_attn_out)
    grad_self_out = contract_cols(grad_attn_out, back_blocks[3]).astype(jnp.bfloat16)
    sq_grad, sk_grad, sv_grad = attend(
        True, tgt_lengths, queries, key_rows, value_rows, self_lse, grad_self_out, earlier
    )
    grad_w0 = contract_rows(inputs, sq_grad) * scaling
    grad_w1 = contract_rows(inputs, sk_grad)
    grad_w2 = contract_rows(inputs, sv_grad)
    grad_inputs = (
        grad_res_one
        + contract_cols(sq_grad, back_blocks[0]) * scaling
        + contract_cols(sk_grad, back_blocks[1])
        + contract_cols(sv_grad, back_blocks[2])
    )
    grad_inputs = grad_inputs.astype(jnp.bfloat16).reshape(
        slots_here, questions, tgt_steps, model_width
    )
    grad_attn = jnp.concatenate(
        [
            grad.astype(jnp.bfloat16)
            for grad in (grad_w0, grad_w1, grad_w2, grad_w3, grad_w4, grad_w5, grad_w6, grad_w7)
        ],
        axis=0,
    )
    small = jnp.concatenate(
        [
            jnp.stack([gain_one, shift_one, gain_two, shift_two, gain_three, shift_three], axis=0),
            grad_bias.reshape(-1, model_width),
            jnp.zeros((6, model_width), jnp.float32)
            .at[0, :3]
            .set(jnp.stack([objective_part, jnp.sum(lengths[0]), jnp.sum(entropy_q[0])])),
        ],
        axis=0,
    )
    table_sum = [over_second(sides, grad_inputs) for sides in table_sum]
    table_sum = [jnp.stack(sides, axis=2) for sides in table_sum]
    table_sum = jnp.concatenate(table_sum, axis=1).reshape(cores, share, -1)
    table_send = pick(table_sum, 1 - core, 0)
    grad_attn, grad_in_w, grad_out_w, grad_inputs, small = scatter_outputs(
        grad_attn,
        grad_in_w.astype(jnp.bfloat16),
        grad_out_w.astype(jnp.bfloat16),
        grad_inputs,
        after(small, table_send),
    )
    grad_memory = to_positions(grad_memory, small)
    kept = pick(table_sum, core, 0)
    given = after(shifted(table_send, "core", 1), small)
    grad_embed = jnp.stack([kept, given])
    grad_embed = jnp.where(core == 0, grad_embed, grad_embed[::-1])
    grad_embed = grad_embed.reshape(vocab_here, -1).astype(jnp.float32)
    grad_norms = small[:6]
    scalars = small[-6]
    loss = scalars[0] / scalars[1]
    entropy = scalars[2] / (questions * n_pb * slot_count)
    grad_bias = small[6:-6].reshape(-1)
    own_bias = grad_bias.shape[0] // (lax.axis_size("pb") * slot_count)
    grad_bias = lax.dynamic_slice_in_dim(
        grad_bias,
        (lax.axis_index("pb") * slot_count + lax.axis_index("slot")) * own_bias,
        own_bias,
    )
    return (
        loss,
        entropy,
        grad_inputs,
        grad_memory,
        grad_attn,
        grad_in_w,
        grad_out_w,
        grad_bias,
        grad_norms,
        grad_embed,
    )


def solution(mesh):
    placed = (
        P(None, "pb", "slot", None),
        P(None, "pb", "slot", None),
        P("pb", None),
        P("pb"),
        P("pb", None),
        P("pb"),
        P("slot", "pb"),
        P(("pb", "slot"), None),
        P(("pb", "slot"), None),
        P(("pb", "slot"), None),
        P(),
        P(),
        P("slot", None),
    )
    return jax.shard_map(
        body,
        mesh=mesh,
        in_specs=placed,
        out_specs=(
            P(),
            P(),
            P(None, "pb", "slot", None),
            P(None, "pb", "slot", None),
            P(("pb", "slot"), None),
            P(("pb", "slot"), None),
            P(("pb", "slot"), None),
            P(("pb", "slot")),
            P(),
            P("slot", "pb"),
        ),
        check_vma=False,
    )
```

```python
import functools

import jax
import jax.numpy as jnp
from jax import lax
from jax.experimental import pallas as pl
from jax.experimental.pallas import tpu as pltpu
from jax.sharding import PartitionSpec as P

HEADS = 16


eps_norm = 1e-05
entropy_weight = 0.25
mask_fill = -1e30
root_half = 0.7071067811865476
inv_root_tau = 0.3989422804014327


def grid_of(n_pb):
    cores = 2 if n_pb % 2 == 0 else 1
    chips = n_pb // cores
    wide = max(d for d in range(1, chips + 1) if chips % d == 0 and d * d <= chips)
    return chips // wide, wide, cores


def shifted(value, axis, step):
    if axis == "slot":
        size = lax.axis_size("slot")
        return lax.ppermute(value, "slot", [(i, (i + step) % size) for i in range(size)])
    n_pb = lax.axis_size("pb")
    tall, wide, cores = grid_of(n_pb)
    pairs = []
    for i in range(n_pb):
        y, x, c = i // (wide * cores), i // cores % wide, i % cores
        if axis == "y":
            y = (y + step) % tall
        elif axis == "x":
            x = (x + step) % wide
        else:
            c = (c + step) % cores
        pairs.append((i, (y * wide + x) * cores + c))
    return lax.ppermute(value, "pb", pairs)


def place_of(axis):
    if axis == "slot":
        return lax.axis_index("slot"), lax.axis_size("slot")
    tall, wide, cores = grid_of(lax.axis_size("pb"))
    i = lax.axis_index("pb")
    if axis == "y":
        return i // (wide * cores), tall
    if axis == "x":
        return i // cores % wide, wide
    return i % cores, cores


def after(value, *tokens):
    for token in tokens:
        first = token[(0,) * token.ndim].astype(jnp.float32)
        value = jnp.where(first == first, value, jnp.zeros_like(value))
    return value


def pick(value, index, dim):
    return lax.dynamic_index_in_dim(value, index, dim, keepdims=False)


def ring_gather(value, axis):
    me, size = place_of(axis)
    found = [(me, value)]
    for step in range(1, size):
        value = shifted(value, axis, 1)
        found.append(((me - step) % size, value))
    return found


def ring_scatter(value, axis, dim, late=None):
    me, size = place_of(axis)
    total = pick(value, (me - 1) % size, dim).astype(jnp.bfloat16)
    for step in range(1, size):
        part = pick(value, (me - 1 - step) % size, dim)
        total = shifted(total, axis, 1)
        if late is not None:
            total = after(total, late)
        total = total.astype(jnp.float32) + part.astype(jnp.float32)
        if step < size - 1:
            total = total.astype(jnp.bfloat16)
    return total


def ring_first(value, axis, dim):
    me, size = place_of(axis)
    return pick(value, (me - 1) % size, dim).astype(jnp.bfloat16)


def gather_all(shard):
    tall, wide, cores = grid_of(lax.axis_size("pb"))
    rows, width = shard.shape
    slots = lax.axis_size("slot")
    column = jnp.zeros((slots, rows, width), shard.dtype)
    for index, block in ring_gather(shard, "slot"):
        column = lax.dynamic_update_index_in_dim(column, block, index, 0)
    column = column.reshape(slots * rows, width)
    half = slots * rows // 2
    core, _ = place_of("core")
    whole = jnp.zeros((tall * wide, cores, 2, half, width), shard.dtype)
    for side, (first, second) in enumerate((("x", "y"), ("y", "x"))):
        part = column[side * half : (side + 1) * half]
        for at_first, block in ring_gather(part, first):
            for at_second, block in ring_gather(block, second):
                x, y = (at_first, at_second) if first == "x" else (at_second, at_first)
                for at_core, block in ring_gather(block, "core"):
                    whole = lax.dynamic_update_slice(
                        whole, block[None, None, None], (y * wide + x, at_core, side, 0, 0)
                    )
    return whole.reshape(tall * wide * cores, slots * rows, width)


def scatter_pb(value, lates=(None, None, None)):
    tall, wide, cores = grid_of(lax.axis_size("pb"))
    rest = value.shape[1:]
    value = value.reshape((tall * wide, cores) + rest)
    value = ring_scatter(value, "core", 1, lates[0]).astype(jnp.bfloat16)
    value = value.reshape((tall, wide) + rest)
    half = rest[0] // 2
    first = ring_scatter(value[:, :, :half], "x", 1, lates[1])
    second = ring_scatter(value[:, :, half:], "y", 0, lates[1])
    first = ring_scatter(first.astype(jnp.bfloat16), "y", 0, lates[2])
    second = ring_scatter(second.astype(jnp.bfloat16), "x", 0, lates[2])
    return jnp.concatenate([first, second], axis=0)


def scatter_all(value):
    n_pb, slots = lax.axis_size("pb"), lax.axis_size("slot")
    rows = value.shape[0] // (n_pb * slots)
    value = value.reshape((n_pb, slots, rows) + value.shape[1:])
    column = scatter_pb(value)
    return ring_scatter(column.astype(jnp.bfloat16), "slot", 0)


def scatter_slot(value, late):
    me, size = place_of("slot")
    parts = [
        after(shifted(pick(value, (me + step) % size, 0), "slot", step), late)
        for step in range(1, size)
    ]
    return sum([part.astype(jnp.float32) for part in parts], pick(value, me, 0).astype(jnp.float32))


def sum_all(value, axes):
    for axis in axes:
        me, size = place_of(axis)
        parts = [value] + [shifted(value, axis, step) for step in range(1, size)]
        placed = jnp.stack(parts)
        value = jnp.sum(placed[(me - jnp.arange(size)) % size], axis=0)
    return value


def to_slots(value):
    me, size = place_of("slot")
    every, questions, steps, width = value.shape
    chunks = value.reshape(every // size, size, questions, steps, width)
    result = jnp.zeros((every // size, questions, size, steps, width), value.dtype)
    for step in range(size):
        block = pick(chunks, (me + step) % size, 1)
        if step:
            block = shifted(block, "slot", step)
        result = lax.dynamic_update_index_in_dim(result, block, (me - step) % size, 2)
    return result.reshape(every // size, questions, size * steps, width)


def leave_slots(value):
    me, size = place_of("slot")
    own, questions, steps, width = value.shape
    chunks = value.reshape(own, questions, size, steps // size, width)
    return [pick(chunks, (me + step) % size, 2) for step in range(size)]


def to_positions(blocks, late=None):
    me, size = place_of("slot")
    own, questions, steps, width = blocks[0].shape
    result = jnp.zeros((own, size, questions, steps, width), blocks[0].dtype)
    for step, block in enumerate(blocks):
        if step:
            block = shifted(block, "slot", step)
            block = block if late is None else after(block, late)
        result = lax.dynamic_update_index_in_dim(result, block, (me - step) % size, 1)
    return result.reshape(size * own, questions, steps, width)


def product(left, right):
    return jnp.dot(left, right, preferred_element_type=jnp.float32)


def contract_rows(left, right):
    return lax.dot_general(
        left, right, (((0,), (0,)), ((), ())), preferred_element_type=jnp.float32
    )


def contract_cols(left, right):
    return lax.dot_general(
        left, right, (((1,), (1,)), ((), ())), preferred_element_type=jnp.float32
    )


def norm_forward(resid, gain, shift):
    row_mean = jnp.mean(resid, axis=-1, keepdims=True)
    centered = resid - row_mean
    inv_root = lax.rsqrt(jnp.mean(centered * centered, axis=-1, keepdims=True) + eps_norm)
    normed = centered * inv_root
    return (normed * gain + shift, normed, inv_root)


def norm_backward(grad_out, normed, inv_root, gain):
    scaled = grad_out * gain
    grad_in = inv_root * (
        scaled
        - jnp.mean(scaled, axis=-1, keepdims=True)
        - normed * jnp.mean(scaled * normed, axis=-1, keepdims=True)
    )
    return (grad_in, jnp.sum(grad_out * normed, axis=0), jnp.sum(grad_out, axis=0))


def two_heads(value):
    left = lax.broadcasted_iota(jnp.int32, value.shape, 1) < value.shape[1] // 2
    none = jnp.zeros_like(value)
    return jnp.concatenate([jnp.where(left, value, none), jnp.where(left, none, value)], axis=0)


def one_pair(value):
    rows = value.shape[0] // 2
    left = lax.broadcasted_iota(jnp.int32, (rows, value.shape[1]), 1) < value.shape[1] // 2
    return jnp.where(left, value[:rows], value[rows:])


def pair_scores(info, causal, queries, key_rows):
    scores = lax.dot_general(
        queries, key_rows, (((1,), (1,)), ((), ())), preferred_element_type=jnp.float32
    )
    column = lax.broadcasted_iota(jnp.int32, scores.shape, 1)
    if causal:
        row = lax.broadcasted_iota(jnp.int32, scores.shape, 0)
        allowed = column <= jnp.where(row < scores.shape[0] // 2, row, row - scores.shape[0] // 2)
    else:
        allowed = column < info[pl.program_id(0)]
    return jnp.where(allowed, scores, mask_fill)


def attend_kernel(causal, info, queries, keys, values, out, logs):
    steps, width = queries.shape
    lane = lax.broadcasted_iota(jnp.int32, (steps, 128), 1)
    kept = jnp.zeros((steps, 128), jnp.float32)

    def first(pair):
        here = slice(pair * 128, (pair + 1) * 128)
        return pair_scores(info, causal, two_heads(queries[:, here]), keys[:, here])

    following = first(0)
    for pair in range(width // 128):
        here = slice(pair * 128, (pair + 1) * 128)
        scores = following
        if pair + 1 < width // 128:
            following = first(pair + 1)
        row_max = jnp.max(scores, axis=1, keepdims=True)
        expos = jnp.exp(scores - row_max)
        row_sum = jnp.sum(expos, axis=1, keepdims=True)
        probs = (expos * (1.0 / row_sum)).astype(jnp.bfloat16)
        out[:, here] = one_pair(
            jnp.dot(probs, values[:, here], preferred_element_type=jnp.float32)
        ).astype(jnp.bfloat16)
        log = row_max + jnp.log(row_sum)
        kept = jnp.where(lane == 2 * pair, log[:steps], kept)
        kept = jnp.where(lane == 2 * pair + 1, log[steps:], kept)
    logs[...] = kept


def attend_back_kernel(causal, info, queries, keys, values, logs, grads, *refs):
    d_queries, d_keys, d_values = refs[-3:]
    steps, width = queries.shape
    rows_first = (((0,), (0,)), ((), ()))

    def first(pair):
        here = slice(pair * 128, (pair + 1) * 128)
        both = two_heads(queries[:, here])
        both_grads = two_heads(grads[:, here])
        scores = pair_scores(info, causal, both, keys[:, here])
        d_probs = lax.dot_general(
            both_grads, values[:, here], (((1,), (1,)), ((), ())), preferred_element_type=jnp.float32
        )
        return both, both_grads, scores, d_probs

    following = first(0)
    for pair in range(width // 128):
        here = slice(pair * 128, (pair + 1) * 128)
        both, both_grads, scores, d_probs = following
        if pair + 1 < width // 128:
            following = first(pair + 1)
        log = jnp.concatenate(
            [logs[:, 2 * pair : 2 * pair + 1], logs[:, 2 * pair + 1 : 2 * pair + 2]], axis=0
        )
        probs = jnp.exp(scores - log)
        d_values[:, here] = lax.dot_general(
            probs.astype(jnp.bfloat16), both_grads, rows_first, preferred_element_type=jnp.float32
        ).astype(jnp.bfloat16)
        delta = jnp.sum(d_probs * probs, axis=1, keepdims=True)
        d_scores = (probs * (d_probs - delta)).astype(jnp.bfloat16)
        d_queries[:, here] = one_pair(
            jnp.dot(d_scores, keys[:, here], preferred_element_type=jnp.float32)
        ).astype(jnp.bfloat16)
        d_keys[:, here] = lax.dot_general(
            d_scores, both, rows_first, preferred_element_type=jnp.float32
        ).astype(jnp.bfloat16)


def attend(causal, lengths, queries, keys, values, logs=None, grads=None, earlier=()):
    count = lengths.shape[0]
    width = queries.shape[1]
    steps, spans = queries.shape[0] // count, keys.shape[0] // count
    short = pl.BlockSpec((steps, width), lambda i, s: (i, 0))
    long = pl.BlockSpec((spans, width), lambda i, s: (i, 0))
    thin = pl.BlockSpec((steps, 128), lambda i, s: (i, 0))
    like = lambda value: jax.ShapeDtypeStruct(value.shape, jnp.bfloat16)
    if grads is None:
        kernel, operands = attend_kernel, (queries, keys, values)
        in_specs, out_specs = [short, long, long], [short, thin]
        out_shape = [like(queries), jax.ShapeDtypeStruct((queries.shape[0], 128), jnp.float32)]
    else:
        kernel, operands = attend_back_kernel, (queries, keys, values, logs, grads, *earlier)
        in_specs, out_specs = [short, long, long, thin, short], [short, long, long]
        in_specs += [pl.BlockSpec(memory_space=pl.ANY)] * len(earlier)
        out_shape = [like(queries), like(keys), like(values)]
    flops = (4 if grads is None else 10) * queries.shape[0] * spans * width
    return pl.pallas_call(
        functools.partial(kernel, causal),
        grid_spec=pltpu.PrefetchScalarGridSpec(
            num_scalar_prefetch=1, grid=(count,), in_specs=in_specs, out_specs=out_specs
        ),
        out_shape=out_shape,
        compiler_params=pltpu.CompilerParams(vmem_limit_bytes=48 << 20),
        cost_estimate=pl.CostEstimate(
            flops=4 * flops, bytes_accessed=8 * keys.shape[0] * width, transcendentals=0
        ),
        name=("self" if causal else "cross") + ("_attend" if grads is None else "_attend_back"),
    )(lengths, *operands)


def gelu_parts(value):
    place = 1.0 / (1.0 + 0.3275911 * root_half * jnp.abs(value))
    bell = jnp.exp(-0.5 * value * value)
    series = 1.061405429
    for factor in (-1.453152027, 1.421413741, -0.284496736, 0.254829592):
        series = series * place + factor
    tail = 0.5 * series * place * bell
    share = jnp.where(value > 0.0, 1.0 - tail, tail)
    return value * share, share + value * (inv_root_tau * bell)


SMALL = pl.CostEstimate(flops=1 << 20, bytes_accessed=1 << 16, transcendentals=0)
PIECE = 128
CHUNK = 256


def vocab_tile(share):
    return max(d for d in range(16, 901, 16) if share % d == 0)


def columns(block):
    return jnp.concatenate([block] * 16, axis=0).T


def each_count(live, chunks, run):
    for taken in range(1, chunks + 1):
        above = live > (taken - 1) * CHUNK
        upto = live <= taken * CHUNK if taken < chunks else live >= 0

        @pl.when(jnp.logical_and(above, upto))
        def _():
            run(taken)


def piece_places(info, step, count):
    base = 1 + step * (count + 1)
    return [pl.multiple_of(info[base + i], 16) for i in range(count)], info[base + count]


def rows_kernel(step, info, ids, own, mate, table, *refs):
    expo, packed, tops, own_sums, mate_sums, own_logs, mate_logs, acc, top, total, marks = refs[-11:]
    expo, packed, tops = expo.at[0], packed.at[0], tops.at[0]
    tile = pl.program_id(0)
    wide = table.shape[0]
    pieces = own.shape[0] // PIECE
    count = 2 * pieces
    places, live = piece_places(info, step, count)

    @pl.when(tile == 0)
    def _():
        acc[...] = jnp.zeros_like(acc)
        top[...] = jnp.full_like(top, mask_fill)
        total[...] = jnp.zeros_like(total)
        tops[...] = jnp.zeros_like(tops)
        packed[...] = jnp.zeros_like(packed)
        marks[...] = jnp.full_like(marks, -1.0)
        for piece in range(count):
            side = own if piece < pieces else mate
            low = piece % pieces * PIECE
            packed[pl.ds(places[piece], PIECE), :] = side[low : low + PIECE, :]
            marks[pl.ds(places[piece], PIECE), :] = columns(ids[piece])

    lane = lax.broadcasted_iota(jnp.int32, (CHUNK, 128), 1)
    column = lax.broadcasted_iota(jnp.int32, (CHUNK, wide), 1)

    def scores(chunk):
        return lax.dot_general(
            packed[chunk * CHUNK : (chunk + 1) * CHUNK, :],
            table[...],
            (((1,), (1,)), ((), ())),
            preferred_element_type=jnp.float32,
        )

    def soften(chunk, logits):
        here = slice(chunk * CHUNK, (chunk + 1) * CHUNK)
        target = marks[here, 0:1].astype(jnp.int32) - tile * wide
        logits = jnp.where(column == target, mask_fill, logits)
        before = top[here, 0:1]
        now = jnp.maximum(before, jnp.max(logits, axis=1, keepdims=True))
        fade = jnp.exp(before - now)
        grown = jnp.exp(logits - now)
        total[here, :] = jnp.broadcast_to(
            total[here, 0:1] * fade + jnp.sum(grown, axis=1, keepdims=True), (CHUNK, 128)
        )
        top[here, :] = jnp.broadcast_to(now, (CHUNK, 128))
        tops[here, :] = jnp.where(lane == tile, now, tops[here, :])
        grown = grown.astype(jnp.bfloat16)
        expo[0, here, :] = grown
        return here, grown, fade

    def gather(here, grown, fade):
        acc[here, :] = acc[here, :] * fade + jnp.dot(
            grown, table[...], preferred_element_type=jnp.float32
        )

    def run(taken):
        logits = [scores(0)]
        late = None
        for chunk in range(taken):
            if chunk + 1 < taken:
                logits.append(scores(chunk + 1))
            ready = soften(chunk, logits[chunk])
            if late is not None:
                gather(*late)
            late = ready
        gather(*late)

    each_count(live, count * PIECE // CHUNK, run)

    @pl.when(tile == pl.num_programs(0) - 1)
    def _():
        for piece in range(count):
            here = pl.ds(places[piece], PIECE)
            mass = total[here, :]
            share = jnp.where(mass > 0.0, 1.0 / jnp.maximum(mass, 1e-30), 0.0)[:, 0:1]
            sums, logs = (own_sums, own_logs) if piece < pieces else (mate_sums, mate_logs)
            low = piece % pieces * PIECE
            sums[low : low + PIECE, :] = (acc[here, :] * share).astype(jnp.bfloat16)
            logs[piece % pieces] = (top[here, :] + jnp.log(jnp.maximum(mass, 1e-30))).T[0:8]


def rows_pass(step, steps, info, ids, own, mate, table, cores, kept, earlier):
    group, width = own.shape
    share = table.shape[0] // cores
    wide = vocab_tile(share)
    tiles = share // wide
    rows = 2 * group
    count = rows // PIECE
    room = rows + PIECE
    whole = lambda i, s: (0, 0)
    cube = lambda i, s: (0, 0, 0)
    return pl.pallas_call(
        functools.partial(rows_kernel, step),
        grid_spec=pltpu.PrefetchScalarGridSpec(
            num_scalar_prefetch=1,
            grid=(tiles,),
            in_specs=[
                pl.BlockSpec((count, 8, 128), lambda i, s: (step, 0, 0)),
                pl.BlockSpec((group, width), whole),
                pl.BlockSpec((group, width), whole),
                pl.BlockSpec((wide, width), lambda i, s: (s[0] * tiles + i, 0)),
            ]
            + [pl.BlockSpec(memory_space=pl.ANY)] * (len(kept) + len(earlier)),
            out_specs=[
                pl.BlockSpec((1, 1, rows, wide), lambda i, s: (step, i, 0, 0)),
                pl.BlockSpec((1, room, width), lambda i, s: (step, 0, 0)),
                pl.BlockSpec((1, room, 128), lambda i, s: (step, 0, 0)),
                pl.BlockSpec((group, width), whole),
                pl.BlockSpec((group, width), whole),
                pl.BlockSpec((count // 2, 8, 128), cube),
                pl.BlockSpec((count // 2, 8, 128), cube),
            ],
            scratch_shapes=[
                pltpu.VMEM((room, width), jnp.float32),
                pltpu.VMEM((room, 128), jnp.float32),
                pltpu.VMEM((room, 128), jnp.float32),
                pltpu.VMEM((room, 128), jnp.float32),
            ],
        ),
        out_shape=[
            jax.ShapeDtypeStruct((steps, tiles, rows, wide), jnp.bfloat16),
            jax.ShapeDtypeStruct((steps, room, width), jnp.bfloat16),
            jax.ShapeDtypeStruct((steps, room, 128), jnp.float32),
            jax.ShapeDtypeStruct((group, width), jnp.bfloat16),
            jax.ShapeDtypeStruct((group, width), jnp.bfloat16),
            jax.ShapeDtypeStruct((count // 2, 8, 128), jnp.float32),
            jax.ShapeDtypeStruct((count // 2, 8, 128), jnp.float32),
        ],
        input_output_aliases={5 + place: place for place in range(len(kept))},
        compiler_params=pltpu.CompilerParams(vmem_limit_bytes=60 << 20),
        cost_estimate=SMALL,
        name=f"rows_pass_{step}",
    )(info, ids, own, mate, table, *kept, *earlier)


def join_kernel(own, other, own_log, other_log, out):
    for piece in range(own_log.shape[0]):
        here = slice(piece * PIECE, (piece + 1) * PIECE)
        log = jnp.logaddexp(own_log[piece], other_log[piece])
        left = columns(jnp.exp(own_log[piece] - log))[:, 0:1]
        right = columns(jnp.exp(other_log[piece] - log))[:, 0:1]
        out[here, :] = (
            own[here, :].astype(jnp.float32) * left + other[here, :].astype(jnp.float32) * right
        ).astype(jnp.bfloat16)


def join_pass(own, other, own_log, other_log):
    rows, width = own.shape
    flat = pl.BlockSpec((CHUNK, width), lambda i: (i, 0))
    cube = pl.BlockSpec((CHUNK // PIECE, 8, 128), lambda i: (i, 0, 0))
    return pl.pallas_call(
        join_kernel,
        grid=(rows // CHUNK,),
        in_specs=[flat, flat, cube, cube],
        out_specs=flat,
        out_shape=jax.ShapeDtypeStruct((rows, width), jnp.bfloat16),
        cost_estimate=SMALL,
        name="join_pass",
    )(own, other, own_log, other_log)


def home_kernel(count, logs, weight, targets, *refs):
    parts, out = refs[:count], refs[-1]
    log = logs[0]
    share = jnp.exp(log - jnp.max(log, axis=0, keepdims=True))
    share = columns(share / jnp.sum(share, axis=0, keepdims=True))
    mean = parts[0][...].astype(jnp.float32) * share[:, 0:1]
    for place in range(1, count):
        mean = mean + parts[place][...].astype(jnp.float32) * share[:, place : place + 1]
    out[...] = columns(weight[0])[:, 0:1] * (targets[0] - mean)


def home_pass(logs, weight, targets, parts, earlier):
    rows, width = parts[0].shape
    questions = targets.shape[0]
    flat = pl.BlockSpec((PIECE, width), lambda i: (i, 0))
    cube = pl.BlockSpec((1, 8, 128), lambda i: (i, 0, 0))
    return pl.pallas_call(
        functools.partial(home_kernel, len(parts)),
        grid=(rows // PIECE,),
        in_specs=[cube, cube, pl.BlockSpec((1, PIECE, width), lambda i: (i % questions, 0, 0))]
        + [flat] * len(parts)
        + [pl.BlockSpec(memory_space=pl.ANY)] * len(earlier),
        out_specs=flat,
        out_shape=jax.ShapeDtypeStruct((rows, width), jnp.float32),
        cost_estimate=SMALL,
        name="home_pass",
    )(logs, weight, targets, *parts, *earlier)


def table_kernel(first, info, facts, tops, rows, expos, *refs):
    outs, acc, scales = refs[-4:-2], refs[-2], refs[-1]
    tile = pl.program_id(0) + first
    sources, _, both, wide = expos.shape
    count = both // PIECE

    @pl.when(pl.program_id(0) == 0)
    def _():
        def ready(source, _):
            places, _ = piece_places(info, source, count)
            scales[source] = jnp.zeros(scales.shape[1:], jnp.float32)
            for piece in range(count):
                scales[source, pl.ds(places[piece], PIECE), :] = columns(facts[source * count + piece])
            raw = scales[source]
            lane = lax.broadcasted_iota(jnp.int32, raw.shape, 1)
            weight = raw[:, 0:1]
            spread = jnp.where(weight == 0.0, 0.0, -weight * jnp.exp(tops[source] - raw[:, 1:2]))
            spread = jnp.where(lane == 127, raw[:, 2:3], spread)
            scales[source] = jnp.where(lane == 126, raw[:, 3:4], spread)
            return 0

        lax.fori_loop(0, sources, ready, 0)

    acc[...] = jnp.zeros_like(acc)

    def add(source, begin, size):
        here = pl.ds(pl.multiple_of(begin, CHUNK), size)
        scale = scales[source, here, :]
        lane = lax.broadcasted_iota(jnp.int32, (size, 128), 1)
        column = lax.broadcasted_iota(jnp.int32, (size, wide), 1)
        spread = jnp.sum(jnp.where(lane == tile, scale, 0.0), axis=1, keepdims=True)
        target = scale[:, 126:127].astype(jnp.int32) - tile * wide
        grad = expos[source, 0, here, :].astype(jnp.float32) * spread
        grad = jnp.where(column == target, scale[:, 127:128], grad).astype(jnp.bfloat16)
        acc[...] += lax.dot_general(
            grad,
            rows[source, here, :],
            (((0,), (0,)), ((), ())),
            preferred_element_type=jnp.float32,
        )

    def add_source(source, _):
        live = info[1 + source * (count + 1) + count]
        chunks = (live + CHUNK - 1) // CHUNK

        @pl.when(chunks == 4)
        def _():
            add(source, 0, 4 * CHUNK)

        @pl.when(jnp.logical_or(chunks == 2, chunks == 3))
        def _():
            add(source, 0, 2 * CHUNK)

        @pl.when(chunks % 2 == 1)
        def _():
            add(source, (chunks - 1) * CHUNK, CHUNK)

        return 0

    lax.fori_loop(0, sources, add_source, 0)
    half = wide // 2
    for side, out in enumerate(outs):
        for place in range(out.shape[0]):
            size = out.shape[3]
            out[place, 0] = acc[
                side * half : (side + 1) * half, place * size : (place + 1) * size
            ].astype(jnp.bfloat16)


def table_pass(info, facts, tops, rows, expos, first, tiles, n_pb, earlier):
    sources, _, both, wide = expos.shape
    _, room, width = rows.shape
    own = width // n_pb
    once = pl.Buffered(1)
    cube = lambda i, s: (0, 0, 0)
    return pl.pallas_call(
        functools.partial(table_kernel, first),
        grid_spec=pltpu.PrefetchScalarGridSpec(
            num_scalar_prefetch=1,
            grid=(tiles,),
            in_specs=[
                pl.BlockSpec(facts.shape, cube, pipeline_mode=once),
                pl.BlockSpec(tops.shape, cube, pipeline_mode=once),
                pl.BlockSpec(rows.shape, cube, pipeline_mode=once),
                pl.BlockSpec((sources, 1, both, wide), lambda i, s: (0, i + first, 0, 0)),
            ]
            + [pl.BlockSpec(memory_space=pl.ANY)] * len(earlier),
            out_specs=[pl.BlockSpec((n_pb, 1, wide // 2, own), lambda i, s: (0, i, 0, 0))] * 2,
            scratch_shapes=[
                pltpu.VMEM((wide, width), jnp.float32),
                pltpu.VMEM((sources, room, 128), jnp.float32),
            ],
        ),
        out_shape=[jax.ShapeDtypeStruct((n_pb, tiles, wide // 2, own), jnp.bfloat16)] * 2,
        compiler_params=pltpu.CompilerParams(vmem_limit_bytes=60 << 20),
        cost_estimate=SMALL,
        name=f"table_pass_{first}",
    )(info, facts, tops, rows, expos, *earlier)


def gather_kernel(*refs):
    mats, rows = refs[:3], refs[3:5]
    full, laid = refs[5:8], refs[8:10]
    send, recv, near = refs[10:]
    slots = full[0].shape[1]
    pb, place = lax.axis_index("pb"), lax.axis_index("slot")
    mate = pb // 2 * 2 + (pb + 1) % 2
    side_x = pb // 4 * 4 + (pb + 2) % 4
    side_y = (pb + 4) % 8
    corner = (side_x + 4) % 8
    barrier = pltpu.get_barrier_semaphore()
    partners = [(mate, place), (side_x, place), (side_y, place)]
    partners += [(pb, (place + step) % slots) for step in range(1, slots)]
    for partner in partners:
        pl.semaphore_signal(barrier, inc=1, device_id=partner, device_id_type=pl.DeviceIdType.MESH)
    pl.semaphore_wait(barrier, len(partners))

    sent, unread, stays, ready = [], {}, [], {}

    def push(source, target, device):
        copy = pltpu.make_async_remote_copy(
            src_ref=source,
            dst_ref=target,
            send_sem=send.at[len(sent)],
            recv_sem=recv.at[len(sent)],
            device_id=device,
            device_id_type=pl.DeviceIdType.MESH,
        )
        copy.start()
        unread[len(sent)] = copy
        sent.append(copy)
        return len(sent) - 1

    def read(number):
        unread.pop(number).wait_recv()

    def put(source, target):
        copy = pltpu.make_async_copy(source, target, near.at[len(stays)])
        copy.start()
        stays.append(copy)

    def move_rows(step):
        goal = (place + step) % slots
        for source, target in zip(rows, laid):
            block = source.at[:, goal]
            spot = target.at[:, :, place]
            if step:
                push(block, spot, (pb, goal))
            else:
                put(block, spot)

    def part(mat, at_pb, origin, half):
        size = full[mat].shape[2] // 2
        return full[mat].at[at_pb, origin, pl.ds(half * size, size)]

    def own_moves(step, mat, origin, source):
        size = full[mat].shape[2] // 2
        first, second = (source.at[pl.ds(half * size, size)] for half in range(2))
        first_at, second_at = (part(mat, pb, origin, half) for half in range(2))
        ready[step, mat] = [
            push(first, first_at, (side_x, place)),
            push(second, second_at, (side_y, place)),
            push(first, first_at, (side_y, place)),
            push(second, second_at, (side_x, place)),
        ]
        push(source, full[mat].at[pb, origin], (mate, place))

    def onward(step, mat, origin):
        over_x, over_y, _, _ = ready[step, mat]
        read(over_x)
        block = part(mat, side_x, origin, 0)
        ready[step, mat].append(push(block, block, (side_y, place)))
        push(block, block, (mate, place))
        read(over_y)
        block = part(mat, side_y, origin, 1)
        ready[step, mat].append(push(block, block, (side_x, place)))
        push(block, block, (mate, place))

    def finish(step, mat, origin):
        _, _, over_y, over_x, first, second = ready[step, mat]
        for number, at_pb, half in (
            (over_y, side_y, 0),
            (over_x, side_x, 1),
            (first, corner, 0),
            (second, corner, 1),
        ):
            read(number)
            block = part(mat, at_pb, origin, half)
            push(block, block, (mate, place))

    count = len(mats)
    following = (pb, (place + 1) % slots)
    ring = [push(mats[mat], full[mat].at[pb, place], following) for mat in range(count)]
    for mat in range(count):
        own_moves(0, mat, place, mats[mat])
        put(mats[mat], full[mat].at[pb, place])
    move_rows(1)
    move_rows(0)
    for step in range(1, slots + 1):
        origin = (place + slots - step) % slots
        before = (place + slots - step + 1) % slots
        if step < slots:
            for mat in range(count):
                read(ring[mat])
                block = full[mat].at[pb, origin]
                if step < slots - 1:
                    ring[mat] = push(block, block, following)
                own_moves(step, mat, origin, block)
        if step == 1:
            move_rows(slots - 1)
        if step == 2:
            for other in range(2, slots - 1):
                move_rows(other)
        for mat in range(count):
            onward(step - 1, mat, before)
        for mat in range(count):
            finish(step - 1, mat, before)
    for number in sorted(unread):
        read(number)
    for copy in sent:
        copy.wait_send()
    for copy in stays:
        copy.wait()


def gather_inputs(x_in, memory, attn_w, ffn_in, ffn_out):
    n_pb, slots = lax.axis_size("pb"), lax.axis_size("slot")
    mats, rows = (attn_w, ffn_in, ffn_out), (x_in, memory)
    width = attn_w.shape[1]
    rows = [row.reshape((-1, slots) + row.shape[1:]) for row in rows]
    if (n_pb, slots) != (8, 4):
        return (
            to_slots(x_in),
            to_slots(memory),
            *(gather_all(mat).reshape(-1, width) for mat in mats),
        )
    shapes = [jax.ShapeDtypeStruct((n_pb, slots) + mat.shape, mat.dtype) for mat in mats]
    for row in rows:
        own, _, questions, steps, _ = row.shape
        shapes.append(jax.ShapeDtypeStruct((own, questions, slots, steps, width), row.dtype))
    copies = 13 * len(mats) * slots + (slots - 1) * (len(mats) + len(rows))
    anywhere = pl.BlockSpec(memory_space=pl.ANY)
    *full, x_here, mem_here = pl.pallas_call(
        gather_kernel,
        in_specs=[anywhere] * 5,
        out_specs=[anywhere] * 5,
        out_shape=shapes,
        scratch_shapes=[
            pltpu.SemaphoreType.DMA((copies,)),
            pltpu.SemaphoreType.DMA((copies,)),
            pltpu.SemaphoreType.DMA((len(mats) + len(rows),)),
        ],
        compiler_params=pltpu.CompilerParams(collective_id=0, has_side_effects=True),
        name="gather_inputs",
    )(*mats, *rows)
    own, questions, _, _, _ = x_here.shape
    return (
        x_here.reshape(own, questions, -1, width),
        mem_here.reshape(own, questions, -1, width),
        *(mat.reshape(-1, width) for mat in full),
    )


UNIT = 64


def scatter_kernel(*refs):
    mats, rows, few = refs[:3], refs[3], refs[4]
    outs, laid, few_out = refs[5:8], refs[8], refs[9]
    (from_core, kept, wide_x, wide_y, narrow_x, narrow_y, from_slot, few_here, few_there, few_slot) = refs[10:20]
    send, recv, near = refs[20:]
    depth = kept.shape[0]
    slots = mats[0].shape[2]
    pb, place = lax.axis_index("pb"), lax.axis_index("slot")
    core, at_x, at_y = pb % 2, pb // 2 % 2, pb // 4
    mate = (pb // 2 * 2 + (pb + 1) % 2, place)
    side_x = (pb // 4 * 4 + (pb + 2) % 4, place)
    side_y = ((pb + 4) % 8, place)
    barrier = pltpu.get_barrier_semaphore()
    partners = [mate, side_x, side_y]
    partners += [(pb, (place + step) % slots) for step in range(1, slots)]
    for partner in partners:
        pl.semaphore_signal(barrier, inc=1, device_id=partner, device_id_type=pl.DeviceIdType.MESH)
    pl.semaphore_wait(barrier, len(partners))

    sent = []

    def push(source, target, device):
        copy = pltpu.make_async_remote_copy(
            src_ref=source,
            dst_ref=target,
            send_sem=send.at[len(sent)],
            recv_sem=recv.at[len(sent)],
            device_id=device,
            device_id_type=pl.DeviceIdType.MESH,
        )
        copy.start()
        sent.append(copy)
        return copy

    stays = []

    def put(source, target):
        copy = pltpu.make_async_copy(source, target, near.at[len(stays)])
        copy.start()
        stays.append(copy)
        return copy

    units = [
        (mat, unit)
        for mat in (1, 2, 0)
        for unit in range(mats[mat].shape[3] // UNIT)
    ]

    def block(number, which):
        mat, unit = units[number]
        return mats[mat].at[:, which, :, pl.ds(unit * UNIT, UNIT)]

    half = UNIT // 2
    first, second = pl.ds(0, half), pl.ds(half, half)
    ahead = 2
    by_core = [push(block(n, 1 - core), from_core.at[n], mate) for n in range(ahead)]
    loads = {n: put(block(n, core), kept.at[n % depth]) for n in range(min(depth, len(units)))}
    by_rows = []
    for step in range(1, slots):
        goal = (place + step) % slots
        by_rows.append(push(rows.at[:, :, goal], laid.at[:, place], (pb, goal)))
    at_home = put(rows.at[:, :, place], laid.at[:, place])
    by_few = push(few, few_there.at[0], mate)

    def total(left, right):
        return (left.astype(jnp.float32) + right.astype(jnp.float32)).astype(jnp.bfloat16)

    over, across, along = {}, {}, {}

    def from_cores(n):
        slot = n % depth
        by_core[n].wait_recv()
        if n + ahead < len(units):
            by_core.append(push(block(n + ahead, 1 - core), from_core.at[n + ahead], mate))
        loads[n].wait()

        def step(i, _):
            y, x, z = i // (2 * slots), i // slots % 2, i % slots
            kept[slot, 2 * y + x, z] = total(kept[slot, 2 * y + x, z], from_core[n, 2 * y + x, z])
            return 0

        lax.fori_loop(0, 4 * slots, step, 0)
        over[n] = [
            push(kept.at[slot, 1 - at_x, :, first], wide_x.at[n, 0], side_x),
            push(kept.at[slot, 2 + 1 - at_x, :, first], wide_x.at[n, 1], side_x),
            push(kept.at[slot, pl.ds(2 * (1 - at_y), 2), :, second], wide_y.at[n], side_y),
        ]

    def over_first(n):
        slot = n % depth
        for copy in over[n]:
            copy.wait_recv()

        def step(i, _):
            side, z = i // slots, i % slots
            spot = 2 * side + at_x
            kept[slot, spot, z, 0:half] = total(kept[slot, spot, z, 0:half], wide_x[n, side, z])
            spot = 2 * at_y + side
            kept[slot, spot, z, half:UNIT] = total(kept[slot, spot, z, half:UNIT], wide_y[n, side, z])
            return 0

        lax.fori_loop(0, 2 * slots, step, 0)
        across[n] = [
            push(kept.at[slot, 2 * (1 - at_y) + at_x, :, first], narrow_y.at[n], side_y),
            push(kept.at[slot, 2 * at_y + 1 - at_x, :, second], narrow_x.at[n], side_x),
        ]

    def over_second(n):
        slot = n % depth
        for copy in across[n]:
            copy.wait_recv()
        spot = 2 * at_y + at_x

        def step(z, _):
            kept[slot, spot, z, 0:half] = total(kept[slot, spot, z, 0:half], narrow_y[n, z])
            kept[slot, spot, z, half:UNIT] = total(kept[slot, spot, z, half:UNIT], narrow_x[n, z])
            return 0

        lax.fori_loop(0, slots, step, 0)
        along[n] = []
        for step_on in range(1, slots):
            goal = (place + step_on) % slots
            along[n].append(push(kept.at[slot, spot, goal], from_slot.at[n, step_on - 1], (pb, goal)))

    def over_slots(n):
        slot = n % depth
        mat, unit = units[n]
        for copy in along[n]:
            copy.wait_recv()
        here = kept[slot, 2 * at_y + at_x, place].astype(jnp.float32)
        for step_on in range(1, slots):
            here = here + from_slot[n, step_on - 1].astype(jnp.float32)
        outs[mat][unit * UNIT : (unit + 1) * UNIT, :] = here
        if n + depth < len(units):
            for copy in over[n] + across[n] + along[n]:
                copy.wait_send()
            loads[n + depth] = put(block(n + depth, core), kept.at[slot])

    stages = (from_cores, over_first, over_second, over_slots)
    for turn in range(len(units) + len(stages) - 1):
        for lag, stage in enumerate(stages):
            if 0 <= turn - lag < len(units):
                stage(turn - lag)
        if turn == 0:
            by_few.wait_recv()
            few_here[0] = few[...] + few_there[0]
            by_few = push(few_here.at[0], few_there.at[1], side_x)
        if turn == 1:
            by_few.wait_recv()
            few_here[1] = few_here[0] + few_there[1]
            by_few = push(few_here.at[1], few_there.at[2], side_y)
        if turn == 2:
            by_few.wait_recv()
            few_here[2] = few_here[1] + few_there[2]
            few_slot[place] = few_here[2]
            by_few = [
                push(few_here.at[2], few_slot.at[place], (pb, (place + step) % slots))
                for step in range(1, slots)
            ]
    for copy in by_few:
        copy.wait_recv()
    every = few_slot[0]
    for step in range(1, slots):
        every = every + few_slot[step]
    few_out[...] = every
    for copy in by_rows:
        copy.wait_recv()
    at_home.wait()
    freed = set()
    for n in range(len(units) - depth):
        freed.update(id(copy) for copy in over[n] + across[n] + along[n])
    for copy in sent:
        if id(copy) not in freed:
            copy.wait_send()


def scatter_outputs(grad_attn, grad_in_w, grad_out_w, grad_inputs, small):
    n_pb, slots = lax.axis_size("pb"), lax.axis_size("slot")
    if (n_pb, slots) != (8, 4):
        return (
            scatter_all(grad_attn),
            scatter_all(grad_in_w),
            scatter_all(grad_out_w),
            to_positions(leave_slots(grad_inputs)),
            sum_all(small, ("core", "x", "y", "slot")),
        )
    width = grad_attn.shape[1]
    mats = [
        mat.reshape(n_pb // 2, 2, slots, -1, width)
        for mat in (grad_attn, grad_in_w, grad_out_w)
    ]
    own, questions, steps, _ = grad_inputs.shape
    rows = grad_inputs.reshape(own, questions, slots, steps // slots, width)
    laid = jax.ShapeDtypeStruct((own, slots, questions, steps // slots, width), rows.dtype)
    units = sum(mat.shape[3] for mat in mats) // UNIT
    depth = 5
    copies = units * (1 + 3 + 2 + slots - 1) + (slots - 1) + 3 + slots - 1
    anywhere, inside = pl.BlockSpec(memory_space=pl.ANY), pl.BlockSpec(memory_space=pltpu.VMEM)
    half = UNIT // 2
    low, high = jnp.bfloat16, jnp.float32
    *shards, laid, small = pl.pallas_call(
        scatter_kernel,
        in_specs=[anywhere] * 4 + [inside],
        out_specs=[inside] * 3 + [anywhere, inside],
        out_shape=[jax.ShapeDtypeStruct(mat.shape[3:], high) for mat in mats]
        + [laid, jax.ShapeDtypeStruct(small.shape, high)],
        scratch_shapes=[
            pltpu.VMEM((units, 4, slots, UNIT, width), low),
            pltpu.VMEM((depth, 4, slots, UNIT, width), low),
            pltpu.VMEM((units, 2, slots, half, width), low),
            pltpu.VMEM((units, 2, slots, half, width), low),
            pltpu.VMEM((units, slots, half, width), low),
            pltpu.VMEM((units, slots, half, width), low),
            pltpu.VMEM((units, slots - 1, UNIT, width), low),
            pltpu.VMEM((3,) + small.shape, high),
            pltpu.VMEM((3,) + small.shape, high),
            pltpu.VMEM((slots,) + small.shape, high),
            pltpu.SemaphoreType.DMA((copies,)),
            pltpu.SemaphoreType.DMA((copies,)),
            pltpu.SemaphoreType.DMA((units + 1,)),
        ],
        compiler_params=pltpu.CompilerParams(
            collective_id=1, has_side_effects=True, vmem_limit_bytes=60 << 20
        ),
        cost_estimate=SMALL,
        name="scatter_outputs",
    )(*mats, rows, small)
    return (*shards, laid.reshape((-1,) + laid.shape[2:]), small)


def body(
    x_in,
    memory,
    doc_scores,
    valid_count,
    target_ids,
    target_len,
    mem_len,
    attn_w,
    ffn_in,
    ffn_out,
    ffn_bias,
    norms,
    embedding,
):
    x_here, mem_here, attn_full, in_full, out_full = gather_inputs(
        x_in, memory, attn_w, ffn_in, ffn_out
    )
    slots_here, questions, tgt_steps, model_width = x_here.shape
    mem_steps = mem_here.shape[2]
    seq_count = slots_here * questions
    head_dim = model_width // HEADS
    scaling = head_dim ** (-0.5)
    blocks = [
        attn_full[block_index * model_width : (block_index + 1) * model_width]
        for block_index in range(8)
    ]

    inputs = x_here.reshape(seq_count * tgt_steps, model_width)
    memory_rows = mem_here.reshape(seq_count * mem_steps, model_width)
    positions = jnp.arange(tgt_steps)
    place, slot_count = place_of("slot")
    core, cores = place_of("core")
    ring = (place - jnp.arange(slot_count)) % slot_count
    lengths_here = [mem_len] + [shifted(mem_len, "slot", step) for step in range(1, slot_count)]
    lengths_here = jnp.stack(lengths_here)[ring].reshape(slots_here, slot_count, questions)
    mem_lengths = pick(lengths_here, place, 1).reshape(seq_count)
    tgt_lengths = jnp.full_like(mem_lengths, tgt_steps)
    queries = (product(inputs, blocks[0]) * scaling).astype(jnp.bfloat16)
    key_rows = product(inputs, blocks[1]).astype(jnp.bfloat16)
    value_rows = product(inputs, blocks[2]).astype(jnp.bfloat16)
    self_out, self_lse = attend(True, tgt_lengths, queries, key_rows, value_rows)
    hidden_one, normed_one, root_one = norm_forward(
        inputs.astype(jnp.float32) + product(self_out, blocks[3]), norms[0], norms[1]
    )
    one_low = hidden_one.astype(jnp.bfloat16)
    cross_queries = (product(one_low, blocks[4]) * scaling).astype(jnp.bfloat16)
    cross_keys = product(memory_rows, blocks[5]).astype(jnp.bfloat16)
    cross_values = product(memory_rows, blocks[6]).astype(jnp.bfloat16)
    cross_out, cross_lse = attend(False, mem_lengths, cross_queries, cross_keys, cross_values)
    hidden_two, normed_two, root_two = norm_forward(
        hidden_one + product(cross_out, blocks[7]), norms[2], norms[3]
    )
    two_low = hidden_two.astype(jnp.bfloat16)
    pre_act = contract_cols(two_low, in_full) + ffn_bias
    act, slope = gelu_parts(pre_act)
    act_low, slope = act.astype(jnp.bfloat16), slope.astype(jnp.bfloat16)
    hidden_three, normed_three, root_three = norm_forward(
        hidden_two + product(act_low, out_full), norms[4], norms[5]
    )
    three_low = hidden_three.astype(jnp.bfloat16).reshape(
        slots_here, questions, tgt_steps, model_width
    )
    vocab_here = embedding.shape[0]
    share = vocab_here // cores
    pieces = slots_here * questions

    def both_cores(value):
        return jnp.stack([value, shifted(value, "core", 1)]) if cores > 1 else value[None]

    tokens = jnp.concatenate([target_ids, valid_count[:, None], target_len[:, None]], axis=1)
    tokens = both_cores(tokens)
    ids_all, valid_all, len_all = tokens[:, :, :tgt_steps], tokens[:, :, -2], tokens[:, :, -1]

    local = target_ids - place * vocab_here
    held = jnp.logical_and(local >= 0, local < vocab_here)
    target_rows = jnp.take(embedding, jnp.clip(local, 0, vocab_here - 1), axis=0)
    target_rows = jnp.where(held[..., None], target_rows, jnp.zeros_like(target_rows))
    target_rows = after(target_rows, x_here)
    found = [shifted(target_rows, "slot", step) for step in range(1, slot_count)]
    target_rows = sum([f.astype(jnp.float32) for f in found], target_rows.astype(jnp.float32))

    slot_ids = jnp.arange(slot_count)[:, None] + slot_count * jnp.arange(slots_here)[None]
    live_piece = slot_ids[:, None, :, None] < valid_all[None, :, None, :]
    long_piece = (len_all + 15) // 16 * 16
    long_piece = jnp.where(live_piece, long_piece[None, :, None, :], 0).reshape(slot_count, -1)
    ends = jnp.cumsum(long_piece, axis=1)
    packing = jnp.concatenate([ends - long_piece, ends[:, -1:]], axis=1)[ring]
    info = jnp.concatenate([core[None], packing.reshape(-1)]).astype(jnp.int32)
    piece_ids = (ids_all - (place * vocab_here + core * share)).astype(jnp.float32)
    piece_ids = jnp.broadcast_to(
        piece_ids[None, :, None], (slot_count, cores, slots_here, questions, tgt_steps)
    ).reshape(-1, 1, tgt_steps)
    ids_rows = jnp.broadcast_to(piece_ids, (piece_ids.shape[0], 8, tgt_steps))

    group = pieces * tgt_steps
    moving = three_low.reshape(group, model_width)
    arriving = [moving] + [shifted(moving, "slot", step) for step in range(1, slot_count)]
    kept, log_list, homes = (), [], []
    for step in range(slot_count):
        moving = arriving[step] if not step else after(arriving[step], own_logs)
        other = shifted(moving, "core", 1)
        earlier = (own_logs,) if step else ()
        *kept, own_sums, mate_sums, own_logs, mate_logs = rows_pass(
            step, slot_count, info, ids_rows, moving, other, embedding, cores, kept, earlier
        )
        log_list += [own_logs[:, 0], mate_logs[:, 0]]
        homes.append(
            join_pass(
                own_sums, shifted(mate_sums, "core", 1), own_logs, shifted(mate_logs, "core", 1)
            )
        )

    def by_slot(value):
        parts = [value] + [shifted(value, "slot", step) for step in range(1, slot_count)]
        return jnp.stack(parts)[ring]

    target_logit = jnp.sum(three_low.astype(jnp.float32) * target_rows[None], axis=-1)
    told = jnp.concatenate(log_list + [target_logit.reshape(-1, tgt_steps)], axis=0)
    told = both_cores(by_slot(told))
    hit_all = told[:, :, -pieces:].reshape(cores, slot_count, slots_here, questions, tgt_steps)
    hit_all = hit_all.transpose(2, 1, 0, 3, 4).reshape(-1, cores, questions, tgt_steps)
    logs = told[:, :, :-pieces].reshape(
        cores, slot_count, slot_count, cores, slots_here, questions, tgt_steps
    )
    logs = jnp.stack([logs[0], logs[1][:, :, ::-1]]) if cores > 1 else logs
    logs = jax.nn.logsumexp(logs, axis=0)
    turns = (jnp.arange(slot_count)[:, None] - jnp.arange(slot_count)[None]) % slot_count
    logs = jnp.take_along_axis(
        logs, turns.reshape((slot_count, slot_count) + (1,) * (logs.ndim - 2)), axis=1
    )
    rest_all = jax.nn.logsumexp(logs, axis=0)
    rest_all = rest_all.transpose(2, 0, 1, 3, 4).reshape(hit_all.shape)
    log_norm = jnp.logaddexp(rest_all, hit_all)
    live = positions < len_all[..., None]
    lengths = len_all.astype(jnp.float32)
    per_slot = jnp.sum(jnp.where(live[None], hit_all - log_norm, 0.0), axis=3) / lengths[None]
    valid = jnp.arange(per_slot.shape[0])[:, None, None] < valid_all[None]
    scores_t = both_cores(doc_scores).transpose(2, 0, 1)
    joint = jnp.where(valid, scores_t + per_slot, mask_fill)
    prior = jnp.where(valid, scores_t, mask_fill)
    joint_total = jax.nn.logsumexp(joint, axis=0)
    neg_marginal = jax.nn.logsumexp(prior, axis=0) - joint_total
    log_post = joint - joint_total
    posterior = jnp.exp(log_post)
    entropy_q = -jnp.sum(posterior * log_post, axis=0)
    objective_part = jnp.sum((lengths * (neg_marginal + entropy_weight * entropy_q))[0])
    slot_weight = -posterior * (1.0 + entropy_weight * (log_post + entropy_q[None]))
    token_weight = jnp.where(live[None], slot_weight[..., None], 0.0)
    hit_weight = token_weight * jax.nn.sigmoid(rest_all - hit_all)

    def own_slots(value):
        value = value[:, 0].reshape(slots_here, slot_count, questions, tgt_steps)
        return pick(value, place, 1)

    def ring_rows(value):
        value = value.reshape(slots_here, slot_count, cores, questions, tgt_steps)
        return value.transpose(1, 2, 0, 3, 4)[ring].reshape(-1, tgt_steps)

    facts = [ring_rows(value) for value in (token_weight, log_norm, hit_weight)]
    facts = jnp.stack(facts + [ids_rows[:, 0]] + [jnp.zeros_like(facts[0])] * 4, axis=1)
    expos, packed, tops = kept
    tiles = expos.shape[1]
    n_pb = lax.axis_size("pb")
    tall, wide, _ = grid_of(n_pb)
    sends = tuple(homes[1:])
    homes[1:] = [
        shifted(homes[step], "slot", slot_count - step) for step in range(1, slot_count)
    ]
    table_grads = []
    for first, count in ((0, tiles),):
        sides = [
            side.reshape((tall, wide, cores) + side.shape[1:])
            for side in table_pass(
                info, facts, tops, packed, expos, first, count, n_pb, sends
            )
        ]
        sends = (ring_first(sides[0], "x", 1), ring_first(sides[1], "y", 0))
        table_grads.append(sides)

    def over_first(sides, late):
        return (
            ring_scatter(sides[0], "x", 1, late).astype(jnp.bfloat16),
            ring_scatter(sides[1], "y", 0, late).astype(jnp.bfloat16),
        )

    def over_second(sides, late):
        return (
            ring_scatter(sides[0], "y", 0, late).astype(jnp.bfloat16),
            ring_scatter(sides[1], "x", 0, late).astype(jnp.bfloat16),
        )

    def second_sends(sides):
        return ring_first(sides[0], "y", 0), ring_first(sides[1], "x", 0)

    home_logs = pick(logs, place, 1)[:, 0][(place + jnp.arange(slot_count)) % slot_count]
    home_logs = home_logs.reshape(slot_count, pieces, tgt_steps).transpose(1, 0, 2)
    home_logs = jnp.pad(
        home_logs, ((0, 0), (0, 8 - slot_count), (0, 0)), constant_values=mask_fill
    )
    own_weight = own_slots(hit_weight).reshape(pieces, 1, tgt_steps)
    own_weight = jnp.broadcast_to(own_weight, (pieces, 8, tgt_steps))
    grad_three = home_pass(home_logs, own_weight, target_rows, homes, sends)
    back_blocks, in_back, out_back = blocks, in_full, out_full
    grad_res_three, gain_three, shift_three = norm_backward(
        grad_three, normed_three, root_three, norms[4]
    )
    grad_ffn = grad_res_three.astype(jnp.bfloat16)
    grad_out_w = contract_rows(act_low, grad_ffn)
    grad_act = lax.optimization_barrier(contract_cols(grad_ffn, out_back))
    grad_pre = (grad_act * slope.astype(jnp.float32)).astype(jnp.bfloat16)
    grad_in_w = contract_rows(grad_pre, two_low)
    grad_bias = jnp.sum(grad_pre.astype(jnp.float32), axis=0)
    grad_two = grad_res_three + product(grad_pre, in_back)
    grad_res_two, gain_two, shift_two = norm_backward(grad_two, normed_two, root_two, norms[2])
    grad_cross = grad_res_two.astype(jnp.bfloat16)
    grad_w7 = contract_rows(cross_out, grad_cross)
    grad_cross_out = contract_cols(grad_cross, back_blocks[7]).astype(jnp.bfloat16)
    cq_grad, ck_grad, cv_grad = attend(
        False, mem_lengths, cross_queries, cross_keys, cross_values, cross_lse, grad_cross_out
    )
    grad_w4 = contract_rows(one_low, cq_grad) * scaling
    grad_w5 = contract_rows(memory_rows, ck_grad)
    grad_w6 = contract_rows(memory_rows, cv_grad)
    grad_memory = (
        contract_cols(ck_grad, back_blocks[5]) + contract_cols(cv_grad, back_blocks[6])
    ).astype(jnp.bfloat16)
    grad_memory = leave_slots(
        grad_memory.reshape(slots_here, questions, mem_steps, model_width)
    )
    table_sum = [over_first(sides, cq_grad) for sides in table_grads]
    earlier = grad_memory[1:] + [send for sides in table_sum for send in second_sends(sides)]
    grad_one = grad_res_two + contract_cols(cq_grad, back_blocks[4]) * scaling
    grad_res_one, gain_one, shift_one = norm_backward(grad_one, normed_one, root_one, norms[0])
    grad_attn_out = grad_res_one.astype(jnp.bfloat16)
    grad_w3 = contract_rows(self_out, grad_attn_out)
    grad_self_out = contract_cols(grad_attn_out, back_blocks[3]).astype(jnp.bfloat16)
    sq_grad, sk_grad, sv_grad = attend(
        True, tgt_lengths, queries, key_rows, value_rows, self_lse, grad_self_out, earlier
    )
    grad_w0 = contract_rows(inputs, sq_grad) * scaling
    grad_w1 = contract_rows(inputs, sk_grad)
    grad_w2 = contract_rows(inputs, sv_grad)
    grad_inputs = (
        grad_res_one
        + contract_cols(sq_grad, back_blocks[0]) * scaling
        + contract_cols(sk_grad, back_blocks[1])
        + contract_cols(sv_grad, back_blocks[2])
    )
    grad_inputs = grad_inputs.astype(jnp.bfloat16).reshape(
        slots_here, questions, tgt_steps, model_width
    )
    grad_attn = jnp.concatenate(
        [
            grad.astype(jnp.bfloat16)
            for grad in (grad_w0, grad_w1, grad_w2, grad_w3, grad_w4, grad_w5, grad_w6, grad_w7)
        ],
        axis=0,
    )
    small = jnp.concatenate(
        [
            jnp.stack([gain_one, shift_one, gain_two, shift_two, gain_three, shift_three], axis=0),
            grad_bias.reshape(-1, model_width),
            jnp.zeros((6, model_width), jnp.float32)
            .at[0, :3]
            .set(jnp.stack([objective_part, jnp.sum(lengths[0]), jnp.sum(entropy_q[0])])),
        ],
        axis=0,
    )
    table_sum = [over_second(sides, grad_inputs) for sides in table_sum]
    table_sum = [jnp.stack(sides, axis=2) for sides in table_sum]
    table_sum = jnp.concatenate(table_sum, axis=1).reshape(cores, share, -1)
    table_send = pick(table_sum, 1 - core, 0)
    grad_attn, grad_in_w, grad_out_w, grad_inputs, small = scatter_outputs(
        grad_attn,
        grad_in_w.astype(jnp.bfloat16),
        grad_out_w.astype(jnp.bfloat16),
        grad_inputs,
        after(small, table_send),
    )
    grad_memory = to_positions(grad_memory, small)
    kept = pick(table_sum, core, 0)
    given = after(shifted(table_send, "core", 1), small)
    grad_embed = jnp.stack([kept, given])
    grad_embed = jnp.where(core == 0, grad_embed, grad_embed[::-1])
    grad_embed = grad_embed.reshape(vocab_here, -1).astype(jnp.float32)
    grad_norms = small[:6]
    scalars = small[-6]
    loss = scalars[0] / scalars[1]
    entropy = scalars[2] / (questions * n_pb * slot_count)
    grad_bias = small[6:-6].reshape(-1)
    own_bias = grad_bias.shape[0] // (lax.axis_size("pb") * slot_count)
    grad_bias = lax.dynamic_slice_in_dim(
        grad_bias,
        (lax.axis_index("pb") * slot_count + lax.axis_index("slot")) * own_bias,
        own_bias,
    )
    return (
        loss,
        entropy,
        grad_inputs,
        grad_memory,
        grad_attn,
        grad_in_w,
        grad_out_w,
        grad_bias,
        grad_norms,
        grad_embed,
    )


def solution(mesh):
    placed = (
        P(None, "pb", "slot", None),
        P(None, "pb", "slot", None),
        P("pb", None),
        P("pb"),
        P("pb", None),
        P("pb"),
        P("slot", "pb"),
        P(("pb", "slot"), None),
        P(("pb", "slot"), None),
        P(("pb", "slot"), None),
        P(),
        P(),
        P("slot", None),
    )
    return jax.shard_map(
        body,
        mesh=mesh,
        in_specs=placed,
        out_specs=(
            P(),
            P(),
            P(None, "pb", "slot", None),
            P(None, "pb", "slot", None),
            P(("pb", "slot"), None),
            P(("pb", "slot"), None),
            P(("pb", "slot"), None),
            P(("pb", "slot")),
            P(),
            P("slot", "pb"),
        ),
        check_vma=False,
    )
```

```python
import functools

import jax
import jax.numpy as jnp
from jax import lax
from jax.experimental import pallas as pl
from jax.experimental.pallas import tpu as pltpu
from jax.sharding import PartitionSpec as P

HEADS = 16


eps_norm = 1e-05
entropy_weight = 0.25
mask_fill = -1e30
root_half = 0.7071067811865476
inv_root_tau = 0.3989422804014327


def grid_of(n_pb):
    cores = 2 if n_pb % 2 == 0 else 1
    chips = n_pb // cores
    wide = max(d for d in range(1, chips + 1) if chips % d == 0 and d * d <= chips)
    return chips // wide, wide, cores


def shifted(value, axis, step):
    if axis == "slot":
        size = lax.axis_size("slot")
        return lax.ppermute(value, "slot", [(i, (i + step) % size) for i in range(size)])
    n_pb = lax.axis_size("pb")
    tall, wide, cores = grid_of(n_pb)
    pairs = []
    for i in range(n_pb):
        y, x, c = i // (wide * cores), i // cores % wide, i % cores
        if axis == "y":
            y = (y + step) % tall
        elif axis == "x":
            x = (x + step) % wide
        else:
            c = (c + step) % cores
        pairs.append((i, (y * wide + x) * cores + c))
    return lax.ppermute(value, "pb", pairs)


def place_of(axis):
    if axis == "slot":
        return lax.axis_index("slot"), lax.axis_size("slot")
    tall, wide, cores = grid_of(lax.axis_size("pb"))
    i = lax.axis_index("pb")
    if axis == "y":
        return i // (wide * cores), tall
    if axis == "x":
        return i // cores % wide, wide
    return i % cores, cores


def after(value, *tokens):
    for token in tokens:
        first = token[(0,) * token.ndim].astype(jnp.float32)
        value = jnp.where(first == first, value, jnp.zeros_like(value))
    return value


def pick(value, index, dim):
    return lax.dynamic_index_in_dim(value, index, dim, keepdims=False)


def ring_gather(value, axis):
    me, size = place_of(axis)
    found = [(me, value)]
    for step in range(1, size):
        value = shifted(value, axis, 1)
        found.append(((me - step) % size, value))
    return found


def ring_scatter(value, axis, dim, late=None):
    me, size = place_of(axis)
    total = pick(value, (me - 1) % size, dim).astype(jnp.bfloat16)
    for step in range(1, size):
        part = pick(value, (me - 1 - step) % size, dim)
        total = shifted(total, axis, 1)
        if late is not None:
            total = after(total, late)
        total = total.astype(jnp.float32) + part.astype(jnp.float32)
        if step < size - 1:
            total = total.astype(jnp.bfloat16)
    return total


def ring_first(value, axis, dim):
    me, size = place_of(axis)
    return pick(value, (me - 1) % size, dim).astype(jnp.bfloat16)


def gather_all(shard):
    tall, wide, cores = grid_of(lax.axis_size("pb"))
    rows, width = shard.shape
    slots = lax.axis_size("slot")
    column = jnp.zeros((slots, rows, width), shard.dtype)
    for index, block in ring_gather(shard, "slot"):
        column = lax.dynamic_update_index_in_dim(column, block, index, 0)
    column = column.reshape(slots * rows, width)
    half = slots * rows // 2
    core, _ = place_of("core")
    whole = jnp.zeros((tall * wide, cores, 2, half, width), shard.dtype)
    for side, (first, second) in enumerate((("x", "y"), ("y", "x"))):
        part = column[side * half : (side + 1) * half]
        for at_first, block in ring_gather(part, first):
            for at_second, block in ring_gather(block, second):
                x, y = (at_first, at_second) if first == "x" else (at_second, at_first)
                for at_core, block in ring_gather(block, "core"):
                    whole = lax.dynamic_update_slice(
                        whole, block[None, None, None], (y * wide + x, at_core, side, 0, 0)
                    )
    return whole.reshape(tall * wide * cores, slots * rows, width)


def scatter_pb(value, lates=(None, None, None)):
    tall, wide, cores = grid_of(lax.axis_size("pb"))
    rest = value.shape[1:]
    value = value.reshape((tall * wide, cores) + rest)
    value = ring_scatter(value, "core", 1, lates[0]).astype(jnp.bfloat16)
    value = value.reshape((tall, wide) + rest)
    half = rest[0] // 2
    first = ring_scatter(value[:, :, :half], "x", 1, lates[1])
    second = ring_scatter(value[:, :, half:], "y", 0, lates[1])
    first = ring_scatter(first.astype(jnp.bfloat16), "y", 0, lates[2])
    second = ring_scatter(second.astype(jnp.bfloat16), "x", 0, lates[2])
    return jnp.concatenate([first, second], axis=0)


def scatter_all(value):
    n_pb, slots = lax.axis_size("pb"), lax.axis_size("slot")
    rows = value.shape[0] // (n_pb * slots)
    value = value.reshape((n_pb, slots, rows) + value.shape[1:])
    column = scatter_pb(value)
    return ring_scatter(column.astype(jnp.bfloat16), "slot", 0)


def scatter_slot(value, late):
    me, size = place_of("slot")
    parts = [
        after(shifted(pick(value, (me + step) % size, 0), "slot", step), late)
        for step in range(1, size)
    ]
    return sum([part.astype(jnp.float32) for part in parts], pick(value, me, 0).astype(jnp.float32))


def sum_all(value, axes):
    for axis in axes:
        me, size = place_of(axis)
        parts = [value] + [shifted(value, axis, step) for step in range(1, size)]
        placed = jnp.stack(parts)
        value = jnp.sum(placed[(me - jnp.arange(size)) % size], axis=0)
    return value


def to_slots(value):
    me, size = place_of("slot")
    every, questions, steps, width = value.shape
    chunks = value.reshape(every // size, size, questions, steps, width)
    result = jnp.zeros((every // size, questions, size, steps, width), value.dtype)
    for step in range(size):
        block = pick(chunks, (me + step) % size, 1)
        if step:
            block = shifted(block, "slot", step)
        result = lax.dynamic_update_index_in_dim(result, block, (me - step) % size, 2)
    return result.reshape(every // size, questions, size * steps, width)


def leave_slots(value):
    me, size = place_of("slot")
    own, questions, steps, width = value.shape
    chunks = value.reshape(own, questions, size, steps // size, width)
    return [pick(chunks, (me + step) % size, 2) for step in range(size)]


def to_positions(blocks, late=None):
    me, size = place_of("slot")
    own, questions, steps, width = blocks[0].shape
    result = jnp.zeros((own, size, questions, steps, width), blocks[0].dtype)
    for step, block in enumerate(blocks):
        if step:
            block = shifted(block, "slot", step)
            block = block if late is None else after(block, late)
        result = lax.dynamic_update_index_in_dim(result, block, (me - step) % size, 1)
    return result.reshape(size * own, questions, steps, width)


def product(left, right):
    return jnp.dot(left, right, preferred_element_type=jnp.float32)


def contract_rows(left, right):
    return lax.dot_general(
        left, right, (((0,), (0,)), ((), ())), preferred_element_type=jnp.float32
    )


def contract_cols(left, right):
    return lax.dot_general(
        left, right, (((1,), (1,)), ((), ())), preferred_element_type=jnp.float32
    )


def norm_forward(resid, gain, shift):
    row_mean = jnp.mean(resid, axis=-1, keepdims=True)
    centered = resid - row_mean
    inv_root = lax.rsqrt(jnp.mean(centered * centered, axis=-1, keepdims=True) + eps_norm)
    normed = centered * inv_root
    return (normed * gain + shift, normed, inv_root)


def norm_backward(grad_out, normed, inv_root, gain):
    scaled = grad_out * gain
    grad_in = inv_root * (
        scaled
        - jnp.mean(scaled, axis=-1, keepdims=True)
        - normed * jnp.mean(scaled * normed, axis=-1, keepdims=True)
    )
    return (grad_in, jnp.sum(grad_out * normed, axis=0), jnp.sum(grad_out, axis=0))


def two_heads(value):
    left = lax.broadcasted_iota(jnp.int32, value.shape, 1) < value.shape[1] // 2
    none = jnp.zeros_like(value)
    return jnp.concatenate([jnp.where(left, value, none), jnp.where(left, none, value)], axis=0)


def one_pair(value):
    rows = value.shape[0] // 2
    left = lax.broadcasted_iota(jnp.int32, (rows, value.shape[1]), 1) < value.shape[1] // 2
    return jnp.where(left, value[:rows], value[rows:])


def pair_scores(info, causal, queries, key_rows):
    scores = lax.dot_general(
        queries, key_rows, (((1,), (1,)), ((), ())), preferred_element_type=jnp.float32
    )
    column = lax.broadcasted_iota(jnp.int32, scores.shape, 1)
    if causal:
        row = lax.broadcasted_iota(jnp.int32, scores.shape, 0)
        allowed = column <= jnp.where(row < scores.shape[0] // 2, row, row - scores.shape[0] // 2)
    else:
        allowed = column < info[pl.program_id(0)]
    return jnp.where(allowed, scores, mask_fill)


def attend_kernel(causal, info, queries, keys, values, out, logs):
    steps, width = queries.shape
    lane = lax.broadcasted_iota(jnp.int32, (steps, 128), 1)
    kept = jnp.zeros((steps, 128), jnp.float32)

    def first(pair):
        here = slice(pair * 128, (pair + 1) * 128)
        return pair_scores(info, causal, two_heads(queries[:, here]), keys[:, here])

    following = first(0)
    for pair in range(width // 128):
        here = slice(pair * 128, (pair + 1) * 128)
        scores = following
        if pair + 1 < width // 128:
            following = first(pair + 1)
        row_max = jnp.max(scores, axis=1, keepdims=True)
        expos = jnp.exp(scores - row_max)
        row_sum = jnp.sum(expos, axis=1, keepdims=True)
        probs = (expos * (1.0 / row_sum)).astype(jnp.bfloat16)
        out[:, here] = one_pair(
            jnp.dot(probs, values[:, here], preferred_element_type=jnp.float32)
        ).astype(jnp.bfloat16)
        log = row_max + jnp.log(row_sum)
        kept = jnp.where(lane == 2 * pair, log[:steps], kept)
        kept = jnp.where(lane == 2 * pair + 1, log[steps:], kept)
    logs[...] = kept


def attend_back_kernel(causal, info, queries, keys, values, logs, grads, *refs):
    d_queries, d_keys, d_values = refs[-3:]
    steps, width = queries.shape
    rows_first = (((0,), (0,)), ((), ()))

    def first(pair):
        here = slice(pair * 128, (pair + 1) * 128)
        both = two_heads(queries[:, here])
        both_grads = two_heads(grads[:, here])
        scores = pair_scores(info, causal, both, keys[:, here])
        d_probs = lax.dot_general(
            both_grads, values[:, here], (((1,), (1,)), ((), ())), preferred_element_type=jnp.float32
        )
        return both, both_grads, scores, d_probs

    following = first(0)
    for pair in range(width // 128):
        here = slice(pair * 128, (pair + 1) * 128)
        both, both_grads, scores, d_probs = following
        if pair + 1 < width // 128:
            following = first(pair + 1)
        log = jnp.concatenate(
            [logs[:, 2 * pair : 2 * pair + 1], logs[:, 2 * pair + 1 : 2 * pair + 2]], axis=0
        )
        probs = jnp.exp(scores - log)
        d_values[:, here] = lax.dot_general(
            probs.astype(jnp.bfloat16), both_grads, rows_first, preferred_element_type=jnp.float32
        ).astype(jnp.bfloat16)
        delta = jnp.sum(d_probs * probs, axis=1, keepdims=True)
        d_scores = (probs * (d_probs - delta)).astype(jnp.bfloat16)
        d_queries[:, here] = one_pair(
            jnp.dot(d_scores, keys[:, here], preferred_element_type=jnp.float32)
        ).astype(jnp.bfloat16)
        d_keys[:, here] = lax.dot_general(
            d_scores, both, rows_first, preferred_element_type=jnp.float32
        ).astype(jnp.bfloat16)


def attend(causal, lengths, queries, keys, values, logs=None, grads=None, earlier=()):
    count = lengths.shape[0]
    width = queries.shape[1]
    steps, spans = queries.shape[0] // count, keys.shape[0] // count
    short = pl.BlockSpec((steps, width), lambda i, s: (i, 0))
    long = pl.BlockSpec((spans, width), lambda i, s: (i, 0))
    thin = pl.BlockSpec((steps, 128), lambda i, s: (i, 0))
    like = lambda value: jax.ShapeDtypeStruct(value.shape, jnp.bfloat16)
    if grads is None:
        kernel, operands = attend_kernel, (queries, keys, values)
        in_specs, out_specs = [short, long, long], [short, thin]
        out_shape = [like(queries), jax.ShapeDtypeStruct((queries.shape[0], 128), jnp.float32)]
    else:
        kernel, operands = attend_back_kernel, (queries, keys, values, logs, grads, *earlier)
        in_specs, out_specs = [short, long, long, thin, short], [short, long, long]
        in_specs += [pl.BlockSpec(memory_space=pl.ANY)] * len(earlier)
        out_shape = [like(queries), like(keys), like(values)]
    flops = (4 if grads is None else 10) * queries.shape[0] * spans * width
    return pl.pallas_call(
        functools.partial(kernel, causal),
        grid_spec=pltpu.PrefetchScalarGridSpec(
            num_scalar_prefetch=1, grid=(count,), in_specs=in_specs, out_specs=out_specs
        ),
        out_shape=out_shape,
        compiler_params=pltpu.CompilerParams(vmem_limit_bytes=48 << 20),
        cost_estimate=pl.CostEstimate(
            flops=4 * flops, bytes_accessed=8 * keys.shape[0] * width, transcendentals=0
        ),
        name=("self" if causal else "cross") + ("_attend" if grads is None else "_attend_back"),
    )(lengths, *operands)


def gelu_parts(value):
    place = 1.0 / (1.0 + 0.3275911 * root_half * jnp.abs(value))
    bell = jnp.exp(-0.5 * value * value)
    series = 1.061405429
    for factor in (-1.453152027, 1.421413741, -0.284496736, 0.254829592):
        series = series * place + factor
    tail = 0.5 * series * place * bell
    share = jnp.where(value > 0.0, 1.0 - tail, tail)
    return value * share, share + value * (inv_root_tau * bell)


SMALL = pl.CostEstimate(flops=1 << 20, bytes_accessed=1 << 16, transcendentals=0)
PIECE = 128
CHUNK = 256


def vocab_tile(share):
    return max(d for d in range(16, 901, 16) if share % d == 0)


def columns(block):
    return jnp.concatenate([block] * 16, axis=0).T


def each_count(live, chunks, run):
    for taken in range(1, chunks + 1):
        above = live > (taken - 1) * CHUNK
        upto = live <= taken * CHUNK if taken < chunks else live >= 0

        @pl.when(jnp.logical_and(above, upto))
        def _():
            run(taken)


def piece_places(info, step, count):
    base = 1 + step * (count + 1)
    return [pl.multiple_of(info[base + i], 16) for i in range(count)], info[base + count]


def rows_kernel(step, info, ids, own, mate, table, *refs):
    expo, packed, tops, own_sums, mate_sums, own_logs, mate_logs, acc, top, total, marks = refs[-11:]
    expo, packed, tops = expo.at[0], packed.at[0], tops.at[0]
    tile = pl.program_id(0)
    wide = table.shape[0]
    pieces = own.shape[0] // PIECE
    count = 2 * pieces
    places, live = piece_places(info, step, count)

    @pl.when(tile == 0)
    def _():
        acc[...] = jnp.zeros_like(acc)
        top[...] = jnp.full_like(top, mask_fill)
        total[...] = jnp.zeros_like(total)
        tops[...] = jnp.zeros_like(tops)
        packed[...] = jnp.zeros_like(packed)
        marks[...] = jnp.full_like(marks, -1.0)
        for piece in range(count):
            side = own if piece < pieces else mate
            low = piece % pieces * PIECE
            packed[pl.ds(places[piece], PIECE), :] = side[low : low + PIECE, :]
            marks[pl.ds(places[piece], PIECE), :] = columns(ids[piece])

    lane = lax.broadcasted_iota(jnp.int32, (CHUNK, 128), 1)
    column = lax.broadcasted_iota(jnp.int32, (CHUNK, wide), 1)

    def scores(chunk):
        return lax.dot_general(
            packed[chunk * CHUNK : (chunk + 1) * CHUNK, :],
            table[...],
            (((1,), (1,)), ((), ())),
            preferred_element_type=jnp.float32,
        )

    def soften(chunk, logits):
        here = slice(chunk * CHUNK, (chunk + 1) * CHUNK)
        target = marks[here, 0:1].astype(jnp.int32) - tile * wide
        logits = jnp.where(column == target, mask_fill, logits)
        before = top[here, 0:1]
        now = jnp.maximum(before, jnp.max(logits, axis=1, keepdims=True))
        fade = jnp.exp(before - now)
        grown = jnp.exp(logits - now)
        total[here, :] = jnp.broadcast_to(
            total[here, 0:1] * fade + jnp.sum(grown, axis=1, keepdims=True), (CHUNK, 128)
        )
        top[here, :] = jnp.broadcast_to(now, (CHUNK, 128))
        tops[here, :] = jnp.where(lane == tile, now, tops[here, :])
        grown = grown.astype(jnp.bfloat16)
        expo[0, here, :] = grown
        return here, grown, fade

    def gather(here, grown, fade):
        acc[here, :] = acc[here, :] * fade + jnp.dot(
            grown, table[...], preferred_element_type=jnp.float32
        )

    def run(taken):
        logits = [scores(0)]
        late = None
        for chunk in range(taken):
            if chunk + 1 < taken:
                logits.append(scores(chunk + 1))
            ready = soften(chunk, logits[chunk])
            if late is not None:
                gather(*late)
            late = ready
        gather(*late)

    each_count(live, count * PIECE // CHUNK, run)

    @pl.when(tile == pl.num_programs(0) - 1)
    def _():
        for piece in range(count):
            here = pl.ds(places[piece], PIECE)
            mass = total[here, :]
            share = jnp.where(mass > 0.0, 1.0 / jnp.maximum(mass, 1e-30), 0.0)[:, 0:1]
            sums, logs = (own_sums, own_logs) if piece < pieces else (mate_sums, mate_logs)
            low = piece % pieces * PIECE
            sums[low : low + PIECE, :] = (acc[here, :] * share).astype(jnp.bfloat16)
            logs[piece % pieces] = (top[here, :] + jnp.log(jnp.maximum(mass, 1e-30))).T[0:8]


def rows_pass(step, steps, info, ids, own, mate, table, cores, kept, earlier):
    group, width = own.shape
    share = table.shape[0] // cores
    wide = vocab_tile(share)
    tiles = share // wide
    rows = 2 * group
    count = rows // PIECE
    room = rows + PIECE
    whole = lambda i, s: (0, 0)
    cube = lambda i, s: (0, 0, 0)
    return pl.pallas_call(
        functools.partial(rows_kernel, step),
        grid_spec=pltpu.PrefetchScalarGridSpec(
            num_scalar_prefetch=1,
            grid=(tiles,),
            in_specs=[
                pl.BlockSpec((count, 8, 128), lambda i, s: (step, 0, 0)),
                pl.BlockSpec((group, width), whole),
                pl.BlockSpec((group, width), whole),
                pl.BlockSpec((wide, width), lambda i, s: (s[0] * tiles + i, 0)),
            ]
            + [pl.BlockSpec(memory_space=pl.ANY)] * (len(kept) + len(earlier)),
            out_specs=[
                pl.BlockSpec((1, 1, rows, wide), lambda i, s: (step, i, 0, 0)),
                pl.BlockSpec((1, room, width), lambda i, s: (step, 0, 0)),
                pl.BlockSpec((1, room, 128), lambda i, s: (step, 0, 0)),
                pl.BlockSpec((group, width), whole),
                pl.BlockSpec((group, width), whole),
                pl.BlockSpec((count // 2, 8, 128), cube),
                pl.BlockSpec((count // 2, 8, 128), cube),
            ],
            scratch_shapes=[
                pltpu.VMEM((room, width), jnp.float32),
                pltpu.VMEM((room, 128), jnp.float32),
                pltpu.VMEM((room, 128), jnp.float32),
                pltpu.VMEM((room, 128), jnp.float32),
            ],
        ),
        out_shape=[
            jax.ShapeDtypeStruct((steps, tiles, rows, wide), jnp.bfloat16),
            jax.ShapeDtypeStruct((steps, room, width), jnp.bfloat16),
            jax.ShapeDtypeStruct((steps, room, 128), jnp.float32),
            jax.ShapeDtypeStruct((group, width), jnp.bfloat16),
            jax.ShapeDtypeStruct((group, width), jnp.bfloat16),
            jax.ShapeDtypeStruct((count // 2, 8, 128), jnp.float32),
            jax.ShapeDtypeStruct((count // 2, 8, 128), jnp.float32),
        ],
        input_output_aliases={5 + place: place for place in range(len(kept))},
        compiler_params=pltpu.CompilerParams(vmem_limit_bytes=60 << 20),
        cost_estimate=SMALL,
        name=f"rows_pass_{step}",
    )(info, ids, own, mate, table, *kept, *earlier)


def join_kernel(count, *refs):
    owns, others, own_logs, other_logs, outs = (
        refs[place * count : (place + 1) * count] for place in range(5)
    )
    for own, other, own_log, other_log, out in zip(owns, others, own_logs, other_logs, outs):
        for piece in range(own_log.shape[0]):
            here = slice(piece * PIECE, (piece + 1) * PIECE)
            log = jnp.logaddexp(own_log[piece], other_log[piece])
            left = columns(jnp.exp(own_log[piece] - log))[:, 0:1]
            right = columns(jnp.exp(other_log[piece] - log))[:, 0:1]
            out[here, :] = (
                own[here, :].astype(jnp.float32) * left + other[here, :].astype(jnp.float32) * right
            ).astype(jnp.bfloat16)


def join_pass(owns, others, own_logs, other_logs):
    count = len(owns)
    rows, width = owns[0].shape
    flat = pl.BlockSpec((CHUNK, width), lambda i: (i, 0))
    cube = pl.BlockSpec((CHUNK // PIECE, 8, 128), lambda i: (i, 0, 0))
    return pl.pallas_call(
        functools.partial(join_kernel, count),
        grid=(rows // CHUNK,),
        in_specs=[flat] * (2 * count) + [cube] * (2 * count),
        out_specs=[flat] * count,
        out_shape=[jax.ShapeDtypeStruct((rows, width), jnp.bfloat16)] * count,
        compiler_params=pltpu.CompilerParams(vmem_limit_bytes=48 << 20),
        cost_estimate=SMALL,
        name="join_pass",
    )(*owns, *others, *own_logs, *other_logs)


def lay_kernel(count, info, *refs):
    out = refs[-1]
    step = (info[0] + count - pl.program_id(0)) % count
    for place in range(count):

        @pl.when(step == place)
        def _():
            out[:, 0] = refs[place][...]


def lay_blocks(blocks, place, earlier):
    count = len(blocks)
    own, questions, steps, width = blocks[0].shape
    whole = lambda i, s: (0, 0, 0, 0)
    return pl.pallas_call(
        functools.partial(lay_kernel, count),
        grid_spec=pltpu.PrefetchScalarGridSpec(
            num_scalar_prefetch=1,
            grid=(count,),
            in_specs=[pl.BlockSpec(blocks[0].shape, whole, pipeline_mode=pl.Buffered(1))] * count
            + [pl.BlockSpec(memory_space=pl.ANY)] * len(earlier),
            out_specs=pl.BlockSpec(
                (own, 1, questions, steps, width), lambda i, s: (0, i, 0, 0, 0)
            ),
        ),
        out_shape=jax.ShapeDtypeStruct((own, count, questions, steps, width), blocks[0].dtype),
        compiler_params=pltpu.CompilerParams(vmem_limit_bytes=48 << 20),
        cost_estimate=SMALL,
        name="lay_blocks",
    )(place.reshape(1).astype(jnp.int32), *blocks, *earlier)


def home_kernel(count, logs, weight, targets, *refs):
    parts, out = refs[:count], refs[-1]
    log = logs[0]
    share = jnp.exp(log - jnp.max(log, axis=0, keepdims=True))
    share = columns(share / jnp.sum(share, axis=0, keepdims=True))
    mean = parts[0][...].astype(jnp.float32) * share[:, 0:1]
    for place in range(1, count):
        mean = mean + parts[place][...].astype(jnp.float32) * share[:, place : place + 1]
    out[...] = columns(weight[0])[:, 0:1] * (targets[0] - mean)


def home_pass(logs, weight, targets, parts, earlier):
    rows, width = parts[0].shape
    questions = targets.shape[0]
    flat = pl.BlockSpec((PIECE, width), lambda i: (i, 0))
    cube = pl.BlockSpec((1, 8, 128), lambda i: (i, 0, 0))
    return pl.pallas_call(
        functools.partial(home_kernel, len(parts)),
        grid=(rows // PIECE,),
        in_specs=[cube, cube, pl.BlockSpec((1, PIECE, width), lambda i: (i % questions, 0, 0))]
        + [flat] * len(parts)
        + [pl.BlockSpec(memory_space=pl.ANY)] * len(earlier),
        out_specs=flat,
        out_shape=jax.ShapeDtypeStruct((rows, width), jnp.float32),
        cost_estimate=SMALL,
        name="home_pass",
    )(logs, weight, targets, *parts, *earlier)


def table_kernel(first, info, facts, tops, rows, expos, *refs):
    outs, acc, scales = refs[-4:-2], refs[-2], refs[-1]
    tile = pl.program_id(0) + first
    sources, _, both, wide = expos.shape
    count = both // PIECE

    @pl.when(pl.program_id(0) == 0)
    def _():
        def ready(source, _):
            places, _ = piece_places(info, source, count)
            scales[source] = jnp.zeros(scales.shape[1:], jnp.float32)
            for piece in range(count):
                scales[source, pl.ds(places[piece], PIECE), :] = columns(facts[source * count + piece])
            raw = scales[source]
            lane = lax.broadcasted_iota(jnp.int32, raw.shape, 1)
            weight = raw[:, 0:1]
            spread = jnp.where(weight == 0.0, 0.0, -weight * jnp.exp(tops[source] - raw[:, 1:2]))
            spread = jnp.where(lane == 127, raw[:, 2:3], spread)
            scales[source] = jnp.where(lane == 126, raw[:, 3:4], spread)
            return 0

        lax.fori_loop(0, sources, ready, 0)

    acc[...] = jnp.zeros_like(acc)

    def add(source, begin, size):
        here = pl.ds(pl.multiple_of(begin, CHUNK), size)
        scale = scales[source, here, :]
        lane = lax.broadcasted_iota(jnp.int32, (size, 128), 1)
        column = lax.broadcasted_iota(jnp.int32, (size, wide), 1)
        spread = jnp.sum(jnp.where(lane == tile, scale, 0.0), axis=1, keepdims=True)
        target = scale[:, 126:127].astype(jnp.int32) - tile * wide
        grad = expos[source, 0, here, :].astype(jnp.float32) * spread
        grad = jnp.where(column == target, scale[:, 127:128], grad).astype(jnp.bfloat16)
        acc[...] += lax.dot_general(
            grad,
            rows[source, here, :],
            (((0,), (0,)), ((), ())),
            preferred_element_type=jnp.float32,
        )

    def add_source(source, _):
        live = info[1 + source * (count + 1) + count]
        chunks = (live + CHUNK - 1) // CHUNK

        @pl.when(chunks == 4)
        def _():
            add(source, 0, 4 * CHUNK)

        @pl.when(jnp.logical_or(chunks == 2, chunks == 3))
        def _():
            add(source, 0, 2 * CHUNK)

        @pl.when(chunks % 2 == 1)
        def _():
            add(source, (chunks - 1) * CHUNK, CHUNK)

        return 0

    lax.fori_loop(0, sources, add_source, 0)
    half = wide // 2
    for side, out in enumerate(outs):
        for place in range(out.shape[0]):
            size = out.shape[3]
            out[place, 0] = acc[
                side * half : (side + 1) * half, place * size : (place + 1) * size
            ].astype(jnp.bfloat16)


def table_pass(info, facts, tops, rows, expos, first, tiles, n_pb, earlier):
    sources, _, both, wide = expos.shape
    _, room, width = rows.shape
    own = width // n_pb
    once = pl.Buffered(1)
    cube = lambda i, s: (0, 0, 0)
    return pl.pallas_call(
        functools.partial(table_kernel, first),
        grid_spec=pltpu.PrefetchScalarGridSpec(
            num_scalar_prefetch=1,
            grid=(tiles,),
            in_specs=[
                pl.BlockSpec(facts.shape, cube, pipeline_mode=once),
                pl.BlockSpec(tops.shape, cube, pipeline_mode=once),
                pl.BlockSpec(rows.shape, cube, pipeline_mode=once),
                pl.BlockSpec((sources, 1, both, wide), lambda i, s: (0, i + first, 0, 0)),
            ]
            + [pl.BlockSpec(memory_space=pl.ANY)] * len(earlier),
            out_specs=[pl.BlockSpec((n_pb, 1, wide // 2, own), lambda i, s: (0, i, 0, 0))] * 2,
            scratch_shapes=[
                pltpu.VMEM((wide, width), jnp.float32),
                pltpu.VMEM((sources, room, 128), jnp.float32),
            ],
        ),
        out_shape=[jax.ShapeDtypeStruct((n_pb, tiles, wide // 2, own), jnp.bfloat16)] * 2,
        compiler_params=pltpu.CompilerParams(vmem_limit_bytes=60 << 20),
        cost_estimate=SMALL,
        name=f"table_pass_{first}",
    )(info, facts, tops, rows, expos, *earlier)


def gather_kernel(*refs):
    mats, rows = refs[:3], refs[3:5]
    full, laid = refs[5:8], refs[8:10]
    send, recv, near = refs[10:]
    slots = full[0].shape[1]
    pb, place = lax.axis_index("pb"), lax.axis_index("slot")
    mate = pb // 2 * 2 + (pb + 1) % 2
    side_x = pb // 4 * 4 + (pb + 2) % 4
    side_y = (pb + 4) % 8
    corner = (side_x + 4) % 8
    barrier = pltpu.get_barrier_semaphore()
    partners = [(mate, place), (side_x, place), (side_y, place)]
    partners += [(pb, (place + step) % slots) for step in range(1, slots)]
    for partner in partners:
        pl.semaphore_signal(barrier, inc=1, device_id=partner, device_id_type=pl.DeviceIdType.MESH)
    pl.semaphore_wait(barrier, len(partners))

    sent, unread, stays, ready = [], {}, [], {}

    def push(source, target, device):
        copy = pltpu.make_async_remote_copy(
            src_ref=source,
            dst_ref=target,
            send_sem=send.at[len(sent)],
            recv_sem=recv.at[len(sent)],
            device_id=device,
            device_id_type=pl.DeviceIdType.MESH,
        )
        copy.start()
        unread[len(sent)] = copy
        sent.append(copy)
        return len(sent) - 1

    def read(number):
        unread.pop(number).wait_recv()

    def put(source, target):
        copy = pltpu.make_async_copy(source, target, near.at[len(stays)])
        copy.start()
        stays.append(copy)

    def move_rows(step):
        goal = (place + step) % slots
        for source, target in zip(rows, laid):
            block = source.at[:, goal]
            spot = target.at[:, :, place]
            if step:
                push(block, spot, (pb, goal))
            else:
                put(block, spot)

    def part(mat, at_pb, origin, half):
        size = full[mat].shape[2] // 2
        return full[mat].at[at_pb, origin, pl.ds(half * size, size)]

    def own_moves(step, mat, origin, source):
        size = full[mat].shape[2] // 2
        first, second = (source.at[pl.ds(half * size, size)] for half in range(2))
        first_at, second_at = (part(mat, pb, origin, half) for half in range(2))
        ready[step, mat] = [
            push(first, first_at, (side_x, place)),
            push(second, second_at, (side_y, place)),
            push(first, first_at, (side_y, place)),
            push(second, second_at, (side_x, place)),
        ]
        push(source, full[mat].at[pb, origin], (mate, place))

    def onward(step, mat, origin):
        over_x, over_y, _, _ = ready[step, mat]
        read(over_x)
        block = part(mat, side_x, origin, 0)
        ready[step, mat].append(push(block, block, (side_y, place)))
        push(block, block, (mate, place))
        read(over_y)
        block = part(mat, side_y, origin, 1)
        ready[step, mat].append(push(block, block, (side_x, place)))
        push(block, block, (mate, place))

    def finish(step, mat, origin):
        _, _, over_y, over_x, first, second = ready[step, mat]
        for number, at_pb, half in (
            (over_y, side_y, 0),
            (over_x, side_x, 1),
            (first, corner, 0),
            (second, corner, 1),
        ):
            read(number)
            block = part(mat, at_pb, origin, half)
            push(block, block, (mate, place))

    count = len(mats)
    following = (pb, (place + 1) % slots)
    ring = [push(mats[mat], full[mat].at[pb, place], following) for mat in range(count)]
    for mat in range(count):
        own_moves(0, mat, place, mats[mat])
        put(mats[mat], full[mat].at[pb, place])
    move_rows(1)
    move_rows(0)
    for step in range(1, slots + 1):
        origin = (place + slots - step) % slots
        before = (place + slots - step + 1) % slots
        if step < slots:
            for mat in range(count):
                read(ring[mat])
                block = full[mat].at[pb, origin]
                if step < slots - 1:
                    ring[mat] = push(block, block, following)
                own_moves(step, mat, origin, block)
        if step == 1:
            move_rows(slots - 1)
        if step == 2:
            for other in range(2, slots - 1):
                move_rows(other)
        for mat in range(count):
            onward(step - 1, mat, before)
        for mat in range(count):
            finish(step - 1, mat, before)
    for number in sorted(unread):
        read(number)
    for copy in sent:
        copy.wait_send()
    for copy in stays:
        copy.wait()


def gather_inputs(x_in, memory, attn_w, ffn_in, ffn_out):
    n_pb, slots = lax.axis_size("pb"), lax.axis_size("slot")
    mats, rows = (attn_w, ffn_in, ffn_out), (x_in, memory)
    width = attn_w.shape[1]
    rows = [row.reshape((-1, slots) + row.shape[1:]) for row in rows]
    if (n_pb, slots) != (8, 4):
        return (
            to_slots(x_in),
            to_slots(memory),
            *(gather_all(mat).reshape(-1, width) for mat in mats),
        )
    shapes = [jax.ShapeDtypeStruct((n_pb, slots) + mat.shape, mat.dtype) for mat in mats]
    for row in rows:
        own, _, questions, steps, _ = row.shape
        shapes.append(jax.ShapeDtypeStruct((own, questions, slots, steps, width), row.dtype))
    copies = 13 * len(mats) * slots + (slots - 1) * (len(mats) + len(rows))
    anywhere = pl.BlockSpec(memory_space=pl.ANY)
    *full, x_here, mem_here = pl.pallas_call(
        gather_kernel,
        in_specs=[anywhere] * 5,
        out_specs=[anywhere] * 5,
        out_shape=shapes,
        scratch_shapes=[
            pltpu.SemaphoreType.DMA((copies,)),
            pltpu.SemaphoreType.DMA((copies,)),
            pltpu.SemaphoreType.DMA((len(mats) + len(rows),)),
        ],
        compiler_params=pltpu.CompilerParams(collective_id=0, has_side_effects=True),
        name="gather_inputs",
    )(*mats, *rows)
    own, questions, _, _, _ = x_here.shape
    return (
        x_here.reshape(own, questions, -1, width),
        mem_here.reshape(own, questions, -1, width),
        *(mat.reshape(-1, width) for mat in full),
    )


UNIT = 64


def scatter_kernel(*refs):
    mats, rows, few = refs[:3], refs[3], refs[4]
    outs, laid, few_out = refs[5:8], refs[8], refs[9]
    (from_core, kept, wide_x, wide_y, narrow_x, narrow_y, from_slot, few_here, few_there, few_slot) = refs[10:20]
    send, recv, near = refs[20:]
    depth = kept.shape[0]
    slots = mats[0].shape[2]
    pb, place = lax.axis_index("pb"), lax.axis_index("slot")
    core, at_x, at_y = pb % 2, pb // 2 % 2, pb // 4
    mate = (pb // 2 * 2 + (pb + 1) % 2, place)
    side_x = (pb // 4 * 4 + (pb + 2) % 4, place)
    side_y = ((pb + 4) % 8, place)
    barrier = pltpu.get_barrier_semaphore()
    partners = [mate, side_x, side_y]
    partners += [(pb, (place + step) % slots) for step in range(1, slots)]
    for partner in partners:
        pl.semaphore_signal(barrier, inc=1, device_id=partner, device_id_type=pl.DeviceIdType.MESH)
    pl.semaphore_wait(barrier, len(partners))

    sent = []

    def push(source, target, device):
        copy = pltpu.make_async_remote_copy(
            src_ref=source,
            dst_ref=target,
            send_sem=send.at[len(sent)],
            recv_sem=recv.at[len(sent)],
            device_id=device,
            device_id_type=pl.DeviceIdType.MESH,
        )
        copy.start()
        sent.append(copy)
        return copy

    stays = []

    def put(source, target):
        copy = pltpu.make_async_copy(source, target, near.at[len(stays)])
        copy.start()
        stays.append(copy)
        return copy

    units = [
        (mat, unit)
        for mat in (1, 2, 0)
        for unit in range(mats[mat].shape[3] // UNIT)
    ]

    def block(number, which):
        mat, unit = units[number]
        return mats[mat].at[:, which, :, pl.ds(unit * UNIT, UNIT)]

    half = UNIT // 2
    first, second = pl.ds(0, half), pl.ds(half, half)
    ahead = 2
    by_core = [push(block(n, 1 - core), from_core.at[n], mate) for n in range(ahead)]
    loads = {n: put(block(n, core), kept.at[n % depth]) for n in range(min(depth, len(units)))}
    by_rows = []
    for step in range(1, slots):
        goal = (place + step) % slots
        by_rows.append(push(rows.at[:, :, goal], laid.at[:, place], (pb, goal)))
    at_home = put(rows.at[:, :, place], laid.at[:, place])
    by_few = push(few, few_there.at[0], mate)

    def total(left, right):
        return (left.astype(jnp.float32) + right.astype(jnp.float32)).astype(jnp.bfloat16)

    over, across, along = {}, {}, {}

    def from_cores(n):
        slot = n % depth
        by_core[n].wait_recv()
        if n + ahead < len(units):
            by_core.append(push(block(n + ahead, 1 - core), from_core.at[n + ahead], mate))
        loads[n].wait()

        def step(i, _):
            y, x, z = i // (2 * slots), i // slots % 2, i % slots
            kept[slot, 2 * y + x, z] = total(kept[slot, 2 * y + x, z], from_core[n, 2 * y + x, z])
            return 0

        lax.fori_loop(0, 4 * slots, step, 0)
        over[n] = [
            push(kept.at[slot, 1 - at_x, :, first], wide_x.at[n, 0], side_x),
            push(kept.at[slot, 2 + 1 - at_x, :, first], wide_x.at[n, 1], side_x),
            push(kept.at[slot, pl.ds(2 * (1 - at_y), 2), :, second], wide_y.at[n], side_y),
        ]

    def over_first(n):
        slot = n % depth
        for copy in over[n]:
            copy.wait_recv()

        def step(i, _):
            side, z = i // slots, i % slots
            spot = 2 * side + at_x
            kept[slot, spot, z, 0:half] = total(kept[slot, spot, z, 0:half], wide_x[n, side, z])
            spot = 2 * at_y + side
            kept[slot, spot, z, half:UNIT] = total(kept[slot, spot, z, half:UNIT], wide_y[n, side, z])
            return 0

        lax.fori_loop(0, 2 * slots, step, 0)
        across[n] = [
            push(kept.at[slot, 2 * (1 - at_y) + at_x, :, first], narrow_y.at[n], side_y),
            push(kept.at[slot, 2 * at_y + 1 - at_x, :, second], narrow_x.at[n], side_x),
        ]

    def over_second(n):
        slot = n % depth
        for copy in across[n]:
            copy.wait_recv()
        spot = 2 * at_y + at_x

        def step(z, _):
            kept[slot, spot, z, 0:half] = total(kept[slot, spot, z, 0:half], narrow_y[n, z])
            kept[slot, spot, z, half:UNIT] = total(kept[slot, spot, z, half:UNIT], narrow_x[n, z])
            return 0

        lax.fori_loop(0, slots, step, 0)
        along[n] = []
        for step_on in range(1, slots):
            goal = (place + step_on) % slots
            along[n].append(push(kept.at[slot, spot, goal], from_slot.at[n, step_on - 1], (pb, goal)))

    def over_slots(n):
        slot = n % depth
        mat, unit = units[n]
        for copy in along[n]:
            copy.wait_recv()
        here = kept[slot, 2 * at_y + at_x, place].astype(jnp.float32)
        for step_on in range(1, slots):
            here = here + from_slot[n, step_on - 1].astype(jnp.float32)
        outs[mat][unit * UNIT : (unit + 1) * UNIT, :] = here
        if n + depth < len(units):
            for copy in over[n] + across[n] + along[n]:
                copy.wait_send()
            loads[n + depth] = put(block(n + depth, core), kept.at[slot])

    stages = (from_cores, over_first, over_second, over_slots)
    for turn in range(len(units) + len(stages) - 1):
        for lag, stage in enumerate(stages):
            if 0 <= turn - lag < len(units):
                stage(turn - lag)
        if turn == 0:
            by_few.wait_recv()
            few_here[0] = few[...] + few_there[0]
            by_few = push(few_here.at[0], few_there.at[1], side_x)
        if turn == 1:
            by_few.wait_recv()
            few_here[1] = few_here[0] + few_there[1]
            by_few = push(few_here.at[1], few_there.at[2], side_y)
        if turn == 2:
            by_few.wait_recv()
            few_here[2] = few_here[1] + few_there[2]
            few_slot[place] = few_here[2]
            by_few = [
                push(few_here.at[2], few_slot.at[place], (pb, (place + step) % slots))
                for step in range(1, slots)
            ]
    for copy in by_few:
        copy.wait_recv()
    every = few_slot[0]
    for step in range(1, slots):
        every = every + few_slot[step]
    few_out[...] = every
    for copy in by_rows:
        copy.wait_recv()
    at_home.wait()
    freed = set()
    for n in range(len(units) - depth):
        freed.update(id(copy) for copy in over[n] + across[n] + along[n])
    for copy in sent:
        if id(copy) not in freed:
            copy.wait_send()


def scatter_outputs(grad_attn, grad_in_w, grad_out_w, grad_inputs, small):
    n_pb, slots = lax.axis_size("pb"), lax.axis_size("slot")
    if (n_pb, slots) != (8, 4):
        return (
            scatter_all(grad_attn),
            scatter_all(grad_in_w),
            scatter_all(grad_out_w),
            to_positions(leave_slots(grad_inputs)),
            sum_all(small, ("core", "x", "y", "slot")),
        )
    width = grad_attn.shape[1]
    mats = [
        mat.reshape(n_pb // 2, 2, slots, -1, width)
        for mat in (grad_attn, grad_in_w, grad_out_w)
    ]
    own, questions, steps, _ = grad_inputs.shape
    rows = grad_inputs.reshape(own, questions, slots, steps // slots, width)
    laid = jax.ShapeDtypeStruct((own, slots, questions, steps // slots, width), rows.dtype)
    units = sum(mat.shape[3] for mat in mats) // UNIT
    depth = 5
    copies = units * (1 + 3 + 2 + slots - 1) + (slots - 1) + 3 + slots - 1
    anywhere, inside = pl.BlockSpec(memory_space=pl.ANY), pl.BlockSpec(memory_space=pltpu.VMEM)
    half = UNIT // 2
    low, high = jnp.bfloat16, jnp.float32
    *shards, laid, small = pl.pallas_call(
        scatter_kernel,
        in_specs=[anywhere] * 4 + [inside],
        out_specs=[inside] * 3 + [anywhere, inside],
        out_shape=[jax.ShapeDtypeStruct(mat.shape[3:], high) for mat in mats]
        + [laid, jax.ShapeDtypeStruct(small.shape, high)],
        scratch_shapes=[
            pltpu.VMEM((units, 4, slots, UNIT, width), low),
            pltpu.VMEM((depth, 4, slots, UNIT, width), low),
            pltpu.VMEM((units, 2, slots, half, width), low),
            pltpu.VMEM((units, 2, slots, half, width), low),
            pltpu.VMEM((units, slots, half, width), low),
            pltpu.VMEM((units, slots, half, width), low),
            pltpu.VMEM((units, slots - 1, UNIT, width), low),
            pltpu.VMEM((3,) + small.shape, high),
            pltpu.VMEM((3,) + small.shape, high),
            pltpu.VMEM((slots,) + small.shape, high),
            pltpu.SemaphoreType.DMA((copies,)),
            pltpu.SemaphoreType.DMA((copies,)),
            pltpu.SemaphoreType.DMA((units + 1,)),
        ],
        compiler_params=pltpu.CompilerParams(
            collective_id=1, has_side_effects=True, vmem_limit_bytes=60 << 20
        ),
        cost_estimate=SMALL,
        name="scatter_outputs",
    )(*mats, rows, small)
    return (*shards, laid.reshape((-1,) + laid.shape[2:]), small)


def body(
    x_in,
    memory,
    doc_scores,
    valid_count,
    target_ids,
    target_len,
    mem_len,
    attn_w,
    ffn_in,
    ffn_out,
    ffn_bias,
    norms,
    embedding,
):
    x_here, mem_here, attn_full, in_full, out_full = gather_inputs(
        x_in, memory, attn_w, ffn_in, ffn_out
    )
    slots_here, questions, tgt_steps, model_width = x_here.shape
    mem_steps = mem_here.shape[2]
    seq_count = slots_here * questions
    head_dim = model_width // HEADS
    scaling = head_dim ** (-0.5)
    blocks = [
        attn_full[block_index * model_width : (block_index + 1) * model_width]
        for block_index in range(8)
    ]

    inputs = x_here.reshape(seq_count * tgt_steps, model_width)
    memory_rows = mem_here.reshape(seq_count * mem_steps, model_width)
    positions = jnp.arange(tgt_steps)
    place, slot_count = place_of("slot")
    core, cores = place_of("core")
    ring = (place - jnp.arange(slot_count)) % slot_count
    lengths_here = [mem_len] + [shifted(mem_len, "slot", step) for step in range(1, slot_count)]
    lengths_here = jnp.stack(lengths_here)[ring].reshape(slots_here, slot_count, questions)
    mem_lengths = pick(lengths_here, place, 1).reshape(seq_count)
    tgt_lengths = jnp.full_like(mem_lengths, tgt_steps)
    queries = (product(inputs, blocks[0]) * scaling).astype(jnp.bfloat16)
    key_rows = product(inputs, blocks[1]).astype(jnp.bfloat16)
    value_rows = product(inputs, blocks[2]).astype(jnp.bfloat16)
    self_out, self_lse = attend(True, tgt_lengths, queries, key_rows, value_rows)
    hidden_one, normed_one, root_one = norm_forward(
        inputs.astype(jnp.float32) + product(self_out, blocks[3]), norms[0], norms[1]
    )
    one_low = hidden_one.astype(jnp.bfloat16)
    cross_queries = (product(one_low, blocks[4]) * scaling).astype(jnp.bfloat16)
    cross_keys = product(memory_rows, blocks[5]).astype(jnp.bfloat16)
    cross_values = product(memory_rows, blocks[6]).astype(jnp.bfloat16)
    cross_out, cross_lse = attend(False, mem_lengths, cross_queries, cross_keys, cross_values)
    hidden_two, normed_two, root_two = norm_forward(
        hidden_one + product(cross_out, blocks[7]), norms[2], norms[3]
    )
    two_low = hidden_two.astype(jnp.bfloat16)
    pre_act = contract_cols(two_low, in_full) + ffn_bias
    act, slope = gelu_parts(pre_act)
    act_low, slope = act.astype(jnp.bfloat16), slope.astype(jnp.bfloat16)
    hidden_three, normed_three, root_three = norm_forward(
        hidden_two + product(act_low, out_full), norms[4], norms[5]
    )
    three_low = hidden_three.astype(jnp.bfloat16).reshape(
        slots_here, questions, tgt_steps, model_width
    )
    vocab_here = embedding.shape[0]
    share = vocab_here // cores
    pieces = slots_here * questions

    def both_cores(value):
        return jnp.stack([value, shifted(value, "core", 1)]) if cores > 1 else value[None]

    tokens = jnp.concatenate([target_ids, valid_count[:, None], target_len[:, None]], axis=1)
    tokens = both_cores(tokens)
    ids_all, valid_all, len_all = tokens[:, :, :tgt_steps], tokens[:, :, -2], tokens[:, :, -1]

    local = target_ids - place * vocab_here
    held = jnp.logical_and(local >= 0, local < vocab_here)
    target_rows = jnp.take(embedding, jnp.clip(local, 0, vocab_here - 1), axis=0)
    target_rows = jnp.where(held[..., None], target_rows, jnp.zeros_like(target_rows))
    target_rows = after(target_rows, x_here)
    found = [shifted(target_rows, "slot", step) for step in range(1, slot_count)]
    target_rows = sum([f.astype(jnp.float32) for f in found], target_rows.astype(jnp.float32))

    slot_ids = jnp.arange(slot_count)[:, None] + slot_count * jnp.arange(slots_here)[None]
    live_piece = slot_ids[:, None, :, None] < valid_all[None, :, None, :]
    long_piece = (len_all + 15) // 16 * 16
    long_piece = jnp.where(live_piece, long_piece[None, :, None, :], 0).reshape(slot_count, -1)
    ends = jnp.cumsum(long_piece, axis=1)
    packing = jnp.concatenate([ends - long_piece, ends[:, -1:]], axis=1)[ring]
    info = jnp.concatenate([core[None], packing.reshape(-1)]).astype(jnp.int32)
    piece_ids = (ids_all - (place * vocab_here + core * share)).astype(jnp.float32)
    piece_ids = jnp.broadcast_to(
        piece_ids[None, :, None], (slot_count, cores, slots_here, questions, tgt_steps)
    ).reshape(-1, 1, tgt_steps)
    ids_rows = jnp.broadcast_to(piece_ids, (piece_ids.shape[0], 8, tgt_steps))

    group = pieces * tgt_steps
    moving = three_low.reshape(group, model_width)
    kept, log_list, joining = (), [], []
    arriving = [moving] + [shifted(moving, "slot", step) for step in range(1, slot_count)]
    for step in range(slot_count):
        moving = arriving[step] if not step else after(arriving[step], own_logs)
        other = shifted(moving, "core", 1)
        earlier = (own_logs,) if step else ()
        *kept, own_sums, mate_sums, own_logs, mate_logs = rows_pass(
            step, slot_count, info, ids_rows, moving, other, embedding, cores, kept, earlier
        )
        log_list += [own_logs[:, 0], mate_logs[:, 0]]
        joining.append(
            (own_sums, shifted(mate_sums, "core", 1), own_logs, shifted(mate_logs, "core", 1))
        )
    homes = list(join_pass(*zip(*joining)))

    def by_slot(value):
        parts = [value] + [shifted(value, "slot", step) for step in range(1, slot_count)]
        return jnp.stack(parts)[ring]

    target_logit = jnp.sum(three_low.astype(jnp.float32) * target_rows[None], axis=-1)
    told = jnp.concatenate(log_list + [target_logit.reshape(-1, tgt_steps)], axis=0)
    told = both_cores(by_slot(told))
    hit_all = told[:, :, -pieces:].reshape(cores, slot_count, slots_here, questions, tgt_steps)
    hit_all = hit_all.transpose(2, 1, 0, 3, 4).reshape(-1, cores, questions, tgt_steps)
    logs = told[:, :, :-pieces].reshape(
        cores, slot_count, slot_count, cores, slots_here, questions, tgt_steps
    )
    logs = jnp.stack([logs[0], logs[1][:, :, ::-1]]) if cores > 1 else logs
    logs = jax.nn.logsumexp(logs, axis=0)
    turns = (jnp.arange(slot_count)[:, None] - jnp.arange(slot_count)[None]) % slot_count
    logs = jnp.take_along_axis(
        logs, turns.reshape((slot_count, slot_count) + (1,) * (logs.ndim - 2)), axis=1
    )
    rest_all = jax.nn.logsumexp(logs, axis=0)
    rest_all = rest_all.transpose(2, 0, 1, 3, 4).reshape(hit_all.shape)
    log_norm = jnp.logaddexp(rest_all, hit_all)
    live = positions < len_all[..., None]
    lengths = len_all.astype(jnp.float32)
    per_slot = jnp.sum(jnp.where(live[None], hit_all - log_norm, 0.0), axis=3) / lengths[None]
    valid = jnp.arange(per_slot.shape[0])[:, None, None] < valid_all[None]
    scores_t = both_cores(doc_scores).transpose(2, 0, 1)
    joint = jnp.where(valid, scores_t + per_slot, mask_fill)
    prior = jnp.where(valid, scores_t, mask_fill)
    joint_total = jax.nn.logsumexp(joint, axis=0)
    neg_marginal = jax.nn.logsumexp(prior, axis=0) - joint_total
    log_post = joint - joint_total
    posterior = jnp.exp(log_post)
    entropy_q = -jnp.sum(posterior * log_post, axis=0)
    objective_part = jnp.sum((lengths * (neg_marginal + entropy_weight * entropy_q))[0])
    slot_weight = -posterior * (1.0 + entropy_weight * (log_post + entropy_q[None]))
    token_weight = jnp.where(live[None], slot_weight[..., None], 0.0)
    hit_weight = token_weight * jax.nn.sigmoid(rest_all - hit_all)

    def own_slots(value):
        value = value[:, 0].reshape(slots_here, slot_count, questions, tgt_steps)
        return pick(value, place, 1)

    def ring_rows(value):
        value = value.reshape(slots_here, slot_count, cores, questions, tgt_steps)
        return value.transpose(1, 2, 0, 3, 4)[ring].reshape(-1, tgt_steps)

    facts = [ring_rows(value) for value in (token_weight, log_norm, hit_weight)]
    facts = jnp.stack(facts + [ids_rows[:, 0]] + [jnp.zeros_like(facts[0])] * 4, axis=1)
    expos, packed, tops = kept
    tiles = expos.shape[1]
    n_pb = lax.axis_size("pb")
    tall, wide, _ = grid_of(n_pb)
    sends = tuple(homes[1:])
    homes[1:] = [
        shifted(homes[step], "slot", slot_count - step) for step in range(1, slot_count)
    ]
    table_grads = []
    for first, count in ((0, tiles),):
        sides = [
            side.reshape((tall, wide, cores) + side.shape[1:])
            for side in table_pass(
                info, facts, tops, packed, expos, first, count, n_pb, sends
            )
        ]
        sends = (ring_first(sides[0], "x", 1), ring_first(sides[1], "y", 0))
        table_grads.append(sides)

    def over_first(sides, late):
        return (
            ring_scatter(sides[0], "x", 1, late).astype(jnp.bfloat16),
            ring_scatter(sides[1], "y", 0, late).astype(jnp.bfloat16),
        )

    def over_second(sides, late):
        return (
            ring_scatter(sides[0], "y", 0, late).astype(jnp.bfloat16),
            ring_scatter(sides[1], "x", 0, late).astype(jnp.bfloat16),
        )

    def second_sends(sides):
        return ring_first(sides[0], "y", 0), ring_first(sides[1], "x", 0)

    home_logs = pick(logs, place, 1)[:, 0][(place + jnp.arange(slot_count)) % slot_count]
    home_logs = home_logs.reshape(slot_count, pieces, tgt_steps).transpose(1, 0, 2)
    home_logs = jnp.pad(
        home_logs, ((0, 0), (0, 8 - slot_count), (0, 0)), constant_values=mask_fill
    )
    own_weight = own_slots(hit_weight).reshape(pieces, 1, tgt_steps)
    own_weight = jnp.broadcast_to(own_weight, (pieces, 8, tgt_steps))
    grad_three = home_pass(home_logs, own_weight, target_rows, homes, sends)
    back_blocks, in_back, out_back = blocks, in_full, out_full
    grad_res_three, gain_three, shift_three = norm_backward(
        grad_three, normed_three, root_three, norms[4]
    )
    grad_ffn = grad_res_three.astype(jnp.bfloat16)
    grad_out_w = contract_rows(act_low, grad_ffn)
    grad_act = lax.optimization_barrier(contract_cols(grad_ffn, out_back))
    grad_pre = (grad_act * slope.astype(jnp.float32)).astype(jnp.bfloat16)
    grad_in_w = contract_rows(grad_pre, two_low)
    grad_bias = jnp.sum(grad_pre.astype(jnp.float32), axis=0)
    grad_two = grad_res_three + product(grad_pre, in_back)
    grad_res_two, gain_two, shift_two = norm_backward(grad_two, normed_two, root_two, norms[2])
    grad_cross = grad_res_two.astype(jnp.bfloat16)
    grad_w7 = contract_rows(cross_out, grad_cross)
    grad_cross_out = contract_cols(grad_cross, back_blocks[7]).astype(jnp.bfloat16)
    cq_grad, ck_grad, cv_grad = attend(
        False, mem_lengths, cross_queries, cross_keys, cross_values, cross_lse, grad_cross_out
    )
    grad_w4 = contract_rows(one_low, cq_grad) * scaling
    grad_w5 = contract_rows(memory_rows, ck_grad)
    grad_w6 = contract_rows(memory_rows, cv_grad)
    grad_memory = (
        contract_cols(ck_grad, back_blocks[5]) + contract_cols(cv_grad, back_blocks[6])
    ).astype(jnp.bfloat16)
    grad_memory = leave_slots(
        grad_memory.reshape(slots_here, questions, mem_steps, model_width)
    )
    table_sum = [over_first(sides, cq_grad) for sides in table_grads]
    earlier = grad_memory[1:] + [send for sides in table_sum for send in second_sends(sides)]
    grad_one = grad_res_two + contract_cols(cq_grad, back_blocks[4]) * scaling
    grad_res_one, gain_one, shift_one = norm_backward(grad_one, normed_one, root_one, norms[0])
    grad_attn_out = grad_res_one.astype(jnp.bfloat16)
    grad_w3 = contract_rows(self_out, grad_attn_out)
    grad_self_out = contract_cols(grad_attn_out, back_blocks[3]).astype(jnp.bfloat16)
    sq_grad, sk_grad, sv_grad = attend(
        True, tgt_lengths, queries, key_rows, value_rows, self_lse, grad_self_out, earlier
    )
    grad_w0 = contract_rows(inputs, sq_grad) * scaling
    grad_w1 = contract_rows(inputs, sk_grad)
    grad_w2 = contract_rows(inputs, sv_grad)
    grad_inputs = (
        grad_res_one
        + contract_cols(sq_grad, back_blocks[0]) * scaling
        + contract_cols(sk_grad, back_blocks[1])
        + contract_cols(sv_grad, back_blocks[2])
    )
    grad_inputs = grad_inputs.astype(jnp.bfloat16).reshape(
        slots_here, questions, tgt_steps, model_width
    )
    grad_attn = jnp.concatenate(
        [
            grad.astype(jnp.bfloat16)
            for grad in (grad_w0, grad_w1, grad_w2, grad_w3, grad_w4, grad_w5, grad_w6, grad_w7)
        ],
        axis=0,
    )
    small = jnp.concatenate(
        [
            jnp.stack([gain_one, shift_one, gain_two, shift_two, gain_three, shift_three], axis=0),
            grad_bias.reshape(-1, model_width),
            jnp.zeros((6, model_width), jnp.float32)
            .at[0, :3]
            .set(jnp.stack([objective_part, jnp.sum(lengths[0]), jnp.sum(entropy_q[0])])),
        ],
        axis=0,
    )
    table_sum = [over_second(sides, grad_inputs) for sides in table_sum]
    table_sum = [jnp.stack(sides, axis=2) for sides in table_sum]
    table_sum = jnp.concatenate(table_sum, axis=1).reshape(cores, share, -1)
    table_send = pick(table_sum, 1 - core, 0)
    grad_attn, grad_in_w, grad_out_w, grad_inputs, small = scatter_outputs(
        grad_attn,
        grad_in_w.astype(jnp.bfloat16),
        grad_out_w.astype(jnp.bfloat16),
        grad_inputs,
        after(small, table_send),
    )
    grad_memory = [grad_memory[0]] + [
        shifted(grad_memory[step], "slot", step) for step in range(1, slot_count)
    ]
    grad_memory = lay_blocks(grad_memory, place, (small,))
    grad_memory = grad_memory.reshape((-1,) + grad_memory.shape[2:])
    kept = pick(table_sum, core, 0)
    given = after(shifted(table_send, "core", 1), small)
    grad_embed = jnp.stack([kept, given])
    grad_embed = jnp.where(core == 0, grad_embed, grad_embed[::-1])
    grad_embed = grad_embed.reshape(vocab_here, -1).astype(jnp.float32)
    grad_norms = small[:6]
    scalars = small[-6]
    loss = scalars[0] / scalars[1]
    entropy = scalars[2] / (questions * n_pb * slot_count)
    grad_bias = small[6:-6].reshape(-1)
    own_bias = grad_bias.shape[0] // (lax.axis_size("pb") * slot_count)
    grad_bias = lax.dynamic_slice_in_dim(
        grad_bias,
        (lax.axis_index("pb") * slot_count + lax.axis_index("slot")) * own_bias,
        own_bias,
    )
    return (
        loss,
        entropy,
        grad_inputs,
        grad_memory,
        grad_attn,
        grad_in_w,
        grad_out_w,
        grad_bias,
        grad_norms,
        grad_embed,
    )


def solution(mesh):
    placed = (
        P(None, "pb", "slot", None),
        P(None, "pb", "slot", None),
        P("pb", None),
        P("pb"),
        P("pb", None),
        P("pb"),
        P("slot", "pb"),
        P(("pb", "slot"), None),
        P(("pb", "slot"), None),
        P(("pb", "slot"), None),
        P(),
        P(),
        P("slot", None),
    )
    return jax.shard_map(
        body,
        mesh=mesh,
        in_specs=placed,
        out_specs=(
            P(),
            P(),
            P(None, "pb", "slot", None),
            P(None, "pb", "slot", None),
            P(("pb", "slot"), None),
            P(("pb", "slot"), None),
            P(("pb", "slot"), None),
            P(("pb", "slot")),
            P(),
            P("slot", "pb"),
        ),
        check_vma=False,
    )
```

```python
import functools

import jax
import jax.numpy as jnp
from jax import lax
from jax.experimental import pallas as pl
from jax.experimental.pallas import tpu as pltpu
from jax.sharding import PartitionSpec as P

HEADS = 16


eps_norm = 1e-05
entropy_weight = 0.25
mask_fill = -1e30
root_half = 0.7071067811865476
inv_root_tau = 0.3989422804014327


def grid_of(n_pb):
    cores = 2 if n_pb % 2 == 0 else 1
    chips = n_pb // cores
    wide = max(d for d in range(1, chips + 1) if chips % d == 0 and d * d <= chips)
    return chips // wide, wide, cores


def shifted(value, axis, step):
    if axis == "slot":
        size = lax.axis_size("slot")
        return lax.ppermute(value, "slot", [(i, (i + step) % size) for i in range(size)])
    n_pb = lax.axis_size("pb")
    tall, wide, cores = grid_of(n_pb)
    pairs = []
    for i in range(n_pb):
        y, x, c = i // (wide * cores), i // cores % wide, i % cores
        if axis == "y":
            y = (y + step) % tall
        elif axis == "x":
            x = (x + step) % wide
        else:
            c = (c + step) % cores
        pairs.append((i, (y * wide + x) * cores + c))
    return lax.ppermute(value, "pb", pairs)


def place_of(axis):
    if axis == "slot":
        return lax.axis_index("slot"), lax.axis_size("slot")
    tall, wide, cores = grid_of(lax.axis_size("pb"))
    i = lax.axis_index("pb")
    if axis == "y":
        return i // (wide * cores), tall
    if axis == "x":
        return i // cores % wide, wide
    return i % cores, cores


def after(value, *tokens):
    for token in tokens:
        first = token[(0,) * token.ndim].astype(jnp.float32)
        value = jnp.where(first == first, value, jnp.zeros_like(value))
    return value


def pick(value, index, dim):
    return lax.dynamic_index_in_dim(value, index, dim, keepdims=False)


def ring_gather(value, axis):
    me, size = place_of(axis)
    found = [(me, value)]
    for step in range(1, size):
        value = shifted(value, axis, 1)
        found.append(((me - step) % size, value))
    return found


def ring_scatter(value, axis, dim, late=None):
    me, size = place_of(axis)
    total = pick(value, (me - 1) % size, dim).astype(jnp.bfloat16)
    for step in range(1, size):
        part = pick(value, (me - 1 - step) % size, dim)
        total = shifted(total, axis, 1)
        if late is not None:
            total = after(total, late)
        total = total.astype(jnp.float32) + part.astype(jnp.float32)
        if step < size - 1:
            total = total.astype(jnp.bfloat16)
    return total


def ring_first(value, axis, dim):
    me, size = place_of(axis)
    return pick(value, (me - 1) % size, dim).astype(jnp.bfloat16)


def gather_all(shard):
    tall, wide, cores = grid_of(lax.axis_size("pb"))
    rows, width = shard.shape
    slots = lax.axis_size("slot")
    column = jnp.zeros((slots, rows, width), shard.dtype)
    for index, block in ring_gather(shard, "slot"):
        column = lax.dynamic_update_index_in_dim(column, block, index, 0)
    column = column.reshape(slots * rows, width)
    half = slots * rows // 2
    core, _ = place_of("core")
    whole = jnp.zeros((tall * wide, cores, 2, half, width), shard.dtype)
    for side, (first, second) in enumerate((("x", "y"), ("y", "x"))):
        part = column[side * half : (side + 1) * half]
        for at_first, block in ring_gather(part, first):
            for at_second, block in ring_gather(block, second):
                x, y = (at_first, at_second) if first == "x" else (at_second, at_first)
                for at_core, block in ring_gather(block, "core"):
                    whole = lax.dynamic_update_slice(
                        whole, block[None, None, None], (y * wide + x, at_core, side, 0, 0)
                    )
    return whole.reshape(tall * wide * cores, slots * rows, width)


def scatter_pb(value, lates=(None, None, None)):
    tall, wide, cores = grid_of(lax.axis_size("pb"))
    rest = value.shape[1:]
    value = value.reshape((tall * wide, cores) + rest)
    value = ring_scatter(value, "core", 1, lates[0]).astype(jnp.bfloat16)
    value = value.reshape((tall, wide) + rest)
    half = rest[0] // 2
    first = ring_scatter(value[:, :, :half], "x", 1, lates[1])
    second = ring_scatter(value[:, :, half:], "y", 0, lates[1])
    first = ring_scatter(first.astype(jnp.bfloat16), "y", 0, lates[2])
    second = ring_scatter(second.astype(jnp.bfloat16), "x", 0, lates[2])
    return jnp.concatenate([first, second], axis=0)


def scatter_all(value):
    n_pb, slots = lax.axis_size("pb"), lax.axis_size("slot")
    rows = value.shape[0] // (n_pb * slots)
    value = value.reshape((n_pb, slots, rows) + value.shape[1:])
    column = scatter_pb(value)
    return ring_scatter(column.astype(jnp.bfloat16), "slot", 0)


def scatter_slot(value, late):
    me, size = place_of("slot")
    parts = [
        after(shifted(pick(value, (me + step) % size, 0), "slot", step), late)
        for step in range(1, size)
    ]
    return sum([part.astype(jnp.float32) for part in parts], pick(value, me, 0).astype(jnp.float32))


def sum_all(value, axes):
    for axis in axes:
        me, size = place_of(axis)
        parts = [value] + [shifted(value, axis, step) for step in range(1, size)]
        placed = jnp.stack(parts)
        value = jnp.sum(placed[(me - jnp.arange(size)) % size], axis=0)
    return value


def to_slots(value):
    me, size = place_of("slot")
    every, questions, steps, width = value.shape
    chunks = value.reshape(every // size, size, questions, steps, width)
    result = jnp.zeros((every // size, questions, size, steps, width), value.dtype)
    for step in range(size):
        block = pick(chunks, (me + step) % size, 1)
        if step:
            block = shifted(block, "slot", step)
        result = lax.dynamic_update_index_in_dim(result, block, (me - step) % size, 2)
    return result.reshape(every // size, questions, size * steps, width)


def leave_slots(value):
    me, size = place_of("slot")
    own, questions, steps, width = value.shape
    chunks = value.reshape(own, questions, size, steps // size, width)
    return [pick(chunks, (me + step) % size, 2) for step in range(size)]


def to_positions(blocks, late=None):
    me, size = place_of("slot")
    own, questions, steps, width = blocks[0].shape
    result = jnp.zeros((own, size, questions, steps, width), blocks[0].dtype)
    for step, block in enumerate(blocks):
        if step:
            block = shifted(block, "slot", step)
            block = block if late is None else after(block, late)
        result = lax.dynamic_update_index_in_dim(result, block, (me - step) % size, 1)
    return result.reshape(size * own, questions, steps, width)


def product(left, right):
    return jnp.dot(left, right, preferred_element_type=jnp.float32)


def contract_rows(left, right):
    return lax.dot_general(
        left, right, (((0,), (0,)), ((), ())), preferred_element_type=jnp.float32
    )


def contract_cols(left, right):
    return lax.dot_general(
        left, right, (((1,), (1,)), ((), ())), preferred_element_type=jnp.float32
    )


def norm_forward(resid, gain, shift):
    row_mean = jnp.mean(resid, axis=-1, keepdims=True)
    centered = resid - row_mean
    inv_root = lax.rsqrt(jnp.mean(centered * centered, axis=-1, keepdims=True) + eps_norm)
    normed = centered * inv_root
    return (normed * gain + shift, normed, inv_root)


def norm_backward(grad_out, normed, inv_root, gain):
    scaled = grad_out * gain
    grad_in = inv_root * (
        scaled
        - jnp.mean(scaled, axis=-1, keepdims=True)
        - normed * jnp.mean(scaled * normed, axis=-1, keepdims=True)
    )
    return (grad_in, jnp.sum(grad_out * normed, axis=0), jnp.sum(grad_out, axis=0))


def two_heads(value):
    left = lax.broadcasted_iota(jnp.int32, value.shape, 1) < value.shape[1] // 2
    none = jnp.zeros_like(value)
    return jnp.concatenate([jnp.where(left, value, none), jnp.where(left, none, value)], axis=0)


def one_pair(value):
    rows = value.shape[0] // 2
    left = lax.broadcasted_iota(jnp.int32, (rows, value.shape[1]), 1) < value.shape[1] // 2
    return jnp.where(left, value[:rows], value[rows:])


def pair_scores(info, causal, queries, key_rows):
    scores = lax.dot_general(
        queries, key_rows, (((1,), (1,)), ((), ())), preferred_element_type=jnp.float32
    )
    column = lax.broadcasted_iota(jnp.int32, scores.shape, 1)
    if causal:
        row = lax.broadcasted_iota(jnp.int32, scores.shape, 0)
        allowed = column <= jnp.where(row < scores.shape[0] // 2, row, row - scores.shape[0] // 2)
    else:
        allowed = column < info[pl.program_id(0)]
    return jnp.where(allowed, scores, mask_fill)


def attend_kernel(causal, info, queries, keys, values, out, logs):
    steps, width = queries.shape
    lane = lax.broadcasted_iota(jnp.int32, (steps, 128), 1)
    kept = jnp.zeros((steps, 128), jnp.float32)

    def first(pair):
        here = slice(pair * 128, (pair + 1) * 128)
        return pair_scores(info, causal, two_heads(queries[:, here]), keys[:, here])

    following = first(0)
    for pair in range(width // 128):
        here = slice(pair * 128, (pair + 1) * 128)
        scores = following
        if pair + 1 < width // 128:
            following = first(pair + 1)
        row_max = jnp.max(scores, axis=1, keepdims=True)
        expos = jnp.exp(scores - row_max)
        row_sum = jnp.sum(expos, axis=1, keepdims=True)
        probs = (expos * (1.0 / row_sum)).astype(jnp.bfloat16)
        out[:, here] = one_pair(
            jnp.dot(probs, values[:, here], preferred_element_type=jnp.float32)
        ).astype(jnp.bfloat16)
        log = row_max + jnp.log(row_sum)
        kept = jnp.where(lane == 2 * pair, log[:steps], kept)
        kept = jnp.where(lane == 2 * pair + 1, log[steps:], kept)
    logs[...] = kept


def attend_back_kernel(causal, info, queries, keys, values, logs, grads, *refs):
    d_queries, d_keys, d_values = refs[-3:]
    steps, width = queries.shape
    rows_first = (((0,), (0,)), ((), ()))

    def first(pair):
        here = slice(pair * 128, (pair + 1) * 128)
        both = two_heads(queries[:, here])
        both_grads = two_heads(grads[:, here])
        scores = pair_scores(info, causal, both, keys[:, here])
        d_probs = lax.dot_general(
            both_grads, values[:, here], (((1,), (1,)), ((), ())), preferred_element_type=jnp.float32
        )
        return both, both_grads, scores, d_probs

    following = first(0)
    for pair in range(width // 128):
        here = slice(pair * 128, (pair + 1) * 128)
        both, both_grads, scores, d_probs = following
        if pair + 1 < width // 128:
            following = first(pair + 1)
        log = jnp.concatenate(
            [logs[:, 2 * pair : 2 * pair + 1], logs[:, 2 * pair + 1 : 2 * pair + 2]], axis=0
        )
        probs = jnp.exp(scores - log)
        d_values[:, here] = lax.dot_general(
            probs.astype(jnp.bfloat16), both_grads, rows_first, preferred_element_type=jnp.float32
        ).astype(jnp.bfloat16)
        delta = jnp.sum(d_probs * probs, axis=1, keepdims=True)
        d_scores = (probs * (d_probs - delta)).astype(jnp.bfloat16)
        d_queries[:, here] = one_pair(
            jnp.dot(d_scores, keys[:, here], preferred_element_type=jnp.float32)
        ).astype(jnp.bfloat16)
        d_keys[:, here] = lax.dot_general(
            d_scores, both, rows_first, preferred_element_type=jnp.float32
        ).astype(jnp.bfloat16)


def attend(causal, lengths, queries, keys, values, logs=None, grads=None, earlier=()):
    count = lengths.shape[0]
    width = queries.shape[1]
    steps, spans = queries.shape[0] // count, keys.shape[0] // count
    short = pl.BlockSpec((steps, width), lambda i, s: (i, 0))
    long = pl.BlockSpec((spans, width), lambda i, s: (i, 0))
    thin = pl.BlockSpec((steps, 128), lambda i, s: (i, 0))
    like = lambda value: jax.ShapeDtypeStruct(value.shape, jnp.bfloat16)
    if grads is None:
        kernel, operands = attend_kernel, (queries, keys, values)
        in_specs, out_specs = [short, long, long], [short, thin]
        out_shape = [like(queries), jax.ShapeDtypeStruct((queries.shape[0], 128), jnp.float32)]
    else:
        kernel, operands = attend_back_kernel, (queries, keys, values, logs, grads, *earlier)
        in_specs, out_specs = [short, long, long, thin, short], [short, long, long]
        in_specs += [pl.BlockSpec(memory_space=pl.ANY)] * len(earlier)
        out_shape = [like(queries), like(keys), like(values)]
    flops = (4 if grads is None else 10) * queries.shape[0] * spans * width
    return pl.pallas_call(
        functools.partial(kernel, causal),
        grid_spec=pltpu.PrefetchScalarGridSpec(
            num_scalar_prefetch=1, grid=(count,), in_specs=in_specs, out_specs=out_specs
        ),
        out_shape=out_shape,
        compiler_params=pltpu.CompilerParams(vmem_limit_bytes=48 << 20),
        cost_estimate=pl.CostEstimate(
            flops=4 * flops, bytes_accessed=8 * keys.shape[0] * width, transcendentals=0
        ),
        name=("self" if causal else "cross") + ("_attend" if grads is None else "_attend_back"),
    )(lengths, *operands)


def gelu_parts(value):
    place = 1.0 / (1.0 + 0.3275911 * root_half * jnp.abs(value))
    bell = jnp.exp(-0.5 * value * value)
    series = 1.061405429
    for factor in (-1.453152027, 1.421413741, -0.284496736, 0.254829592):
        series = series * place + factor
    tail = 0.5 * series * place * bell
    share = jnp.where(value > 0.0, 1.0 - tail, tail)
    return value * share, share + value * (inv_root_tau * bell)


SMALL = pl.CostEstimate(flops=1 << 20, bytes_accessed=1 << 16, transcendentals=0)
PIECE = 128
CHUNK = 256


def vocab_tile(share):
    return max(d for d in range(16, 901, 16) if share % d == 0)


def columns(block):
    return jnp.concatenate([block] * 16, axis=0).T


def each_count(live, chunks, run):
    for taken in range(1, chunks + 1):
        above = live > (taken - 1) * CHUNK
        upto = live <= taken * CHUNK if taken < chunks else live >= 0

        @pl.when(jnp.logical_and(above, upto))
        def _():
            run(taken)


def piece_places(info, step, count):
    base = 1 + step * (count + 1)
    return [pl.multiple_of(info[base + i], 16) for i in range(count)], info[base + count]


def rows_kernel(step, info, ids, own, mate, table, *refs):
    expo, packed, tops, own_sums, mate_sums, own_logs, mate_logs, acc, top, total, marks = refs[-11:]
    expo, packed, tops = expo.at[0], packed.at[0], tops.at[0]
    tile = pl.program_id(0)
    wide = table.shape[0]
    pieces = own.shape[0] // PIECE
    count = 2 * pieces
    places, live = piece_places(info, step, count)

    @pl.when(tile == 0)
    def _():
        acc[...] = jnp.zeros_like(acc)
        top[...] = jnp.full_like(top, mask_fill)
        total[...] = jnp.zeros_like(total)
        tops[...] = jnp.zeros_like(tops)
        packed[...] = jnp.zeros_like(packed)
        marks[...] = jnp.full_like(marks, -1.0)
        for piece in range(count):
            side = own if piece < pieces else mate
            low = piece % pieces * PIECE
            packed[pl.ds(places[piece], PIECE), :] = side[low : low + PIECE, :]
            marks[pl.ds(places[piece], PIECE), :] = columns(ids[piece])

    lane = lax.broadcasted_iota(jnp.int32, (CHUNK, 128), 1)
    column = lax.broadcasted_iota(jnp.int32, (CHUNK, wide), 1)

    def scores(chunk):
        return lax.dot_general(
            packed[chunk * CHUNK : (chunk + 1) * CHUNK, :],
            table[...],
            (((1,), (1,)), ((), ())),
            preferred_element_type=jnp.float32,
        )

    def soften(chunk, logits):
        here = slice(chunk * CHUNK, (chunk + 1) * CHUNK)
        target = marks[here, 0:1].astype(jnp.int32) - tile * wide
        logits = jnp.where(column == target, mask_fill, logits)
        before = top[here, 0:1]
        now = jnp.maximum(before, jnp.max(logits, axis=1, keepdims=True))
        fade = jnp.exp(before - now)
        grown = jnp.exp(logits - now)
        total[here, :] = jnp.broadcast_to(
            total[here, 0:1] * fade + jnp.sum(grown, axis=1, keepdims=True), (CHUNK, 128)
        )
        top[here, :] = jnp.broadcast_to(now, (CHUNK, 128))
        tops[here, :] = jnp.where(lane == tile, now, tops[here, :])
        grown = grown.astype(jnp.bfloat16)
        expo[0, here, :] = grown
        return here, grown, fade

    def gather(here, grown, fade):
        acc[here, :] = acc[here, :] * fade + jnp.dot(
            grown, table[...], preferred_element_type=jnp.float32
        )

    def run(taken):
        logits = [scores(0)]
        late = None
        for chunk in range(taken):
            if chunk + 1 < taken:
                logits.append(scores(chunk + 1))
            ready = soften(chunk, logits[chunk])
            if late is not None:
                gather(*late)
            late = ready
        gather(*late)

    each_count(live, count * PIECE // CHUNK, run)

    @pl.when(tile == pl.num_programs(0) - 1)
    def _():
        for piece in range(count):
            here = pl.ds(places[piece], PIECE)
            mass = total[here, :]
            share = jnp.where(mass > 0.0, 1.0 / jnp.maximum(mass, 1e-30), 0.0)[:, 0:1]
            sums, logs = (own_sums, own_logs) if piece < pieces else (mate_sums, mate_logs)
            low = piece % pieces * PIECE
            sums[low : low + PIECE, :] = (acc[here, :] * share).astype(jnp.bfloat16)
            logs[piece % pieces] = (top[here, :] + jnp.log(jnp.maximum(mass, 1e-30))).T[0:8]


def rows_pass(step, steps, info, ids, own, mate, table, cores, kept, earlier):
    group, width = own.shape
    share = table.shape[0] // cores
    wide = vocab_tile(share)
    tiles = share // wide
    rows = 2 * group
    count = rows // PIECE
    room = rows + PIECE
    whole = lambda i, s: (0, 0)
    cube = lambda i, s: (0, 0, 0)
    return pl.pallas_call(
        functools.partial(rows_kernel, step),
        grid_spec=pltpu.PrefetchScalarGridSpec(
            num_scalar_prefetch=1,
            grid=(tiles,),
            in_specs=[
                pl.BlockSpec((count, 8, 128), lambda i, s: (step, 0, 0)),
                pl.BlockSpec((group, width), whole),
                pl.BlockSpec((group, width), whole),
                pl.BlockSpec((wide, width), lambda i, s: (s[0] * tiles + i, 0)),
            ]
            + [pl.BlockSpec(memory_space=pl.ANY)] * (len(kept) + len(earlier)),
            out_specs=[
                pl.BlockSpec((1, 1, rows, wide), lambda i, s: (step, i, 0, 0)),
                pl.BlockSpec((1, room, width), lambda i, s: (step, 0, 0)),
                pl.BlockSpec((1, room, 128), lambda i, s: (step, 0, 0)),
                pl.BlockSpec((group, width), whole),
                pl.BlockSpec((group, width), whole),
                pl.BlockSpec((count // 2, 8, 128), cube),
                pl.BlockSpec((count // 2, 8, 128), cube),
            ],
            scratch_shapes=[
                pltpu.VMEM((room, width), jnp.float32),
                pltpu.VMEM((room, 128), jnp.float32),
                pltpu.VMEM((room, 128), jnp.float32),
                pltpu.VMEM((room, 128), jnp.float32),
            ],
        ),
        out_shape=[
            jax.ShapeDtypeStruct((steps, tiles, rows, wide), jnp.bfloat16),
            jax.ShapeDtypeStruct((steps, room, width), jnp.bfloat16),
            jax.ShapeDtypeStruct((steps, room, 128), jnp.float32),
            jax.ShapeDtypeStruct((group, width), jnp.bfloat16),
            jax.ShapeDtypeStruct((group, width), jnp.bfloat16),
            jax.ShapeDtypeStruct((count // 2, 8, 128), jnp.float32),
            jax.ShapeDtypeStruct((count // 2, 8, 128), jnp.float32),
        ],
        input_output_aliases={5 + place: place for place in range(len(kept))},
        compiler_params=pltpu.CompilerParams(vmem_limit_bytes=60 << 20),
        cost_estimate=SMALL,
        name=f"rows_pass_{step}",
    )(info, ids, own, mate, table, *kept, *earlier)


def join_kernel(own, other, own_log, other_log, out):
    for piece in range(own_log.shape[0]):
        here = slice(piece * PIECE, (piece + 1) * PIECE)
        log = jnp.logaddexp(own_log[piece], other_log[piece])
        left = columns(jnp.exp(own_log[piece] - log))[:, 0:1]
        right = columns(jnp.exp(other_log[piece] - log))[:, 0:1]
        out[here, :] = (
            own[here, :].astype(jnp.float32) * left + other[here, :].astype(jnp.float32) * right
        ).astype(jnp.bfloat16)


def join_pass(own, other, own_log, other_log):
    rows, width = own.shape
    flat = pl.BlockSpec((CHUNK, width), lambda i: (i, 0))
    cube = pl.BlockSpec((CHUNK // PIECE, 8, 128), lambda i: (i, 0, 0))
    return pl.pallas_call(
        join_kernel,
        grid=(rows // CHUNK,),
        in_specs=[flat, flat, cube, cube],
        out_specs=flat,
        out_shape=jax.ShapeDtypeStruct((rows, width), jnp.bfloat16),
        cost_estimate=SMALL,
        name="join_pass",
    )(own, other, own_log, other_log)


def lay_kernel(count, info, *refs):
    out = refs[-1]
    step = (info[0] + count - pl.program_id(0)) % count
    for place in range(count):

        @pl.when(step == place)
        def _():
            out[:, 0] = refs[place][...]


def lay_blocks(blocks, place, earlier):
    count = len(blocks)
    own, questions, steps, width = blocks[0].shape
    whole = lambda i, s: (0, 0, 0, 0)
    return pl.pallas_call(
        functools.partial(lay_kernel, count),
        grid_spec=pltpu.PrefetchScalarGridSpec(
            num_scalar_prefetch=1,
            grid=(count,),
            in_specs=[pl.BlockSpec(blocks[0].shape, whole, pipeline_mode=pl.Buffered(1))] * count
            + [pl.BlockSpec(memory_space=pl.ANY)] * len(earlier),
            out_specs=pl.BlockSpec(
                (own, 1, questions, steps, width), lambda i, s: (0, i, 0, 0, 0)
            ),
        ),
        out_shape=jax.ShapeDtypeStruct((own, count, questions, steps, width), blocks[0].dtype),
        compiler_params=pltpu.CompilerParams(vmem_limit_bytes=48 << 20),
        cost_estimate=SMALL,
        name="lay_blocks",
    )(place.reshape(1).astype(jnp.int32), *blocks, *earlier)


def home_kernel(count, logs, weight, targets, *refs):
    parts, out = refs[:count], refs[-1]
    log = logs[0]
    share = jnp.exp(log - jnp.max(log, axis=0, keepdims=True))
    share = columns(share / jnp.sum(share, axis=0, keepdims=True))
    mean = parts[0][...].astype(jnp.float32) * share[:, 0:1]
    for place in range(1, count):
        mean = mean + parts[place][...].astype(jnp.float32) * share[:, place : place + 1]
    out[...] = columns(weight[0])[:, 0:1] * (targets[0] - mean)


def home_pass(logs, weight, targets, parts, earlier):
    rows, width = parts[0].shape
    questions = targets.shape[0]
    flat = pl.BlockSpec((PIECE, width), lambda i: (i, 0))
    cube = pl.BlockSpec((1, 8, 128), lambda i: (i, 0, 0))
    return pl.pallas_call(
        functools.partial(home_kernel, len(parts)),
        grid=(rows // PIECE,),
        in_specs=[cube, cube, pl.BlockSpec((1, PIECE, width), lambda i: (i % questions, 0, 0))]
        + [flat] * len(parts)
        + [pl.BlockSpec(memory_space=pl.ANY)] * len(earlier),
        out_specs=flat,
        out_shape=jax.ShapeDtypeStruct((rows, width), jnp.float32),
        cost_estimate=SMALL,
        name="home_pass",
    )(logs, weight, targets, *parts, *earlier)


def table_kernel(first, info, facts, tops, rows, expos, *refs):
    outs, acc, scales = refs[-4:-2], refs[-2], refs[-1]
    tile = pl.program_id(0) + first
    sources, _, both, wide = expos.shape
    count = both // PIECE

    @pl.when(pl.program_id(0) == 0)
    def _():
        def ready(source, _):
            places, _ = piece_places(info, source, count)
            scales[source] = jnp.zeros(scales.shape[1:], jnp.float32)
            for piece in range(count):
                scales[source, pl.ds(places[piece], PIECE), :] = columns(facts[source * count + piece])
            raw = scales[source]
            lane = lax.broadcasted_iota(jnp.int32, raw.shape, 1)
            weight = raw[:, 0:1]
            spread = jnp.where(weight == 0.0, 0.0, -weight * jnp.exp(tops[source] - raw[:, 1:2]))
            spread = jnp.where(lane == 127, raw[:, 2:3], spread)
            scales[source] = jnp.where(lane == 126, raw[:, 3:4], spread)
            return 0

        lax.fori_loop(0, sources, ready, 0)

    acc[...] = jnp.zeros_like(acc)

    def add(source, begin, size):
        here = pl.ds(pl.multiple_of(begin, CHUNK), size)
        scale = scales[source, here, :]
        lane = lax.broadcasted_iota(jnp.int32, (size, 128), 1)
        column = lax.broadcasted_iota(jnp.int32, (size, wide), 1)
        spread = jnp.sum(jnp.where(lane == tile, scale, 0.0), axis=1, keepdims=True)
        target = scale[:, 126:127].astype(jnp.int32) - tile * wide
        grad = expos[source, 0, here, :].astype(jnp.float32) * spread
        grad = jnp.where(column == target, scale[:, 127:128], grad).astype(jnp.bfloat16)
        acc[...] += lax.dot_general(
            grad,
            rows[source, here, :],
            (((0,), (0,)), ((), ())),
            preferred_element_type=jnp.float32,
        )

    def add_source(source, _):
        live = info[1 + source * (count + 1) + count]
        chunks = (live + CHUNK - 1) // CHUNK

        @pl.when(chunks == 4)
        def _():
            add(source, 0, 4 * CHUNK)

        @pl.when(jnp.logical_or(chunks == 2, chunks == 3))
        def _():
            add(source, 0, 2 * CHUNK)

        @pl.when(chunks % 2 == 1)
        def _():
            add(source, (chunks - 1) * CHUNK, CHUNK)

        return 0

    lax.fori_loop(0, sources, add_source, 0)
    half = wide // 2
    for side, out in enumerate(outs):
        for place in range(out.shape[0]):
            size = out.shape[3]
            out[place, 0] = acc[
                side * half : (side + 1) * half, place * size : (place + 1) * size
            ].astype(jnp.bfloat16)


def table_pass(info, facts, tops, rows, expos, first, tiles, n_pb, earlier):
    sources, _, both, wide = expos.shape
    _, room, width = rows.shape
    own = width // n_pb
    once = pl.Buffered(1)
    cube = lambda i, s: (0, 0, 0)
    return pl.pallas_call(
        functools.partial(table_kernel, first),
        grid_spec=pltpu.PrefetchScalarGridSpec(
            num_scalar_prefetch=1,
            grid=(tiles,),
            in_specs=[
                pl.BlockSpec(facts.shape, cube, pipeline_mode=once),
                pl.BlockSpec(tops.shape, cube, pipeline_mode=once),
                pl.BlockSpec(rows.shape, cube, pipeline_mode=once),
                pl.BlockSpec((sources, 1, both, wide), lambda i, s: (0, i + first, 0, 0)),
            ]
            + [pl.BlockSpec(memory_space=pl.ANY)] * len(earlier),
            out_specs=[pl.BlockSpec((n_pb, 1, wide // 2, own), lambda i, s: (0, i, 0, 0))] * 2,
            scratch_shapes=[
                pltpu.VMEM((wide, width), jnp.float32),
                pltpu.VMEM((sources, room, 128), jnp.float32),
            ],
        ),
        out_shape=[jax.ShapeDtypeStruct((n_pb, tiles, wide // 2, own), jnp.bfloat16)] * 2,
        compiler_params=pltpu.CompilerParams(vmem_limit_bytes=60 << 20),
        cost_estimate=SMALL,
        name=f"table_pass_{first}",
    )(info, facts, tops, rows, expos, *earlier)


def gather_kernel(*refs):
    mats, rows = refs[:3], refs[3:5]
    full, laid = refs[5:8], refs[8:10]
    send, recv, near = refs[10:]
    slots = full[0].shape[1]
    pb, place = lax.axis_index("pb"), lax.axis_index("slot")
    mate = pb // 2 * 2 + (pb + 1) % 2
    side_x = pb // 4 * 4 + (pb + 2) % 4
    side_y = (pb + 4) % 8
    corner = (side_x + 4) % 8
    barrier = pltpu.get_barrier_semaphore()
    partners = [(mate, place), (side_x, place), (side_y, place)]
    partners += [(pb, (place + step) % slots) for step in range(1, slots)]
    for partner in partners:
        pl.semaphore_signal(barrier, inc=1, device_id=partner, device_id_type=pl.DeviceIdType.MESH)
    pl.semaphore_wait(barrier, len(partners))

    sent, unread, stays, ready = [], {}, [], {}

    def push(source, target, device):
        copy = pltpu.make_async_remote_copy(
            src_ref=source,
            dst_ref=target,
            send_sem=send.at[len(sent)],
            recv_sem=recv.at[len(sent)],
            device_id=device,
            device_id_type=pl.DeviceIdType.MESH,
        )
        copy.start()
        unread[len(sent)] = copy
        sent.append(copy)
        return len(sent) - 1

    def read(number):
        unread.pop(number).wait_recv()

    def put(source, target):
        copy = pltpu.make_async_copy(source, target, near.at[len(stays)])
        copy.start()
        stays.append(copy)

    def move_rows(step):
        goal = (place + step) % slots
        for source, target in zip(rows, laid):
            block = source.at[:, goal]
            spot = target.at[:, :, place]
            if step:
                push(block, spot, (pb, goal))
            else:
                put(block, spot)

    def part(mat, at_pb, origin, half):
        size = full[mat].shape[2] // 2
        return full[mat].at[at_pb, origin, pl.ds(half * size, size)]

    def own_moves(step, mat, origin, source):
        size = full[mat].shape[2] // 2
        first, second = (source.at[pl.ds(half * size, size)] for half in range(2))
        first_at, second_at = (part(mat, pb, origin, half) for half in range(2))
        ready[step, mat] = [
            push(first, first_at, (side_x, place)),
            push(second, second_at, (side_y, place)),
            push(first, first_at, (side_y, place)),
            push(second, second_at, (side_x, place)),
        ]
        push(source, full[mat].at[pb, origin], (mate, place))

    def onward(step, mat, origin):
        over_x, over_y, _, _ = ready[step, mat]
        read(over_x)
        block = part(mat, side_x, origin, 0)
        ready[step, mat].append(push(block, block, (side_y, place)))
        push(block, block, (mate, place))
        read(over_y)
        block = part(mat, side_y, origin, 1)
        ready[step, mat].append(push(block, block, (side_x, place)))
        push(block, block, (mate, place))

    def finish(step, mat, origin):
        _, _, over_y, over_x, first, second = ready[step, mat]
        for number, at_pb, half in (
            (over_y, side_y, 0),
            (over_x, side_x, 1),
            (first, corner, 0),
            (second, corner, 1),
        ):
            read(number)
            block = part(mat, at_pb, origin, half)
            push(block, block, (mate, place))

    count = len(mats)
    following = (pb, (place + 1) % slots)
    ring = [push(mats[mat], full[mat].at[pb, place], following) for mat in range(count)]
    for mat in range(count):
        own_moves(0, mat, place, mats[mat])
        put(mats[mat], full[mat].at[pb, place])
    move_rows(1)
    move_rows(0)
    for step in range(1, slots + 1):
        origin = (place + slots - step) % slots
        before = (place + slots - step + 1) % slots
        if step < slots:
            for mat in range(count):
                read(ring[mat])
                block = full[mat].at[pb, origin]
                if step < slots - 1:
                    ring[mat] = push(block, block, following)
                own_moves(step, mat, origin, block)
        if step == 1:
            move_rows(slots - 1)
        if step == 2:
            for other in range(2, slots - 1):
                move_rows(other)
        for mat in range(count):
            onward(step - 1, mat, before)
        for mat in range(count):
            finish(step - 1, mat, before)
    for number in sorted(unread):
        read(number)
    for copy in sent:
        copy.wait_send()
    for copy in stays:
        copy.wait()


def gather_inputs(x_in, memory, attn_w, ffn_in, ffn_out):
    n_pb, slots = lax.axis_size("pb"), lax.axis_size("slot")
    mats, rows = (attn_w, ffn_in, ffn_out), (x_in, memory)
    width = attn_w.shape[1]
    rows = [row.reshape((-1, slots) + row.shape[1:]) for row in rows]
    if (n_pb, slots) != (8, 4):
        return (
            to_slots(x_in),
            to_slots(memory),
            *(gather_all(mat).reshape(-1, width) for mat in mats),
        )
    shapes = [jax.ShapeDtypeStruct((n_pb, slots) + mat.shape, mat.dtype) for mat in mats]
    for row in rows:
        own, _, questions, steps, _ = row.shape
        shapes.append(jax.ShapeDtypeStruct((own, questions, slots, steps, width), row.dtype))
    copies = 13 * len(mats) * slots + (slots - 1) * (len(mats) + len(rows))
    anywhere = pl.BlockSpec(memory_space=pl.ANY)
    *full, x_here, mem_here = pl.pallas_call(
        gather_kernel,
        in_specs=[anywhere] * 5,
        out_specs=[anywhere] * 5,
        out_shape=shapes,
        scratch_shapes=[
            pltpu.SemaphoreType.DMA((copies,)),
            pltpu.SemaphoreType.DMA((copies,)),
            pltpu.SemaphoreType.DMA((len(mats) + len(rows),)),
        ],
        compiler_params=pltpu.CompilerParams(collective_id=0, has_side_effects=True),
        name="gather_inputs",
    )(*mats, *rows)
    own, questions, _, _, _ = x_here.shape
    return (
        x_here.reshape(own, questions, -1, width),
        mem_here.reshape(own, questions, -1, width),
        *(mat.reshape(-1, width) for mat in full),
    )


UNIT = 64


def scatter_kernel(*refs):
    mats, rows, few = refs[:3], refs[3], refs[4]
    outs, laid, few_out = refs[5:8], refs[8], refs[9]
    (from_core, kept, wide_x, wide_y, narrow_x, narrow_y, from_slot, few_here, few_there, few_slot) = refs[10:20]
    send, recv, near = refs[20:]
    depth = kept.shape[0]
    slots = mats[0].shape[2]
    pb, place = lax.axis_index("pb"), lax.axis_index("slot")
    core, at_x, at_y = pb % 2, pb // 2 % 2, pb // 4
    mate = (pb // 2 * 2 + (pb + 1) % 2, place)
    side_x = (pb // 4 * 4 + (pb + 2) % 4, place)
    side_y = ((pb + 4) % 8, place)
    barrier = pltpu.get_barrier_semaphore()
    partners = [mate, side_x, side_y]
    partners += [(pb, (place + step) % slots) for step in range(1, slots)]
    for partner in partners:
        pl.semaphore_signal(barrier, inc=1, device_id=partner, device_id_type=pl.DeviceIdType.MESH)
    pl.semaphore_wait(barrier, len(partners))

    sent = []

    def push(source, target, device):
        copy = pltpu.make_async_remote_copy(
            src_ref=source,
            dst_ref=target,
            send_sem=send.at[len(sent)],
            recv_sem=recv.at[len(sent)],
            device_id=device,
            device_id_type=pl.DeviceIdType.MESH,
        )
        copy.start()
        sent.append(copy)
        return copy

    stays = []

    def put(source, target):
        copy = pltpu.make_async_copy(source, target, near.at[len(stays)])
        copy.start()
        stays.append(copy)
        return copy

    units = [
        (mat, unit)
        for mat in (1, 2, 0)
        for unit in range(mats[mat].shape[3] // UNIT)
    ]

    def block(number, which):
        mat, unit = units[number]
        return mats[mat].at[:, which, :, pl.ds(unit * UNIT, UNIT)]

    half = UNIT // 2
    first, second = pl.ds(0, half), pl.ds(half, half)
    ahead = 2
    by_core = [push(block(n, 1 - core), from_core.at[n], mate) for n in range(ahead)]
    loads = {n: put(block(n, core), kept.at[n % depth]) for n in range(min(depth, len(units)))}
    by_rows = []
    for step in range(1, slots):
        goal = (place + step) % slots
        by_rows.append(push(rows.at[:, :, goal], laid.at[:, place], (pb, goal)))
    at_home = put(rows.at[:, :, place], laid.at[:, place])
    by_few = push(few, few_there.at[0], mate)

    def total(left, right):
        return (left.astype(jnp.float32) + right.astype(jnp.float32)).astype(jnp.bfloat16)

    over, across, along = {}, {}, {}

    def from_cores(n):
        slot = n % depth
        by_core[n].wait_recv()
        if n + ahead < len(units):
            by_core.append(push(block(n + ahead, 1 - core), from_core.at[n + ahead], mate))
        loads[n].wait()

        def step(i, _):
            y, x, z = i // (2 * slots), i // slots % 2, i % slots
            kept[slot, 2 * y + x, z] = total(kept[slot, 2 * y + x, z], from_core[n, 2 * y + x, z])
            return 0

        lax.fori_loop(0, 4 * slots, step, 0)
        over[n] = [
            push(kept.at[slot, 1 - at_x, :, first], wide_x.at[n, 0], side_x),
            push(kept.at[slot, 2 + 1 - at_x, :, first], wide_x.at[n, 1], side_x),
            push(kept.at[slot, pl.ds(2 * (1 - at_y), 2), :, second], wide_y.at[n], side_y),
        ]

    def over_first(n):
        slot = n % depth
        for copy in over[n]:
            copy.wait_recv()

        def step(i, _):
            side, z = i // slots, i % slots
            spot = 2 * side + at_x
            kept[slot, spot, z, 0:half] = total(kept[slot, spot, z, 0:half], wide_x[n, side, z])
            spot = 2 * at_y + side
            kept[slot, spot, z, half:UNIT] = total(kept[slot, spot, z, half:UNIT], wide_y[n, side, z])
            return 0

        lax.fori_loop(0, 2 * slots, step, 0)
        across[n] = [
            push(kept.at[slot, 2 * (1 - at_y) + at_x, :, first], narrow_y.at[n], side_y),
            push(kept.at[slot, 2 * at_y + 1 - at_x, :, second], narrow_x.at[n], side_x),
        ]

    def over_second(n):
        slot = n % depth
        for copy in across[n]:
            copy.wait_recv()
        spot = 2 * at_y + at_x

        def step(z, _):
            kept[slot, spot, z, 0:half] = total(kept[slot, spot, z, 0:half], narrow_y[n, z])
            kept[slot, spot, z, half:UNIT] = total(kept[slot, spot, z, half:UNIT], narrow_x[n, z])
            return 0

        lax.fori_loop(0, slots, step, 0)
        along[n] = []
        for step_on in range(1, slots):
            goal = (place + step_on) % slots
            along[n].append(push(kept.at[slot, spot, goal], from_slot.at[n, step_on - 1], (pb, goal)))

    def over_slots(n):
        slot = n % depth
        mat, unit = units[n]
        for copy in along[n]:
            copy.wait_recv()
        here = kept[slot, 2 * at_y + at_x, place].astype(jnp.float32)
        for step_on in range(1, slots):
            here = here + from_slot[n, step_on - 1].astype(jnp.float32)
        outs[mat][unit * UNIT : (unit + 1) * UNIT, :] = here
        if n + depth < len(units):
            for copy in over[n] + across[n] + along[n]:
                copy.wait_send()
            loads[n + depth] = put(block(n + depth, core), kept.at[slot])

    stages = (from_cores, over_first, over_second, over_slots)
    for turn in range(len(units) + len(stages) - 1):
        for lag, stage in enumerate(stages):
            if 0 <= turn - lag < len(units):
                stage(turn - lag)
        if turn == 0:
            by_few.wait_recv()
            few_here[0] = few[...] + few_there[0]
            by_few = push(few_here.at[0], few_there.at[1], side_x)
        if turn == 1:
            by_few.wait_recv()
            few_here[1] = few_here[0] + few_there[1]
            by_few = push(few_here.at[1], few_there.at[2], side_y)
        if turn == 2:
            by_few.wait_recv()
            few_here[2] = few_here[1] + few_there[2]
            few_slot[place] = few_here[2]
            by_few = [
                push(few_here.at[2], few_slot.at[place], (pb, (place + step) % slots))
                for step in range(1, slots)
            ]
    for copy in by_few:
        copy.wait_recv()
    every = few_slot[0]
    for step in range(1, slots):
        every = every + few_slot[step]
    few_out[...] = every
    for copy in by_rows:
        copy.wait_recv()
    at_home.wait()
    freed = set()
    for n in range(len(units) - depth):
        freed.update(id(copy) for copy in over[n] + across[n] + along[n])
    for copy in sent:
        if id(copy) not in freed:
            copy.wait_send()


def scatter_outputs(grad_attn, grad_in_w, grad_out_w, grad_inputs, small):
    n_pb, slots = lax.axis_size("pb"), lax.axis_size("slot")
    if (n_pb, slots) != (8, 4):
        return (
            scatter_all(grad_attn),
            scatter_all(grad_in_w),
            scatter_all(grad_out_w),
            to_positions(leave_slots(grad_inputs)),
            sum_all(small, ("core", "x", "y", "slot")),
        )
    width = grad_attn.shape[1]
    mats = [
        mat.reshape(n_pb // 2, 2, slots, -1, width)
        for mat in (grad_attn, grad_in_w, grad_out_w)
    ]
    own, questions, steps, _ = grad_inputs.shape
    rows = grad_inputs.reshape(own, questions, slots, steps // slots, width)
    laid = jax.ShapeDtypeStruct((own, slots, questions, steps // slots, width), rows.dtype)
    units = sum(mat.shape[3] for mat in mats) // UNIT
    depth = 5
    copies = units * (1 + 3 + 2 + slots - 1) + (slots - 1) + 3 + slots - 1
    anywhere, inside = pl.BlockSpec(memory_space=pl.ANY), pl.BlockSpec(memory_space=pltpu.VMEM)
    half = UNIT // 2
    low, high = jnp.bfloat16, jnp.float32
    *shards, laid, small = pl.pallas_call(
        scatter_kernel,
        in_specs=[anywhere] * 4 + [inside],
        out_specs=[inside] * 3 + [anywhere, inside],
        out_shape=[jax.ShapeDtypeStruct(mat.shape[3:], high) for mat in mats]
        + [laid, jax.ShapeDtypeStruct(small.shape, high)],
        scratch_shapes=[
            pltpu.VMEM((units, 4, slots, UNIT, width), low),
            pltpu.VMEM((depth, 4, slots, UNIT, width), low),
            pltpu.VMEM((units, 2, slots, half, width), low),
            pltpu.VMEM((units, 2, slots, half, width), low),
            pltpu.VMEM((units, slots, half, width), low),
            pltpu.VMEM((units, slots, half, width), low),
            pltpu.VMEM((units, slots - 1, UNIT, width), low),
            pltpu.VMEM((3,) + small.shape, high),
            pltpu.VMEM((3,) + small.shape, high),
            pltpu.VMEM((slots,) + small.shape, high),
            pltpu.SemaphoreType.DMA((copies,)),
            pltpu.SemaphoreType.DMA((copies,)),
            pltpu.SemaphoreType.DMA((units + 1,)),
        ],
        compiler_params=pltpu.CompilerParams(
            collective_id=1, has_side_effects=True, vmem_limit_bytes=60 << 20
        ),
        cost_estimate=SMALL,
        name="scatter_outputs",
    )(*mats, rows, small)
    return (*shards, laid.reshape((-1,) + laid.shape[2:]), small)


def body(
    x_in,
    memory,
    doc_scores,
    valid_count,
    target_ids,
    target_len,
    mem_len,
    attn_w,
    ffn_in,
    ffn_out,
    ffn_bias,
    norms,
    embedding,
):
    x_here, mem_here, attn_full, in_full, out_full = gather_inputs(
        x_in, memory, attn_w, ffn_in, ffn_out
    )
    slots_here, questions, tgt_steps, model_width = x_here.shape
    mem_steps = mem_here.shape[2]
    seq_count = slots_here * questions
    head_dim = model_width // HEADS
    scaling = head_dim ** (-0.5)
    blocks = [
        attn_full[block_index * model_width : (block_index + 1) * model_width]
        for block_index in range(8)
    ]

    inputs = x_here.reshape(seq_count * tgt_steps, model_width)
    memory_rows = mem_here.reshape(seq_count * mem_steps, model_width)
    positions = jnp.arange(tgt_steps)
    place, slot_count = place_of("slot")
    core, cores = place_of("core")
    ring = (place - jnp.arange(slot_count)) % slot_count
    lengths_here = [mem_len] + [shifted(mem_len, "slot", step) for step in range(1, slot_count)]
    lengths_here = jnp.stack(lengths_here)[ring].reshape(slots_here, slot_count, questions)
    mem_lengths = pick(lengths_here, place, 1).reshape(seq_count)
    tgt_lengths = jnp.full_like(mem_lengths, tgt_steps)
    queries = (product(inputs, blocks[0]) * scaling).astype(jnp.bfloat16)
    key_rows = product(inputs, blocks[1]).astype(jnp.bfloat16)
    value_rows = product(inputs, blocks[2]).astype(jnp.bfloat16)
    self_out, self_lse = attend(True, tgt_lengths, queries, key_rows, value_rows)
    hidden_one, normed_one, root_one = norm_forward(
        inputs.astype(jnp.float32) + product(self_out, blocks[3]), norms[0], norms[1]
    )
    one_low = hidden_one.astype(jnp.bfloat16)
    cross_queries = (product(one_low, blocks[4]) * scaling).astype(jnp.bfloat16)
    cross_keys = product(memory_rows, blocks[5]).astype(jnp.bfloat16)
    cross_values = product(memory_rows, blocks[6]).astype(jnp.bfloat16)
    cross_out, cross_lse = attend(False, mem_lengths, cross_queries, cross_keys, cross_values)
    hidden_two, normed_two, root_two = norm_forward(
        hidden_one + product(cross_out, blocks[7]), norms[2], norms[3]
    )
    two_low = hidden_two.astype(jnp.bfloat16)
    pre_act = contract_cols(two_low, in_full) + ffn_bias
    act, slope = gelu_parts(pre_act)
    act_low, slope = act.astype(jnp.bfloat16), slope.astype(jnp.bfloat16)
    hidden_three, normed_three, root_three = norm_forward(
        hidden_two + product(act_low, out_full), norms[4], norms[5]
    )
    three_low = hidden_three.astype(jnp.bfloat16).reshape(
        slots_here, questions, tgt_steps, model_width
    )
    vocab_here = embedding.shape[0]
    share = vocab_here // cores
    pieces = slots_here * questions

    def both_cores(value):
        return jnp.stack([value, shifted(value, "core", 1)]) if cores > 1 else value[None]

    tokens = jnp.concatenate([target_ids, valid_count[:, None], target_len[:, None]], axis=1)
    tokens = both_cores(tokens)
    ids_all, valid_all, len_all = tokens[:, :, :tgt_steps], tokens[:, :, -2], tokens[:, :, -1]

    local = target_ids - place * vocab_here
    held = jnp.logical_and(local >= 0, local < vocab_here)
    target_rows = jnp.take(embedding, jnp.clip(local, 0, vocab_here - 1), axis=0)
    target_rows = jnp.where(held[..., None], target_rows, jnp.zeros_like(target_rows))
    target_rows = after(target_rows, x_here)
    found = [shifted(target_rows, "slot", step) for step in range(1, slot_count)]
    target_rows = sum([f.astype(jnp.float32) for f in found], target_rows.astype(jnp.float32))

    slot_ids = jnp.arange(slot_count)[:, None] + slot_count * jnp.arange(slots_here)[None]
    live_piece = slot_ids[:, None, :, None] < valid_all[None, :, None, :]
    long_piece = (len_all + 15) // 16 * 16
    long_piece = jnp.where(live_piece, long_piece[None, :, None, :], 0).reshape(slot_count, -1)
    ends = jnp.cumsum(long_piece, axis=1)
    packing = jnp.concatenate([ends - long_piece, ends[:, -1:]], axis=1)[ring]
    info = jnp.concatenate([core[None], packing.reshape(-1)]).astype(jnp.int32)
    piece_ids = (ids_all - (place * vocab_here + core * share)).astype(jnp.float32)
    piece_ids = jnp.broadcast_to(
        piece_ids[None, :, None], (slot_count, cores, slots_here, questions, tgt_steps)
    ).reshape(-1, 1, tgt_steps)
    ids_rows = jnp.broadcast_to(piece_ids, (piece_ids.shape[0], 8, tgt_steps))

    group = pieces * tgt_steps
    moving = three_low.reshape(group, model_width)
    arriving = [moving] + [shifted(moving, "slot", step) for step in range(1, slot_count)]
    kept, log_list, homes = (), [], []
    for step in range(slot_count):
        moving = arriving[step] if not step else after(arriving[step], own_logs)
        other = shifted(moving, "core", 1)
        earlier = (own_logs,) if step else ()
        *kept, own_sums, mate_sums, own_logs, mate_logs = rows_pass(
            step, slot_count, info, ids_rows, moving, other, embedding, cores, kept, earlier
        )
        log_list += [own_logs[:, 0], mate_logs[:, 0]]
        homes.append(
            join_pass(
                own_sums, shifted(mate_sums, "core", 1), own_logs, shifted(mate_logs, "core", 1)
            )
        )

    def by_slot(value):
        parts = [value] + [shifted(value, "slot", step) for step in range(1, slot_count)]
        return jnp.stack(parts)[ring]

    target_logit = jnp.sum(three_low.astype(jnp.float32) * target_rows[None], axis=-1)
    told = jnp.concatenate(log_list + [target_logit.reshape(-1, tgt_steps)], axis=0)
    told = both_cores(by_slot(told))
    hit_all = told[:, :, -pieces:].reshape(cores, slot_count, slots_here, questions, tgt_steps)
    hit_all = hit_all.transpose(2, 1, 0, 3, 4).reshape(-1, cores, questions, tgt_steps)
    logs = told[:, :, :-pieces].reshape(
        cores, slot_count, slot_count, cores, slots_here, questions, tgt_steps
    )
    logs = jnp.stack([logs[0], logs[1][:, :, ::-1]]) if cores > 1 else logs
    logs = jax.nn.logsumexp(logs, axis=0)
    turns = (jnp.arange(slot_count)[:, None] - jnp.arange(slot_count)[None]) % slot_count
    logs = jnp.take_along_axis(
        logs, turns.reshape((slot_count, slot_count) + (1,) * (logs.ndim - 2)), axis=1
    )
    rest_all = jax.nn.logsumexp(logs, axis=0)
    rest_all = rest_all.transpose(2, 0, 1, 3, 4).reshape(hit_all.shape)
    log_norm = jnp.logaddexp(rest_all, hit_all)
    live = positions < len_all[..., None]
    lengths = len_all.astype(jnp.float32)
    per_slot = jnp.sum(jnp.where(live[None], hit_all - log_norm, 0.0), axis=3) / lengths[None]
    valid = jnp.arange(per_slot.shape[0])[:, None, None] < valid_all[None]
    scores_t = both_cores(doc_scores).transpose(2, 0, 1)
    joint = jnp.where(valid, scores_t + per_slot, mask_fill)
    prior = jnp.where(valid, scores_t, mask_fill)
    joint_total = jax.nn.logsumexp(joint, axis=0)
    neg_marginal = jax.nn.logsumexp(prior, axis=0) - joint_total
    log_post = joint - joint_total
    posterior = jnp.exp(log_post)
    entropy_q = -jnp.sum(posterior * log_post, axis=0)
    objective_part = jnp.sum((lengths * (neg_marginal + entropy_weight * entropy_q))[0])
    slot_weight = -posterior * (1.0 + entropy_weight * (log_post + entropy_q[None]))
    token_weight = jnp.where(live[None], slot_weight[..., None], 0.0)
    hit_weight = token_weight * jax.nn.sigmoid(rest_all - hit_all)

    def own_slots(value):
        value = value[:, 0].reshape(slots_here, slot_count, questions, tgt_steps)
        return pick(value, place, 1)

    def ring_rows(value):
        value = value.reshape(slots_here, slot_count, cores, questions, tgt_steps)
        return value.transpose(1, 2, 0, 3, 4)[ring].reshape(-1, tgt_steps)

    facts = [ring_rows(value) for value in (token_weight, log_norm, hit_weight)]
    facts = jnp.stack(facts + [ids_rows[:, 0]] + [jnp.zeros_like(facts[0])] * 4, axis=1)
    expos, packed, tops = kept
    tiles = expos.shape[1]
    n_pb = lax.axis_size("pb")
    tall, wide, _ = grid_of(n_pb)
    sends = tuple(homes[1:])
    homes[1:] = [
        shifted(homes[step], "slot", slot_count - step) for step in range(1, slot_count)
    ]
    table_grads = []
    for first, count in ((0, tiles),):
        sides = [
            side.reshape((tall, wide, cores) + side.shape[1:])
            for side in table_pass(
                info, facts, tops, packed, expos, first, count, n_pb, sends
            )
        ]
        sends = (ring_first(sides[0], "x", 1), ring_first(sides[1], "y", 0))
        table_grads.append(sides)

    def over_first(sides, late):
        return (
            ring_scatter(sides[0], "x", 1, late).astype(jnp.bfloat16),
            ring_scatter(sides[1], "y", 0, late).astype(jnp.bfloat16),
        )

    def over_second(sides, late):
        return (
            ring_scatter(sides[0], "y", 0, late).astype(jnp.bfloat16),
            ring_scatter(sides[1], "x", 0, late).astype(jnp.bfloat16),
        )

    def second_sends(sides):
        return ring_first(sides[0], "y", 0), ring_first(sides[1], "x", 0)

    home_logs = pick(logs, place, 1)[:, 0][(place + jnp.arange(slot_count)) % slot_count]
    home_logs = home_logs.reshape(slot_count, pieces, tgt_steps).transpose(1, 0, 2)
    home_logs = jnp.pad(
        home_logs, ((0, 0), (0, 8 - slot_count), (0, 0)), constant_values=mask_fill
    )
    own_weight = own_slots(hit_weight).reshape(pieces, 1, tgt_steps)
    own_weight = jnp.broadcast_to(own_weight, (pieces, 8, tgt_steps))
    grad_three = home_pass(home_logs, own_weight, target_rows, homes, sends)
    back_blocks, in_back, out_back = blocks, in_full, out_full
    grad_res_three, gain_three, shift_three = norm_backward(
        grad_three, normed_three, root_three, norms[4]
    )
    grad_ffn = grad_res_three.astype(jnp.bfloat16)
    grad_out_w = contract_rows(act_low, grad_ffn)
    grad_act = lax.optimization_barrier(contract_cols(grad_ffn, out_back))
    grad_pre = (grad_act * slope.astype(jnp.float32)).astype(jnp.bfloat16)
    grad_in_w = contract_rows(grad_pre, two_low)
    grad_bias = jnp.sum(grad_pre.astype(jnp.float32), axis=0)
    grad_two = grad_res_three + product(grad_pre, in_back)
    grad_res_two, gain_two, shift_two = norm_backward(grad_two, normed_two, root_two, norms[2])
    grad_cross = grad_res_two.astype(jnp.bfloat16)
    grad_w7 = contract_rows(cross_out, grad_cross)
    grad_cross_out = contract_cols(grad_cross, back_blocks[7]).astype(jnp.bfloat16)
    cq_grad, ck_grad, cv_grad = attend(
        False, mem_lengths, cross_queries, cross_keys, cross_values, cross_lse, grad_cross_out
    )
    grad_w4 = contract_rows(one_low, cq_grad) * scaling
    grad_w5 = contract_rows(memory_rows, ck_grad)
    grad_w6 = contract_rows(memory_rows, cv_grad)
    grad_memory = (
        contract_cols(ck_grad, back_blocks[5]) + contract_cols(cv_grad, back_blocks[6])
    ).astype(jnp.bfloat16)
    grad_memory = leave_slots(
        grad_memory.reshape(slots_here, questions, mem_steps, model_width)
    )
    table_sum = [over_first(sides, cq_grad) for sides in table_grads]
    earlier = grad_memory[1:] + [send for sides in table_sum for send in second_sends(sides)]
    grad_one = grad_res_two + contract_cols(cq_grad, back_blocks[4]) * scaling
    grad_res_one, gain_one, shift_one = norm_backward(grad_one, normed_one, root_one, norms[0])
    grad_attn_out = grad_res_one.astype(jnp.bfloat16)
    grad_w3 = contract_rows(self_out, grad_attn_out)
    grad_self_out = contract_cols(grad_attn_out, back_blocks[3]).astype(jnp.bfloat16)
    sq_grad, sk_grad, sv_grad = attend(
        True, tgt_lengths, queries, key_rows, value_rows, self_lse, grad_self_out, earlier
    )
    grad_w0 = contract_rows(inputs, sq_grad) * scaling
    grad_w1 = contract_rows(inputs, sk_grad)
    grad_w2 = contract_rows(inputs, sv_grad)
    grad_inputs = (
        grad_res_one
        + contract_cols(sq_grad, back_blocks[0]) * scaling
        + contract_cols(sk_grad, back_blocks[1])
        + contract_cols(sv_grad, back_blocks[2])
    )
    grad_inputs = grad_inputs.astype(jnp.bfloat16).reshape(
        slots_here, questions, tgt_steps, model_width
    )
    grad_attn = jnp.concatenate(
        [
            grad.astype(jnp.bfloat16)
            for grad in (grad_w0, grad_w1, grad_w2, grad_w3, grad_w4, grad_w5, grad_w6, grad_w7)
        ],
        axis=0,
    )
    small = jnp.concatenate(
        [
            jnp.stack([gain_one, shift_one, gain_two, shift_two, gain_three, shift_three], axis=0),
            grad_bias.reshape(-1, model_width),
            jnp.zeros((6, model_width), jnp.float32)
            .at[0, :3]
            .set(jnp.stack([objective_part, jnp.sum(lengths[0]), jnp.sum(entropy_q[0])])),
        ],
        axis=0,
    )
    table_sum = [over_second(sides, grad_inputs) for sides in table_sum]
    table_sum = [jnp.stack(sides, axis=2) for sides in table_sum]
    table_sum = jnp.concatenate(table_sum, axis=1).reshape(cores, share, -1)
    table_send = pick(table_sum, 1 - core, 0)
    grad_attn, grad_in_w, grad_out_w, grad_inputs, small = scatter_outputs(
        grad_attn,
        grad_in_w.astype(jnp.bfloat16),
        grad_out_w.astype(jnp.bfloat16),
        grad_inputs,
        after(small, table_send),
    )
    grad_memory = [grad_memory[0]] + [
        shifted(grad_memory[step], "slot", step) for step in range(1, slot_count)
    ]
    grad_memory = lay_blocks(grad_memory, place, (small,))
    grad_memory = grad_memory.reshape((-1,) + grad_memory.shape[2:])
    kept = pick(table_sum, core, 0)
    given = after(shifted(table_send, "core", 1), small)
    grad_embed = jnp.stack([kept, given])
    grad_embed = jnp.where(core == 0, grad_embed, grad_embed[::-1])
    grad_embed = grad_embed.reshape(vocab_here, -1).astype(jnp.float32)
    grad_norms = small[:6]
    scalars = small[-6]
    loss = scalars[0] / scalars[1]
    entropy = scalars[2] / (questions * n_pb * slot_count)
    grad_bias = small[6:-6].reshape(-1)
    own_bias = grad_bias.shape[0] // (lax.axis_size("pb") * slot_count)
    grad_bias = lax.dynamic_slice_in_dim(
        grad_bias,
        (lax.axis_index("pb") * slot_count + lax.axis_index("slot")) * own_bias,
        own_bias,
    )
    return (
        loss,
        entropy,
        grad_inputs,
        grad_memory,
        grad_attn,
        grad_in_w,
        grad_out_w,
        grad_bias,
        grad_norms,
        grad_embed,
    )


def solution(mesh):
    placed = (
        P(None, "pb", "slot", None),
        P(None, "pb", "slot", None),
        P("pb", None),
        P("pb"),
        P("pb", None),
        P("pb"),
        P("slot", "pb"),
        P(("pb", "slot"), None),
        P(("pb", "slot"), None),
        P(("pb", "slot"), None),
        P(),
        P(),
        P("slot", None),
    )
    return jax.shard_map(
        body,
        mesh=mesh,
        in_specs=placed,
        out_specs=(
            P(),
            P(),
            P(None, "pb", "slot", None),
            P(None, "pb", "slot", None),
            P(("pb", "slot"), None),
            P(("pb", "slot"), None),
            P(("pb", "slot"), None),
            P(("pb", "slot")),
            P(),
            P("slot", "pb"),
        ),
        check_vma=False,
    )
```
